32 devices in a mesh: rows: 8 (over z, x), tp: 4 (over y, core).
Axes of the slice: x: 2, y: 2, z: 4, core: 2. Of those that a mesh axis runs over, the one named last changes fastest.
Arguments:
- node_feats: bfloat16 [2048, 512], P('rows'), may hold values from -6 to 6
- edge_feats: bfloat16 [16384, 512], P('rows'), may hold values from -6 to 6
- edge_receiver: int32 [16384], P('rows'), may hold values from 0 to 255
- edge_slot: int32 [16384], P('rows'), may hold values from 0 to 255
- edge_mask: int32 [16384], P('rows'), may hold values 0 or 1
- serve_rows: int32 [64, 32], P('rows'), may hold values from 0 to 255
- node_cot: bfloat16 [2048, 512], P('rows')
- edge_cot: bfloat16 [16384, 512], P('rows')
- edge_in_weight: float32 [1536, 512], P(None, 'tp'), may hold values from -0.15625 to 0.15625
- edge_out_weight: float32 [512, 512], P('tp'), may hold values from -0.25 to 0.25
- node_in_weight: float32 [1024, 512], P(None, 'tp'), may hold values from -0.1875 to 0.1875
- node_out_weight: float32 [512, 512], P('tp'), may hold values from -0.25 to 0.25
- hidden_bias: float32 [2, 512], P(None, 'tp'), may hold values from -3 to 3
- feature_vectors: float32 [6, 512], replicated
- edge_in_first: float32 [1536, 512], P(None, 'tp')
- edge_out_first: float32 [512, 512], P('tp')
- node_in_first: float32 [1024, 512], P(None, 'tp')
- node_out_first: float32 [512, 512], P('tp')
- hidden_bias_first: float32 [2, 512], P(None, 'tp')
- feature_vectors_first: float32 [6, 512], replicated
- edge_in_second: float32 [1536, 512], P(None, 'tp')
- edge_out_second: float32 [512, 512], P('tp')
- node_in_second: float32 [1024, 512], P(None, 'tp')
- node_out_second: float32 [512, 512], P('tp')
- hidden_bias_second: float32 [2, 512], P(None, 'tp')
- feature_vectors_second: float32 [6, 512], replicated
Outputs:
- new_nodes: bfloat16 [2048, 512], P('rows')
- new_edges: bfloat16 [16384, 512], P('rows')
- node_gradient: bfloat16 [2048, 512], P('rows')
- edge_gradient: bfloat16 [16384, 512], P('rows')
- gradient_norm: float32 [1], replicated
- new_edge_in: float32 [1536, 512], P(None, 'tp')
- new_edge_out: float32 [512, 512], P('tp')
- new_node_in: float32 [1024, 512], P(None, 'tp')
- new_node_out: float32 [512, 512], P('tp')
- new_hidden_bias: float32 [2, 512], P(None, 'tp')
- new_feature_vectors: float32 [6, 512], replicated
- new_edge_in_first: float32 [1536, 512], P(None, 'tp')
- new_edge_out_first: float32 [512, 512], P('tp')
- new_node_in_first: float32 [1024, 512], P(None, 'tp')
- new_node_out_first: float32 [512, 512], P('tp')
- new_hidden_bias_first: float32 [2, 512], P(None, 'tp')
- new_feature_vectors_first: float32 [6, 512], replicated
- new_edge_in_second: float32 [1536, 512], P(None, 'tp')
- new_edge_out_second: float32 [512, 512], P('tp')
- new_node_in_second: float32 [1024, 512], P(None, 'tp')
- new_node_out_second: float32 [512, 512], P('tp')
- new_hidden_bias_second: float32 [2, 512], P(None, 'tp')
- new_feature_vectors_second: float32 [6, 512], replicated
The draws below stay inside these ranges and needn't reach their ends.
Inputs may be any that keep to these rules, and one draw needn't show every extreme that they name: `serve_rows`: row p * 8 + d holds the local indices of the 32 nodes of device p whose latents device d receives. `edge_slot`: an edge of device d with slot s has as sender the node named in entry s % 32 of row (s // 32) * 8 + d of serve_rows. `edge_receiver`: index of the receiver among the 256 nodes of the edge's own device.
All inputs are finite; a program needn't handle non-finite values. No bound on the sum of `edge_mask` on one device may be relied on, other than what follows from the above.
Results may differ from the reference program's by a relative error of at most 0.0081.
Values may be sent and summed in bfloat16 or wider, within the bound.
A program may use at most 128 MiB of HBM per device.

```python
import math
import jax
import jax.numpy as jnp
from jax import lax

LAT = 512
HID = 512
N_DEV = 256
CAP = 32
OWNERS = 8
EDGE_DEV = 2048
NODES = 2048
EDGES = 16384


def vector_share():
    ratio = 0.015 * EDGES / HID
    return ratio / (1.0 + ratio)


def grad_scale(kind_factor):
    total_count = 7 * LAT * HID + 2 * HID
    return kind_factor * math.sqrt(1.0 - vector_share()) / math.sqrt(total_count)


def vector_scale():
    return math.sqrt(vector_share() / (4 * LAT))


def first_draw(key, salt, array_shape, magnitude):
    normal_draw = jnp.clip(jax.random.normal(jax.random.fold_in(key, salt), array_shape, jnp.float32), -4.0, 4.0)
    return normal_draw * (0.11 * magnitude)


def second_draw(key, salt, array_shape, magnitude):
    spread = jnp.exp(jax.random.uniform(jax.random.fold_in(key, salt), array_shape, jnp.float32, math.log(0.5), math.log(8.0)))
    return spread * (0.001 / 0.999 * magnitude * magnitude)


def vector_table(key):
    normal_draw = jnp.clip(jax.random.normal(jax.random.fold_in(key, 11), (6, LAT), jnp.float32), -3.0, 3.0)
    row_index = jnp.arange(6)[:, None]
    is_gain = (row_index == 1) | (row_index == 4)
    return jnp.where(is_gain, 1.0 + 0.15 * normal_draw, 0.5 * normal_draw)


def cot_draw(key, salt, row_count, gain_row):
    gains = vector_table(key)[gain_row]
    noise_key = jax.random.fold_in(key, salt)
    noise = jnp.clip(jax.random.normal(noise_key, (row_count, LAT), jnp.float32), -4.0, 4.0)
    offset = 0.2
    return noise + (offset / gains)[None, :]


def draw_node_cot(key, part):
    return cot_draw(key, 31, NODES, 4).astype(jnp.bfloat16)


def draw_edge_cot(key, part):
    return cot_draw(key, 37, EDGES, 1).astype(jnp.bfloat16)


def draw_feature_vectors(key, part):
    return vector_table(key)


def draw_edge_in_first(key, part):
    return first_draw(key, 101, (3 * LAT, HID), grad_scale(1.0))


def draw_edge_out_first(key, part):
    return first_draw(key, 102, (HID, LAT), grad_scale(1.0))


def draw_node_in_first(key, part):
    return first_draw(key, 103, (2 * LAT, HID), grad_scale(0.35))


def draw_node_out_first(key, part):
    return first_draw(key, 104, (HID, LAT), grad_scale(0.35))


def draw_hidden_bias_first(key, part):
    return first_draw(key, 105, (2, HID), grad_scale(1.0))


def draw_feature_vectors_first(key, part):
    return first_draw(key, 106, (6, LAT), vector_scale())


def draw_edge_in_second(key, part):
    return second_draw(key, 201, (3 * LAT, HID), grad_scale(1.0))


def draw_edge_out_second(key, part):
    return second_draw(key, 202, (HID, LAT), grad_scale(1.0))


def draw_node_in_second(key, part):
    return second_draw(key, 203, (2 * LAT, HID), grad_scale(0.35))


def draw_node_out_second(key, part):
    return second_draw(key, 204, (HID, LAT), grad_scale(0.35))


def draw_hidden_bias_second(key, part):
    return second_draw(key, 205, (2, HID), grad_scale(1.0))


def draw_feature_vectors_second(key, part):
    return second_draw(key, 206, (6, LAT), vector_scale())


def set_ends(values, own_key, low, top_value):
    longest = values.shape.index(max(values.shape))
    spots = []
    for shift in (0, 1):
        where = [jax.random.randint(jax.random.fold_in(own_key, axis), (), 0, length) for axis, length in enumerate(values.shape)]
        where[longest] = (where[longest] + shift) % values.shape[longest]
        spots.append(tuple(where))
    return values.at[spots[0]].set(low).at[spots[1]].set(top_value)


def level_of(rng, shape, split, low, high):
    def one(dim, shards_of):
        heights = jax.random.uniform(jax.random.fold_in(jax.random.fold_in(rng, 6), dim), (shards_of,), jnp.float32, low / len(split), high / len(split))
        return jnp.repeat(jnp.exp(heights), shape[dim] // shards_of).reshape((-1,) + (1,) * (len(shape) - dim - 1))

    factor_of = one(*split[0])
    for cut in split[1:]:
        factor_of = factor_of * one(*cut)
    return factor_of


def scatter_about(stream_key, extent, scale, bound, pieces=(), kind=jnp.bfloat16):
    entries = jax.random.normal(stream_key, extent, jnp.float32) * scale
    if len(pieces) > 0:
        entries = level_of(stream_key, extent, pieces, -0.22, 0.18) * entries
    return jnp.clip(entries, min=-bound, max=bound).astype(kind)


def setup_inputs(seed: int = 0) -> dict:
    key_list = jax.random.split(jax.random.key(seed), 27)
    node_feats = scatter_about(key_list[0], (NODES, LAT), 1.0, 6.0, ((0, 8),))
    edge_feats = scatter_about(key_list[1], (EDGES, LAT), 1.0, 6.0, ((0, 8),))
    edge_receiver = set_ends(jax.random.randint(key_list[2], (EDGES,), 0, N_DEV), jax.random.fold_in(key_list[2], 1), 0, N_DEV - 1).astype(jnp.int32)
    edge_slot = set_ends(jax.random.randint(key_list[3], (EDGES,), 0, OWNERS * CAP), jax.random.fold_in(key_list[3], 1), 0, (OWNERS * CAP) - 1).astype(jnp.int32)
    edge_mask = set_ends((jax.random.randint(key_list[4], (EDGES,), 0, 8) < 7).astype(jnp.int32), jax.random.fold_in(key_list[4], 1), 0, 1)
    serve_rows = set_ends(jax.random.randint(key_list[5], (OWNERS * OWNERS, CAP), 0, N_DEV), jax.random.fold_in(key_list[5], 1), 0, N_DEV - 1).astype(jnp.int32)
    node_cot = draw_node_cot(jax.random.fold_in(key_list[26], 71), 0)
    edge_cot = draw_edge_cot(jax.random.fold_in(key_list[26], 71), 0)
    edge_in_weight = scatter_about(key_list[8], (3 * LAT, HID), (3 * LAT) ** -0.5, 0.15625, ((1, 4),), jnp.float32)
    edge_out_weight = scatter_about(key_list[9], (HID, LAT), HID ** -0.5, 0.25, ((0, 4),), jnp.float32)
    node_in_weight = scatter_about(key_list[10], (2 * LAT, HID), (2 * LAT) ** -0.5, 0.1875, ((1, 4),), jnp.float32)
    node_out_weight = scatter_about(key_list[11], (HID, LAT), HID ** -0.5, 0.25, ((0, 4),), jnp.float32)
    hidden_bias = scatter_about(key_list[12], (2, HID), 0.5, 3.0, ((1, 4),), jnp.float32)
    feature_vectors = draw_feature_vectors(jax.random.fold_in(key_list[26], 71), 0)
    edge_in_first = draw_edge_in_first(jax.random.fold_in(key_list[26], 71), 0)
    edge_out_first = draw_edge_out_first(jax.random.fold_in(key_list[26], 71), 0)
    node_in_first = draw_node_in_first(jax.random.fold_in(key_list[26], 71), 0)
    node_out_first = draw_node_out_first(jax.random.fold_in(key_list[26], 71), 0)
    hidden_bias_first = draw_hidden_bias_first(jax.random.fold_in(key_list[26], 71), 0)
    feature_vectors_first = draw_feature_vectors_first(jax.random.fold_in(key_list[26], 71), 0)
    edge_in_second = draw_edge_in_second(jax.random.fold_in(key_list[26], 71), 0)
    edge_out_second = draw_edge_out_second(jax.random.fold_in(key_list[26], 71), 0)
    node_in_second = draw_node_in_second(jax.random.fold_in(key_list[26], 71), 0)
    node_out_second = draw_node_out_second(jax.random.fold_in(key_list[26], 71), 0)
    hidden_bias_second = draw_hidden_bias_second(jax.random.fold_in(key_list[26], 71), 0)
    feature_vectors_second = draw_feature_vectors_second(jax.random.fold_in(key_list[26], 71), 0)
    return dict(node_feats=node_feats, edge_feats=edge_feats, edge_receiver=edge_receiver, edge_slot=edge_slot, edge_mask=edge_mask, serve_rows=serve_rows, node_cot=node_cot, edge_cot=edge_cot, edge_in_weight=edge_in_weight, edge_out_weight=edge_out_weight, node_in_weight=node_in_weight, node_out_weight=node_out_weight, hidden_bias=hidden_bias, feature_vectors=feature_vectors, edge_in_first=edge_in_first, edge_out_first=edge_out_first, node_in_first=node_in_first, node_out_first=node_out_first, hidden_bias_first=hidden_bias_first, feature_vectors_first=feature_vectors_first, edge_in_second=edge_in_second, edge_out_second=edge_out_second, node_in_second=node_in_second, node_out_second=node_out_second, hidden_bias_second=hidden_bias_second, feature_vectors_second=feature_vectors_second)


@jax.custom_vjp
def low(v):
    return lax.optimization_barrier(v.astype(jnp.bfloat16)).astype(jnp.float32)

@jax.custom_vjp
def low_back(v):
    return v

def low_keep(v):
    return (low(v), None)

def low_pass(kept, grad):
    return (grad,)

def back_keep(v):
    return (v, None)

def back_low(kept, grad):
    return (low(grad),)
low.defvjp(low_keep, low_pass)
low_back.defvjp(back_keep, back_low)
beta_one = 0.9
beta_two = 0.999
adam_step = 7.0
adam_eps = 1e-08
learn_rate = 0.05
vector_rate = 0.3
decay_rate = 0.1
clip_level = 1.0

def matmul(left, right):
    return jnp.dot(left, right, precision=lax.Precision.HIGHEST, preferred_element_type=jnp.float32)

def layer_norm(values, gain, shift):
    center = values - lax.optimization_barrier(jnp.mean(values, axis=-1, keepdims=True))
    variance = lax.optimization_barrier(jnp.mean(center * center, axis=-1, keepdims=True))
    return center * lax.rsqrt(variance + 1e-05) * gain + shift

def adam_update(weight, first, second, gradient, factor, rate):
    clipped = gradient * factor
    first_new = beta_one * first + (1.0 - beta_one) * clipped
    second_new = beta_two * second + (1.0 - beta_two) * clipped * clipped
    bias_one = 1.0 - beta_one ** adam_step
    bias_two = 1.0 - beta_two ** adam_step
    moved = first_new / bias_one / (jnp.sqrt(second_new / bias_two) + adam_eps) + decay_rate * weight
    return (weight - rate * moved, first_new, second_new)

def reference(node_feats, edge_feats, edge_receiver, edge_slot, edge_mask, serve_rows, node_cot, edge_cot, edge_in_weight, edge_out_weight, node_in_weight, node_out_weight, hidden_bias, feature_vectors, edge_in_first, edge_out_first, node_in_first, node_out_first, hidden_bias_first, feature_vectors_first, edge_in_second, edge_out_second, node_in_second, node_out_second, hidden_bias_second, feature_vectors_second):
    device = jnp.arange(EDGES, dtype=jnp.int32) // EDGE_DEV
    owner_dev = edge_slot // CAP
    column = edge_slot % CAP
    sender = owner_dev * N_DEV + serve_rows[owner_dev * OWNERS + device, column]
    receiver = device * N_DEV + edge_receiver
    mask_float = edge_mask.astype(jnp.float32)[:, None]

    def forward(node_in, edge_in, edge_first, edge_second, node_first, node_second, biases, vectors):
        edge_mat = low(edge_first)
        edge_pre = matmul(edge_in, edge_mat[:LAT]) + matmul(node_in[sender], edge_mat[LAT:2 * LAT])
        edge_pre = edge_pre + matmul(node_in[receiver], edge_mat[2 * LAT:]) + biases[0]
        edge_pre = low_back(edge_pre)
        edge_hidden = low(jax.nn.silu(edge_pre))
        edge_outer = low_back(matmul(edge_hidden, low(edge_second)) + vectors[0])
        update = layer_norm(edge_outer, vectors[1], vectors[2])
        masked = mask_float * update
        new_edges = edge_in + masked
        aggregate = low(jax.ops.segment_sum(masked, receiver, num_segments=NODES))
        node_mat = low(node_first)
        node_pre = matmul(node_in, node_mat[:LAT]) + matmul(aggregate, node_mat[LAT:]) + biases[1]
        node_pre = low_back(node_pre)
        node_hidden = low(jax.nn.silu(node_pre))
        node_outer = low_back(matmul(node_hidden, low(node_second)) + vectors[3])
        new_nodes = node_in + layer_norm(node_outer, vectors[4], vectors[5])
        return (new_nodes, new_edges)
    floats = (node_feats.astype(jnp.float32), edge_feats.astype(jnp.float32), edge_in_weight, edge_out_weight, node_in_weight, node_out_weight, hidden_bias, feature_vectors)
    outputs, pullback = jax.vjp(forward, *floats)
    gradients = pullback((node_cot.astype(jnp.float32), edge_cot.astype(jnp.float32)))
    new_nodes = outputs[0].astype(jnp.bfloat16)
    new_edges = outputs[1].astype(jnp.bfloat16)
    node_gradient = gradients[0].astype(jnp.bfloat16)
    edge_gradient = gradients[1].astype(jnp.bfloat16)
    square_sum = jnp.sum(gradients[2] * gradients[2]) + jnp.sum(gradients[3] * gradients[3])
    square_sum = square_sum + jnp.sum(gradients[4] * gradients[4]) + jnp.sum(gradients[5] * gradients[5])
    square_sum = square_sum + jnp.sum(gradients[6] * gradients[6]) + jnp.sum(gradients[7] * gradients[7])
    gradient_norm = jnp.sqrt(square_sum)
    factor = clip_level / jnp.maximum(gradient_norm, clip_level)
    edge_in_new = adam_update(edge_in_weight, edge_in_first, edge_in_second, gradients[2], factor, learn_rate)
    edge_out_new = adam_update(edge_out_weight, edge_out_first, edge_out_second, gradients[3], factor, learn_rate)
    node_in_new = adam_update(node_in_weight, node_in_first, node_in_second, gradients[4], factor, learn_rate)
    node_out_new = adam_update(node_out_weight, node_out_first, node_out_second, gradients[5], factor, learn_rate)
    bias_new = adam_update(hidden_bias, hidden_bias_first, hidden_bias_second, gradients[6], factor, vector_rate)
    vector_new = adam_update(feature_vectors, feature_vectors_first, feature_vectors_second, gradients[7], factor, vector_rate)
    return (new_nodes, new_edges, node_gradient, edge_gradient, gradient_norm.reshape(1), edge_in_new[0], edge_out_new[0], node_in_new[0], node_out_new[0], bias_new[0], vector_new[0], edge_in_new[1], edge_out_new[1], node_in_new[1], node_out_new[1], bias_new[1], vector_new[1], edge_in_new[2], edge_out_new[2], node_in_new[2], node_out_new[2], bias_new[2], vector_new[2])
```

```python
import functools
import types

import jax
import jax.numpy as jnp
from jax import lax
from jax.experimental import pallas as pl
from jax.experimental.pallas import tpu as pltpu
from jax.sharding import PartitionSpec as P

BF = jnp.bfloat16
F32 = jnp.float32
MESH = pl.DeviceIdType.MESH
LANES = 128
TILE = 256

beta_one = 0.9
beta_two = 0.999
adam_step = 7.0
adam_eps = 1e-08
learn_rate = 0.05
vector_rate = 0.3
decay_rate = 0.1
clip_level = 1.0


def mm(left, right):
    return jnp.dot(left, right, preferred_element_type=F32)


def nt(left, right):
    return lax.dot_general(left, right, (((1,), (1,)), ((), ())), preferred_element_type=F32)


def tn(left, right):
    return lax.dot_general(left, right, (((0,), (0,)), ((), ())), preferred_element_type=F32)


def two(values):
    high = values.astype(BF)
    return high, (values - high.astype(F32)).astype(BF)


def aligned(start, step):
    return start if isinstance(start, int) else pl.multiple_of(start, step)


def rows_of(start, size, step=16):
    return pl.ds(aligned(start, step), size)


def hot(cond):
    return jnp.where(cond, 1.0, 0.0).astype(BF)


def normalize(values):
    center = values - jnp.mean(values, axis=1, keepdims=True)
    inverse = lax.rsqrt(jnp.mean(center * center, axis=1, keepdims=True) + 1e-05)
    return center * inverse, inverse


def norm_back(scaled, normed, inverse):
    first = jnp.mean(scaled, axis=1, keepdims=True)
    second = jnp.mean(scaled * normed, axis=1, keepdims=True)
    return inverse * (scaled - first - normed * second)


def row_sum(values):
    return jnp.sum(values, axis=0, keepdims=True)


def layer(names, d, *refs):
    s = types.SimpleNamespace(**dict(zip(names, refs, strict=True)))
    R, N, E, L, H, Q, CAP = d.R, d.N, d.E, d.L, d.H, d.Q, d.CAP
    EH, S = E // 2, R * CAP
    tiles = EH // TILE
    r = lax.axis_index("rows")
    t = lax.axis_index("tp")
    h, c = t // 2, lax.rem(t, 2)
    oh, oc = 1 - h, 1 - c
    pair = t + 1 - 2 * c
    far = t + 2 - 4 * h
    diag = pair + 2 - 4 * h
    edge0 = c * EH

    def local(src, dst, sem):
        return pltpu.make_async_copy(src, dst, sem)

    def remote(src, dst, send, recv, device):
        return pltpu.make_async_remote_copy(
            src_ref=src, dst_ref=dst, send_sem=send, recv_sem=recv, device_id=device, device_id_type=MESH
        )

    loads = [
        local(s.wei_h, s.wei32, s.lsem.at[0]),
        local(s.nf_h, s.nf, s.lsem.at[1]),
        local(s.ef_h.at[rows_of(edge0, EH)], s.ef, s.lsem.at[2]),
        local(s.weo_h, s.weo32, s.lsem.at[3]),
        local(s.wni_h, s.wni32, s.lsem.at[4]),
        local(s.wno_h, s.wno32, s.lsem.at[5]),
        local(s.ncot_h, s.ncot, s.lsem.at[6]),
        local(s.ecot_h.at[rows_of(edge0, EH)], s.ecot, s.lsem.at[7]),
    ]
    for load in loads:
        load.start()

    barrier = pltpu.get_barrier_semaphore()
    for peer in (pair, far, diag):
        pl.semaphore_signal(barrier, inc=1, device_id=(r, peer), device_id_type=MESH)

    def greet(k, carry):
        pl.semaphore_signal(barrier, inc=1, device_id=(lax.rem(r + k, R), t), device_id_type=MESH)
        return carry

    lax.fori_loop(1, R, greet, 0)
    pl.semaphore_wait(barrier, R + 2)

    def block(i, tt):
        lane = pl.ds(pl.multiple_of(tt * Q, Q), Q)
        if i < 3:
            half_lane = pl.ds(pl.multiple_of(lax.rem(tt, 2) * Q, Q), Q)
            return s.wei.at[tt // 2, pl.ds((0, 2 * L, L)[i], L), half_lane]
        if i == 3:
            return s.weo.at[lane, :]
        if i < 6:
            return s.wni.at[pl.ds((L, 0)[i - 4], L), lane]
        if i == 6:
            return s.wno.at[lane, :]
        return s.bias.at[:, lane]

    def weight_copy(i, way):
        who = (t, t, far)[way]
        ref = block(i, who)
        return remote(ref, ref, s.wsend.at[i, way], s.wrecv.at[i, way], (r, (pair, far, pair)[way]))

    def weight_wait(i, way):
        ref = block(i, (pair, far, diag)[way])
        remote(ref, ref, s.wsend.at[i, way], s.wrecv.at[i, way], (r, (pair, far, pair)[way])).wait_recv()

    def weight_send(i):
        for way in (1, 0):
            weight_copy(i, way).start()

    def weight_forward(i):
        weight_wait(i, 1)
        weight_copy(i, 2).start()

    def weight_done(i):
        for way in (0, 1, 2):
            weight_copy(i, way).wait_send()

    own_lane = pl.ds(pl.multiple_of(t * Q, Q), Q)
    own_half_lane = pl.ds(pl.multiple_of(c * Q, Q), Q)
    loads[0].wait()
    for i in range(3):
        at = pl.ds((0, 2 * L, L)[i], L)
        s.wei[h, at, own_half_lane] = s.wei32[at, :].astype(BF)
        weight_send(i)
    s.bias[:, own_lane] = s.hb[...]
    weight_send(7)
    loads[1].wait()

    def serve(k, carry):
        at = rows_of(k * TILE, TILE)
        table = hot(s.serve_col[at, :] == lax.broadcasted_iota(jnp.int32, (TILE, N), 1))
        s.served[at, :] = mm(table, s.nf[...]).astype(BF)
        return carry

    lax.fori_loop(0, S // TILE, serve, 0)
    mine = rows_of(r * CAP, CAP)

    def served_copy(k):
        to = lax.rem(r + k, R)
        return remote(
            s.served.at[rows_of(to * CAP, CAP)], s.slots.at[mine], s.ssend.at[k], s.srecv.at[k], (to, t)
        )

    def served_start(k, carry):
        served_copy(k).start()
        return carry

    lax.fori_loop(1, R, served_start, 0)
    s.slots[mine, :] = s.served[mine, :]

    loads[3].wait()
    s.weo[own_lane, :] = s.weo32[...].astype(BF)
    weight_send(3)
    loads[4].wait()
    for i in (4, 5):
        at = pl.ds((L, 0)[i - 4], L)
        s.wni[at, own_lane] = s.wni32[at, :].astype(BF)
        weight_send(i)
    loads[5].wait()
    s.wno[own_lane, :] = s.wno32[...].astype(BF)
    weight_send(6)

    per = EH // LANES
    at = rows_of(c * per, per, 8)
    for source, target in ((s.rec2, s.rcol), (s.slot2, s.scol), (s.mask2, s.mcol)):
        turned = jnp.transpose(source[at, :].astype(F32))
        for k in range(per):
            target[k * LANES : (k + 1) * LANES, :] = turned[:, k : k + 1]
    lanes_here = pl.ds(pl.multiple_of(edge0, EH), EH)
    s.rhot_t[...] = hot(s.rec1[:, lanes_here] == lax.broadcasted_iota(jnp.int32, (N, EH), 0))

    def slot_table(k, carry):
        rows = rows_of(k * TILE, TILE)
        s.shot_t[rows, :] = hot(
            s.slot1[:, lanes_here] == lax.broadcasted_iota(jnp.int32, (TILE, EH), 0) + k * TILE
        )
        return carry

    lax.fori_loop(0, S // TILE, slot_table, 0)

    def receivers(k, carry):
        rows = rows_of(k * TILE, TILE)
        index = s.rcol[rows, :].astype(jnp.int32)
        table = hot(index == lax.broadcasted_iota(jnp.int32, (TILE, N), 1))
        s.rhot[rows, :] = table
        s.xr[rows, :] = mm(table, s.nf[...]).astype(BF)
        return carry

    lax.fori_loop(0, tiles, receivers, 0)

    def served_wait(k, carry):
        source = lax.rem(r + R - k, R)
        ref = s.slots.at[rows_of(source * CAP, CAP)]
        remote(ref, ref, s.ssend.at[k], s.srecv.at[k], (source, t)).wait_recv()
        served_copy(k).wait_send()
        return carry

    lax.fori_loop(1, R, served_wait, 0)

    def senders(k, carry):
        rows = rows_of(k * TILE, TILE)
        index = s.scol[rows, :].astype(jnp.int32)
        table = hot(index == lax.broadcasted_iota(jnp.int32, (TILE, S), 1))
        s.xs[rows, :] = mm(table, s.slots[...]).astype(BF)
        return carry

    lax.fori_loop(0, tiles, senders, 0)
    loads[2].wait()

    def first_layer(which):
        def body(k, carry):
            rows = rows_of(k * TILE, TILE)
            value = mm(s.ef[rows, :], s.wei[which, 0:L, :])
            value = value + mm(s.xr[rows, :], s.wei[which, 2 * L : 3 * L, :])
            s.pre[which, rows, :] = value + mm(s.xs[rows, :], s.wei[which, L : 2 * L, :])
            return carry

        lax.fori_loop(0, tiles, body, 0)

    for i in range(3):
        weight_wait(i, 0)
    first_layer(h)
    for i in range(4):
        weight_forward(i)
    for i in range(3):
        weight_wait(i, 2)
    first_layer(oh)
    weight_wait(7, 0)
    weight_forward(7)
    weight_wait(7, 2)
    weight_wait(3, 0)
    weight_wait(3, 2)

    half = H // 2
    s.aggp[...] = jnp.zeros_like(s.aggp)

    def out_copies(k, source, target, which):
        here = s.__dict__[source].at[rows_of(k * TILE, TILE)]
        there = s.__dict__[target].at[rows_of(edge0 + k * TILE, TILE)]
        other = s.__dict__[target].at[rows_of(oc * EH + k * TILE, TILE)]
        keep = local(here, there, s.osem.at[which, k])
        send = remote(here, there, s.osend.at[which, k], s.orecv.at[which, k], (r, pair))
        take = remote(here, other, s.osend.at[which, k], s.orecv.at[which, k], (r, pair))
        return keep, send, take

    def forward(k, carry):
        rows = rows_of(k * TILE, TILE)
        hidden = []
        for p in (0, 1):
            pre = s.pre[p, rows, :] + s.bias[0:1, p * half : (p + 1) * half]
            sig = 1.0 / (1.0 + jnp.exp(-pre))
            value = (pre * sig).astype(BF)
            s.hid[p, rows, :] = value
            s.pre[p, rows, :] = sig * (1.0 + pre * (1.0 - sig))
            hidden.append(value)
        outer = mm(hidden[0], s.weo[0:half, :]) + mm(hidden[1], s.weo[half:H, :]) + s.fv[0:1, :]
        normed, inverse = normalize(outer)
        s.normed[rows, :] = normed
        s.inv[rows, :] = inverse
        masked = s.mcol[rows, :] * (normed * s.fv[1:2, :] + s.fv[2:3, :])
        s.ne[rows, :] = (s.ef[rows, :].astype(F32) + masked).astype(BF)
        keep, send, _ = out_copies(k, "ne", "ne_h", 0)
        keep.start()
        send.start()
        high, low = two(masked)
        table = s.rhot_t[:, pl.ds(pl.multiple_of(k * TILE, TILE), TILE)]
        s.aggp[...] += mm(table, high) + mm(table, low)
        return carry

    lax.fori_loop(0, tiles, forward, 0)
    swap = remote(s.aggp, s.aggr, s.xsend.at[0], s.xrecv.at[0], (r, pair))
    swap.start()
    for i in (4, 5, 6):
        weight_wait(i, 0)
        weight_forward(i)
    for i in (4, 5, 6):
        weight_wait(i, 2)
    own_term = mm(s.nf[...], s.wni[0:L, :])
    swap.wait()

    agg = (s.aggp[...] + s.aggr[...]).astype(BF)
    pre = own_term + mm(agg, s.wni[L : 2 * L, :]) + s.bias[1:2, :]
    sig = 1.0 / (1.0 + jnp.exp(-pre))
    node_hidden = (pre * sig).astype(BF)
    slope_of = sig * (1.0 + pre * (1.0 - sig))
    outer = mm(node_hidden, s.wno[...]) + s.fv[3:4, :]
    normed, inverse = normalize(outer)
    s.nn[...] = (s.nf[...].astype(F32) + (normed * s.fv[4:5, :] + s.fv[5:6, :])).astype(BF)
    nn_copy = local(s.nn, s.nn_h, s.nsem.at[0])
    nn_copy.start()
    loads[6].wait()
    up = s.ncot[...].astype(F32)
    node_outer_grad = norm_back(up * s.fv[4:5, :], normed, inverse).astype(BF)
    node_slope = (nt(node_outer_grad, s.wno[...]) * slope_of).astype(BF)
    agg_high, agg_low = two(nt(node_slope, s.wni[L : 2 * L, :]))
    s.agh[...] = agg_high
    s.agl[...] = agg_low
    s.ntp[...] = 0.5 * (up + nt(node_slope, s.wni[0:L, :]))
    s.vsum[0:3, :] = jnp.zeros((3, L), F32)
    s.vsum[3:4, :] = 0.5 * row_sum(node_outer_grad.astype(F32))
    s.vsum[4:5, :] = 0.5 * row_sum(up * normed)
    s.vsum[5:6, :] = 0.5 * row_sum(up)
    s.vsum[6:7, :] = jnp.zeros((1, H), F32)
    s.vsum[7:8, :] = 0.5 * row_sum(node_slope.astype(F32))
    for q in range(H // Q):
        s.nsl[q] = node_slope[:, q * Q : (q + 1) * Q]
        s.nhid[q] = node_hidden[:, q * Q : (q + 1) * Q]
    s.g[c, 0:L, :] = tn(s.nf[...], s.nsl[t])
    s.g[c, L : 2 * L, :] = tn(agg, s.nsl[t])
    node_out_grad = tn(s.nhid[t], node_outer_grad)
    for q in range(L // LANES):
        s.g[c, 2 * L + q * Q : 2 * L + (q + 1) * Q, :] = node_out_grad[:, q * LANES : (q + 1) * LANES]

    loads[7].wait()
    s.rs[...] = jnp.zeros_like(s.rs)
    s.ss[...] = jnp.zeros_like(s.ss)

    def backward(k, carry):
        rows = rows_of(k * TILE, TILE)
        cot = s.ecot[rows, :].astype(F32)
        table = s.rhot[rows, :]
        up = s.mcol[rows, :] * (cot + (mm(table, s.agh[...]) + mm(table, s.agl[...])))
        normed = s.normed[rows, :]
        grad = norm_back(up * s.fv[1:2, :], normed, s.inv[rows, :]).astype(BF)
        s.og[rows, :] = grad
        s.vsum[0:1, :] += row_sum(grad.astype(F32))
        s.vsum[1:2, :] += row_sum(up * normed)
        s.vsum[2:3, :] += row_sum(up)
        wide = []
        for p in (0, 1):
            value = nt(grad, s.weo[p * half : (p + 1) * half, :]) * s.pre[p, rows, :]
            value = value.astype(BF)
            s.sl[p, rows, :] = value
            s.vsum[6:7, p * half : (p + 1) * half] += row_sum(value.astype(F32))
            wide.append(value)
        s.eg[rows, :] = (cot + (nt(wide[0], s.wei[0, 0:L, :]) + nt(wide[1], s.wei[1, 0:L, :]))).astype(BF)
        keep, send, _ = out_copies(k, "eg", "eg_h", 1)
        keep.start()
        send.start()
        lanes = pl.ds(pl.multiple_of(k * TILE, TILE), TILE)
        table = s.rhot_t[:, lanes]
        for p in (0, 1):
            s.rs[p] += mm(table, wide[p])

        def slots(j, carry):
            at = rows_of(j * TILE, TILE)
            for p in (0, 1):
                s.ss[p, at, :] += mm(s.shot_t[at, lanes], wide[p])
            return carry

        lax.fori_loop(0, S // TILE, slots, 0)
        return carry

    lax.fori_loop(0, tiles, backward, 0)

    def slot_grad(k, carry):
        at = rows_of(k * TILE, TILE)
        value = nt(s.ss[0, at, :].astype(BF), s.wei[0, L : 2 * L, :])
        s.served[at, :] = (value + nt(s.ss[1, at, :].astype(BF), s.wei[1, L : 2 * L, :])).astype(BF)
        return carry

    lax.fori_loop(0, S // TILE, slot_grad, 0)

    def back_copy(k):
        to = lax.rem(r + k, R)
        return remote(
            s.served.at[rows_of(to * CAP, CAP)], s.ret.at[mine], s.bsend.at[k], s.brecv.at[k], (to, t)
        )

    def back_start(k, carry):
        back_copy(k).start()
        return carry

    lax.fori_loop(1, R, back_start, 0)
    s.ret[mine, :] = s.served[mine, :]

    node_rows, edge_out_rows, edge_in_rows = 0, 3 * L, 4 * L
    edge_part = tn(s.ef[...], s.sl[h])
    recv_part = tn(s.nf[...], s.rs[h].astype(BF))
    out_part = tn(s.hid[h], s.og[...])
    for p in (0, 1):
        cols = slice(p * Q, (p + 1) * Q)
        s.g[p, edge_in_rows : edge_in_rows + L, :] = edge_part[:, cols]
        s.g[p, edge_in_rows + 2 * L : edge_in_rows + 3 * L, :] = recv_part[:, cols]
        for q in range(L // LANES):
            at = edge_out_rows + q * Q
            s.g[p, at : at + Q, :] = out_part[cols, q * LANES : (q + 1) * LANES]
        s.g[p, edge_in_rows + L : edge_in_rows + 2 * L, :] = jnp.zeros((L, Q), F32)

    def sender_part(k, carry):
        at = rows_of(k * TILE, TILE)
        value = tn(s.slots[at, :], s.ss[h, at, :].astype(BF))
        for p in (0, 1):
            s.g[p, edge_in_rows + L : edge_in_rows + 2 * L, :] += value[:, p * Q : (p + 1) * Q]
        return carry

    lax.fori_loop(0, S // TILE, sender_part, 0)

    def partner(bit):
        value = lax.rem(r // bit, 2)
        return value, (r + bit - 2 * bit * value, t)

    def plan(base, size, paired):
        steps = []
        low, count = base, size
        if paired:
            steps.append(("pair", (r, pair), base, base, size))
        bit = 1
        while bit < R:
            value, device = partner(bit)
            if (count // 2) % 16 == 0:
                count = count // 2
                keep, send = low + value * count, low + (1 - value) * count
                steps.append(("halve", device, send, keep, count))
                low = keep
            else:
                steps.append(("whole", device, low, low, count))
            bit *= 2
        return steps

    def reduce_copy(n, k, step):
        kind, device, send, keep, count = step
        return remote(
            s.sb.at[rows_of(send, count)],
            s.rb.at[k, rows_of(send, count)],
            s.gsend.at[n, k],
            s.grecv.at[n, k],
            device,
        )

    def reduce_start(n, k, step):
        kind, device, send, keep, count = step
        at = rows_of(send, count)
        s.sb[at, :] = s.g[oc if kind == "pair" else c, at, :].astype(BF)
        reduce_copy(n, k, step).start()

    def reduce_finish(n, k, step):
        kind, device, send, keep, count = step
        reduce_copy(n, k, step).wait_send()
        at = rows_of(keep, count)
        ref = s.rb.at[k, at]
        remote(ref, ref, s.gsend.at[n, k], s.grecv.at[n, k], device).wait_recv()
        own = s.sb[at, :].astype(F32) if kind == "whole" else s.g[c, at, :]
        s.g[c, at, :] = own + s.rb[k, at, :].astype(F32)

    def spread_copy(n, k, step, start):
        kind, device, send, keep, count = step
        at = rows_of(start, count)
        return remote(s.fin.at[at], s.fin.at[at], s.fsend.at[n, k], s.frecv.at[n, k], device)

    def chunk_sum(n, steps):
        for k, step in enumerate(steps):
            reduce_start(n, k, step)
            reduce_finish(n, k, step)
        kind, device, send, keep, count = steps[-1]
        at = rows_of(keep, count)
        s.fin[at, :] = s.g[c, at, :].astype(BF)
        for k, step in reversed(list(enumerate(steps))):
            if step[0] == "halve":
                spread_copy(n, k, step, step[3]).start()
                spread_copy(n, k, step, step[3]).wait_send()
                spread_copy(n, k, step, step[2]).wait_recv()

    peers = [(r, pair)]
    bit = 1
    while bit < R:
        peers.append(partner(bit)[1])
        bit *= 2
    for k, device in enumerate(peers):
        copy = remote(s.vsum, s.vrecv.at[k], s.vsem.at[0, k], s.vsem.at[1, k], device)
        copy.start()
        copy.wait()
        s.vsum[...] += s.vrecv[k]

    chunk_sum(0, plan(node_rows, 3 * L, False))
    chunk_sum(1, plan(edge_out_rows, 4 * L, True))

    def back_wait(k, carry):
        source = lax.rem(r + R - k, R)
        ref = s.ret.at[rows_of(source * CAP, CAP)]
        remote(ref, ref, s.bsend.at[k], s.brecv.at[k], (source, t)).wait_recv()
        back_copy(k).wait_send()
        return carry

    lax.fori_loop(1, R, back_wait, 0)
    for p in (0, 1):
        s.ntp[...] += nt(s.rs[p].astype(BF), s.wei[p, 2 * L : 3 * L, :])

    def gathered(k, carry):
        lanes = pl.ds(pl.multiple_of(k * TILE, TILE), TILE)
        table = hot(s.serve_row[:, lanes] == lax.broadcasted_iota(jnp.int32, (N, TILE), 0))
        s.ntp[...] += mm(table, s.ret[rows_of(k * TILE, TILE), :])
        return carry

    lax.fori_loop(0, S // TILE, gathered, 0)
    swap = remote(s.ntp, s.ntr, s.xsend.at[1], s.xrecv.at[1], (r, pair))
    swap.start()
    swap.wait()
    s.ng[...] = (s.ntp[...] + s.ntr[...]).astype(BF)
    ng_copy = local(s.ng, s.ng_h, s.nsem.at[1])
    ng_copy.start()

    total = jnp.zeros((8, LANES), F32)
    squares = s.fin[...].astype(F32)
    squares = squares * squares
    total = jnp.sum(squares.reshape(-1, 8, LANES), axis=0)
    own_bias = s.vsum[:, own_lane]
    row = lax.broadcasted_iota(jnp.int32, (8, LANES), 0)
    total = total + jnp.where(row >= 6, own_bias * own_bias, 0.0)
    own_rows = rows_of(t * 8, 8, 8)
    s.nsq[own_rows, :] = total
    for k, peer in enumerate((pair, far, diag)):
        ref = s.nsq.at[own_rows]
        remote(ref, ref, s.qsem.at[0, k], s.qsem.at[1, k], (r, peer)).start()
    for k, peer in enumerate((pair, far, diag)):
        ref = s.nsq.at[rows_of(peer * 8, 8, 8)]
        remote(ref, ref, s.qsem.at[0, k], s.qsem.at[1, k], (r, peer)).wait()
    total = s.nsq[0:8, :] + s.nsq[8:16, :] + s.nsq[16:24, :] + s.nsq[24:32, :]
    vectors = s.vsum[0:6, :]
    square = jnp.sum(total) + jnp.sum(vectors * vectors)
    s.norm_o[...] = jnp.sqrt(jnp.full((8, LANES), square, F32))
    s.fin_o[...] = s.fin[...]
    s.vec_o[...] = s.vsum[...]

    for i in range(8):
        weight_done(i)

    def finish(k, carry):
        for source, target, which in (("ne", "ne_h", 0), ("eg", "eg_h", 1)):
            keep, send, take = out_copies(k, source, target, which)
            keep.wait()
            send.wait_send()
            take.wait_recv()
        return carry

    lax.fori_loop(0, tiles, finish, 0)
    nn_copy.wait()
    ng_copy.wait()


def adam(weight, first, second, gradient, factor, rate):
    clipped = gradient * factor
    first_new = beta_one * first + (1.0 - beta_one) * clipped
    second_new = beta_two * second + (1.0 - beta_two) * clipped * clipped
    bias_one = 1.0 - beta_one**adam_step
    bias_two = 1.0 - beta_two**adam_step
    moved = first_new / bias_one / (jnp.sqrt(second_new / bias_two) + adam_eps) + decay_rate * weight
    return weight - rate * moved, first_new, second_new


def update(L, fin, vec, bias_grad, norm, *refs):
    ins, outs = refs[:18], refs[18:]
    factor = clip_level / jnp.maximum(norm[0:1, 0:1], clip_level)

    def one(k, grad, at, rate):
        values = adam(ins[k][at], ins[6 + k][at], ins[12 + k][at], grad, factor, rate)
        for n, value in enumerate(values):
            outs[6 * n + k][at] = value

    one(2, fin[0 : 2 * L, :].astype(F32), (slice(None), slice(None)), learn_rate)
    one(0, fin[4 * L : 7 * L, :].astype(F32), (slice(None), slice(None)), learn_rate)
    for q in range(L // LANES):
        at = (slice(None), slice(q * LANES, (q + 1) * LANES))
        one(3, fin[2 * L + q * LANES : 2 * L + (q + 1) * LANES, :].astype(F32), at, learn_rate)
        one(1, fin[3 * L + q * LANES : 3 * L + (q + 1) * LANES, :].astype(F32), at, learn_rate)
    one(4, bias_grad[...], (slice(None), slice(None)), vector_rate)
    one(5, vec[0:6, :], (slice(None), slice(None)), vector_rate)


def device_step(
    node_feats,
    edge_feats,
    edge_receiver,
    edge_slot,
    edge_mask,
    serve_rows,
    node_cot,
    edge_cot,
    *rest,
):
    weights = rest[:6]
    d = types.SimpleNamespace()
    d.R = lax.axis_size("rows")
    d.N, d.L = node_feats.shape
    d.E = edge_feats.shape[0]
    d.Q = weights[0].shape[1]
    d.H = d.Q * lax.axis_size("tp")
    d.CAP = serve_rows.shape[1]
    R, N, E, L, H, Q = d.R, d.N, d.E, d.L, d.H, d.Q
    EH, S = E // 2, R * d.CAP
    steps = 1
    while 2 ** (steps - 1) < R:
        steps += 1
    tiles = EH // TILE
    G = 7 * L
    any_spec = pl.BlockSpec(memory_space=pl.ANY)
    vmem_spec = pl.BlockSpec(memory_space=pltpu.VMEM)
    inputs = dict(
        nf_h=(node_feats, any_spec),
        ef_h=(edge_feats, any_spec),
        ncot_h=(node_cot, any_spec),
        ecot_h=(edge_cot, any_spec),
        wei_h=(weights[0], any_spec),
        weo_h=(weights[1], any_spec),
        wni_h=(weights[2], any_spec),
        wno_h=(weights[3], any_spec),
        hb=(jnp.pad(weights[4], ((0, 6), (0, 0))), vmem_spec),
        fv=(jnp.pad(weights[5], ((0, 2), (0, 0))), vmem_spec),
        rec2=(edge_receiver.reshape(-1, LANES), vmem_spec),
        slot2=(edge_slot.reshape(-1, LANES), vmem_spec),
        mask2=(edge_mask.reshape(-1, LANES), vmem_spec),
        rec1=(edge_receiver.reshape(1, -1), vmem_spec),
        slot1=(edge_slot.reshape(1, -1), vmem_spec),
        serve_col=(serve_rows.reshape(-1, 1), vmem_spec),
        serve_row=(serve_rows.reshape(1, -1), vmem_spec),
    )
    outputs = dict(
        nn_h=(jax.ShapeDtypeStruct((N, L), BF), any_spec),
        ne_h=(jax.ShapeDtypeStruct((E, L), BF), any_spec),
        ng_h=(jax.ShapeDtypeStruct((N, L), BF), any_spec),
        eg_h=(jax.ShapeDtypeStruct((E, L), BF), any_spec),
        fin_o=(jax.ShapeDtypeStruct((G, Q), BF), vmem_spec),
        vec_o=(jax.ShapeDtypeStruct((8, L), F32), vmem_spec),
        norm_o=(jax.ShapeDtypeStruct((8, LANES), F32), vmem_spec),
    )
    dma = pltpu.SemaphoreType.DMA
    scratch = dict(
        wei32=pltpu.VMEM((3 * L, Q), F32),
        weo32=pltpu.VMEM((Q, L), F32),
        wni32=pltpu.VMEM((2 * L, Q), F32),
        wno32=pltpu.VMEM((Q, L), F32),
        nf=pltpu.VMEM((N, L), BF),
        ef=pltpu.VMEM((EH, L), BF),
        ncot=pltpu.VMEM((N, L), BF),
        ecot=pltpu.VMEM((EH, L), BF),
        wei=pltpu.VMEM((2, 3 * L, H // 2), BF),
        weo=pltpu.VMEM((H, L), BF),
        wni=pltpu.VMEM((2 * L, H), BF),
        wno=pltpu.VMEM((H, L), BF),
        bias=pltpu.VMEM((8, H), F32),
        served=pltpu.VMEM((S, L), BF),
        slots=pltpu.VMEM((S, L), BF),
        ret=pltpu.VMEM((S, L), BF),
        rcol=pltpu.VMEM((EH, 1), F32),
        scol=pltpu.VMEM((EH, 1), F32),
        mcol=pltpu.VMEM((EH, 1), F32),
        rhot=pltpu.VMEM((EH, N), BF),
        rhot_t=pltpu.VMEM((N, EH), BF),
        shot_t=pltpu.VMEM((S, EH), BF),
        xr=pltpu.VMEM((EH, L), BF),
        xs=pltpu.VMEM((EH, L), BF),
        pre=pltpu.VMEM((2, EH, H // 2), F32),
        hid=pltpu.VMEM((2, EH, H // 2), BF),
        normed=pltpu.VMEM((EH, L), F32),
        inv=pltpu.VMEM((EH, 1), F32),
        ne=pltpu.VMEM((EH, L), BF),
        eg=pltpu.VMEM((EH, L), BF),
        aggp=pltpu.VMEM((N, L), F32),
        aggr=pltpu.VMEM((N, L), F32),
        nn=pltpu.VMEM((N, L), BF),
        ng=pltpu.VMEM((N, L), BF),
        agh=pltpu.VMEM((N, L), BF),
        agl=pltpu.VMEM((N, L), BF),
        ntp=pltpu.VMEM((N, L), F32),
        ntr=pltpu.VMEM((N, L), F32),
        nsl=pltpu.VMEM((H // Q, N, Q), BF),
        nhid=pltpu.VMEM((H // Q, N, Q), BF),
        og=pltpu.VMEM((EH, L), BF),
        sl=pltpu.VMEM((2, EH, H // 2), BF),
        rs=pltpu.VMEM((2, N, H // 2), F32),
        ss=pltpu.VMEM((2, S, H // 2), F32),
        g=pltpu.VMEM((2, G, Q), F32),
        sb=pltpu.VMEM((G, Q), BF),
        rb=pltpu.VMEM((steps, G, Q), BF),
        fin=pltpu.VMEM((G, Q), BF),
        vsum=pltpu.VMEM((8, L), F32),
        vrecv=pltpu.VMEM((steps, 8, L), F32),
        nsq=pltpu.VMEM((32, LANES), F32),
        lsem=dma((8,)),
        wsend=dma((8, 3)),
        wrecv=dma((8, 3)),
        ssend=dma((R,)),
        srecv=dma((R,)),
        bsend=dma((R,)),
        brecv=dma((R,)),
        osem=dma((2, tiles)),
        osend=dma((2, tiles)),
        orecv=dma((2, tiles)),
        xsend=dma((2,)),
        xrecv=dma((2,)),
        nsem=dma((2,)),
        gsend=dma((2, steps)),
        grecv=dma((2, steps)),
        fsend=dma((2, steps)),
        frecv=dma((2, steps)),
        vsem=dma((2, steps)),
        qsem=dma((2, 3)),
    )
    names = (*inputs, *outputs, *scratch)
    new_nodes, new_edges, node_gradient, edge_gradient, fin, vec, norm = pl.pallas_call(
        functools.partial(layer, names, d),
        out_shape=[shape for shape, _ in outputs.values()],
        in_specs=[spec for _, spec in inputs.values()],
        out_specs=[spec for _, spec in outputs.values()],
        scratch_shapes=list(scratch.values()),
        compiler_params=pltpu.CompilerParams(
            collective_id=0, has_side_effects=True, vmem_limit_bytes=60 * 1024 * 1024
        ),
    )(*[value for value, _ in inputs.values()])

    bias_grad = lax.dynamic_slice(vec, (6, lax.axis_index("tp") * Q), (2, Q))
    states = rest
    new_states = pl.pallas_call(
        functools.partial(update, L),
        out_shape=[jax.ShapeDtypeStruct(x.shape, F32) for x in states],
        in_specs=[vmem_spec] * (4 + len(states)),
        out_specs=[vmem_spec] * len(states),
        compiler_params=pltpu.CompilerParams(vmem_limit_bytes=48 * 1024 * 1024),
    )(fin, vec, bias_grad, norm, *states)
    return (new_nodes, new_edges, node_gradient, edge_gradient, norm[0, 0:1], *new_states)


def solution(mesh):
    split = [P(None, "tp"), P("tp", None), P(None, "tp"), P("tp", None), P(None, "tp"), P()]
    row = P("rows", None)
    return jax.shard_map(
        device_step,
        mesh=mesh,
        in_specs=(row, row, P("rows"), P("rows"), P("rows"), row, row, row, *split, *split, *split),
        out_specs=(row, row, row, row, P(), *split, *split, *split),
        check_vma=False,
    )
```

```python
import functools
import math
import types

import jax
import jax.numpy as jnp
from jax import lax
from jax.experimental import pallas as pl
from jax.experimental.pallas import tpu as pltpu
from jax.sharding import PartitionSpec as P

BF = jnp.bfloat16
F32 = jnp.float32
MESH = pl.DeviceIdType.MESH
LANES = 128
TILE = 256

beta_one = 0.9
beta_two = 0.999
adam_step = 7.0
adam_eps = 1e-08
learn_rate = 0.05
vector_rate = 0.3
decay_rate = 0.1
clip_level = 1.0


def mm(left, right):
    return jnp.dot(left, right, preferred_element_type=F32)


def nt(left, right):
    return lax.dot_general(left, right, (((1,), (1,)), ((), ())), preferred_element_type=F32)


def tn(left, right):
    return lax.dot_general(left, right, (((0,), (0,)), ((), ())), preferred_element_type=F32)


def two(values):
    high = values.astype(BF)
    return high, (values - high.astype(F32)).astype(BF)


def aligned(start, step):
    return start if isinstance(start, int) else pl.multiple_of(start, step)


def rows_of(start, size, step=16):
    return pl.ds(aligned(start, step), size)


def hot(cond):
    return jnp.where(cond, 1.0, 0.0).astype(BF)


def normalize(values):
    center = values - jnp.mean(values, axis=1, keepdims=True)
    inverse = lax.rsqrt(jnp.mean(center * center, axis=1, keepdims=True) + 1e-05)
    return center * inverse, inverse


def norm_back(scaled, normed, inverse):
    first = jnp.mean(scaled, axis=1, keepdims=True)
    second = jnp.mean(scaled * normed, axis=1, keepdims=True)
    return inverse * (scaled - first - normed * second)


def row_sum(values):
    return jnp.sum(values, axis=0, keepdims=True)


def layer(names, d, *refs):
    s = types.SimpleNamespace(**dict(zip(names, refs, strict=True)))
    R, N, E, L, H, Q, CAP = d.R, d.N, d.E, d.L, d.H, d.Q, d.CAP
    EH, S, half, LH = E // 2, R * CAP, H // 2, L // 2
    tiles, slot_tiles, nb = EH // TILE, S // TILE, R // 4
    r = lax.axis_index("rows")
    t = lax.axis_index("tp")
    h, c = t // 2, lax.rem(t, 2)
    oh, oc = 1 - h, 1 - c
    pair = t + 1 - 2 * c
    far = t + 2 - 4 * h
    diag = pair + 2 - 4 * h
    a, b = lax.rem(r, 4), r // 4
    edge0 = c * EH
    own_lane = pl.ds(pl.multiple_of(t * Q, Q), Q)
    core_lane = pl.ds(pl.multiple_of(c * Q, Q), Q)
    col_lane = pl.ds(pl.multiple_of(c * LH, LH), LH)

    def local(src, dst, sem):
        return pltpu.make_async_copy(src, dst, sem)

    def remote(src, dst, send, recv, device):
        return pltpu.make_async_remote_copy(
            src_ref=src, dst_ref=dst, send_sem=send, recv_sem=recv, device_id=device, device_id_type=MESH
        )

    def loop(low, high, body):
        def step(k, carry):
            body(k)
            return carry

        lax.fori_loop(low, high, step, 0)

    loads = [
        local(s.wei_h, s.wei32, s.lsem.at[0]),
        local(s.nf_h, s.nf, s.lsem.at[1]),
        local(s.ef_h.at[rows_of(edge0, EH)], s.ef, s.lsem.at[2]),
        local(s.weo_h, s.weo32, s.lsem.at[3]),
        local(s.wni_h, s.wni32, s.lsem.at[4]),
        local(s.wno_h, s.wno32, s.lsem.at[5]),
        local(s.ncot_h, s.ncot, s.lsem.at[6]),
        local(s.ecot_h.at[rows_of(edge0, EH)], s.ecot, s.lsem.at[7]),
    ]
    for load in loads:
        load.start()

    barrier = pltpu.get_barrier_semaphore()
    for peer in (pair, far, diag):
        pl.semaphore_signal(barrier, inc=1, device_id=(r, peer), device_id_type=MESH)

    def greet(k):
        pl.semaphore_signal(barrier, inc=1, device_id=(lax.rem(r + k, R), t), device_id_type=MESH)

    loop(1, R, greet)

    def block(i, tt):
        lane = pl.ds(pl.multiple_of(tt * Q, Q), Q)
        if i < 3:
            half_lane = pl.ds(pl.multiple_of(lax.rem(tt, 2) * Q, Q), Q)
            return s.wei.at[tt // 2, pl.ds((0, 2 * L, L)[i], L), half_lane]
        if i == 3:
            return s.weo.at[lane, :]
        if i < 6:
            return s.wni.at[pl.ds((L, 0)[i - 4], L), lane]
        if i == 6:
            return s.wno.at[lane, :]
        return s.bias.at[:, lane]

    def weight_copy(i, way, who):
        ref = block(i, who)
        return remote(ref, ref, s.wsend.at[i, way], s.wrecv.at[i, way], (r, (pair, far, pair)[way]))

    def weight_send(i):
        weight_copy(i, 1, t).start()
        weight_copy(i, 0, t).start()

    def weight_wait(i, way):
        weight_copy(i, way, (pair, far, diag)[way]).wait_recv()

    def weight_forward(i):
        weight_wait(i, 1)
        weight_copy(i, 2, far).start()

    loads[0].wait()
    for i in range(3):
        at = pl.ds((0, 2 * L, L)[i], L)
        s.wei[h, at, core_lane] = s.wei32[at, :].astype(BF)
    s.bias[0:2, own_lane] = s.hb[...]
    s.bias[2:8, own_lane] = jnp.zeros((6, Q), F32)
    loads[1].wait()

    turned = jnp.transpose(s.serve[...].astype(F32))
    for k in range(R):
        s.serve_col[k * CAP : (k + 1) * CAP, :] = turned[:, k : k + 1]

    def serve(k):
        at = rows_of(k * TILE, TILE)
        table = s.serve_col[at, :].astype(jnp.int32) == lax.broadcasted_iota(jnp.int32, (TILE, N), 1)
        table = jnp.where(table, 1.0, 0.0)
        s.serve_t[:, pl.ds(pl.multiple_of(k * TILE, TILE), TILE)] = jnp.transpose(table).astype(BF)
        s.served[at, :] = mm(table.astype(BF), s.nf[:, col_lane]).astype(BF)

    loop(0, slot_tiles, serve)
    pl.semaphore_wait(barrier, R + 2)

    for i in range(3):
        weight_send(i)
    weight_send(7)
    mine = rows_of(r * CAP, CAP)

    def served_copy(k):
        to = lax.rem(r + k, R)
        return remote(
            s.served.at[rows_of(to * CAP, CAP)],
            s.slots.at[mine, col_lane],
            s.ssend.at[k],
            s.srecv.at[k],
            (to, t),
        )

    loop(1, R, lambda k: served_copy(k).start())
    s.slots[mine, col_lane] = s.served[mine, :]
    loads[3].wait()
    s.weo[own_lane, :] = s.weo32[...].astype(BF)
    weight_send(3)
    loads[4].wait()
    for i in (4, 5):
        at = pl.ds((L, 0)[i - 4], L)
        s.wni[at, own_lane] = s.wni32[at, :].astype(BF)
        weight_send(i)
    loads[5].wait()
    s.wno[own_lane, :] = s.wno32[...].astype(BF)
    weight_send(6)

    per = EH // LANES
    at = rows_of(c * per, per, 8)
    for source, target in ((s.rec2, s.rcol), (s.slot2, s.scol), (s.mask2, s.mcol)):
        turned = jnp.transpose(source[at, :].astype(F32))
        for k in range(per):
            target[k * LANES : (k + 1) * LANES, :] = turned[:, k : k + 1]
    lanes_here = pl.ds(pl.multiple_of(edge0, EH), EH)
    s.rhot_t[...] = hot(s.rec1[:, lanes_here] == lax.broadcasted_iota(jnp.int32, (N, EH), 0))

    def slot_table(k):
        rows = rows_of(k * TILE, TILE)
        s.shot_t[rows, :] = hot(
            s.slot1[:, lanes_here] == lax.broadcasted_iota(jnp.int32, (TILE, EH), 0) + k * TILE
        )

    loop(0, slot_tiles, slot_table)

    def receivers(k):
        rows = rows_of(k * TILE, TILE)
        index = s.rcol[rows, :].astype(jnp.int32)
        table = hot(index == lax.broadcasted_iota(jnp.int32, (TILE, N), 1))
        s.rhot[rows, :] = table
        s.xr[rows, :] = mm(table, s.nf[...]).astype(BF)

    loop(0, tiles, receivers)
    s.g[...] = jnp.zeros_like(s.g)
    loads[2].wait()

    def first_edges(which):
        def body(k):
            rows = rows_of(k * TILE, TILE)
            s.pre[which, rows, :] = mm(s.ef[rows, :], s.wei[which, 0:L, :])

        loop(0, tiles, body)

    def first_more(which, source, low):
        def body(k):
            rows = rows_of(k * TILE, TILE)
            s.pre[which, rows, :] += mm(source[rows, :], s.wei[which, low : low + L, :])

        loop(0, tiles, body)

    weight_wait(0, 0)
    first_edges(h)
    weight_wait(1, 0)
    first_more(h, s.xr, 2 * L)
    weight_forward(0)

    def served_wait(k):
        source = lax.rem(r + R - k, R)
        ref = s.slots.at[rows_of(source * CAP, CAP), col_lane]
        remote(ref, ref, s.ssend.at[k], s.srecv.at[k], (source, t)).wait_recv()

    loop(1, R, served_wait)
    slot_swap = remote(s.slots.at[:, col_lane], s.slots.at[:, col_lane], s.xsend.at[2], s.xrecv.at[2], (r, pair))
    slot_swap.start()
    weight_wait(0, 2)
    first_edges(oh)
    weight_forward(1)
    other_lane = pl.ds(pl.multiple_of(oc * LH, LH), LH)
    ref = s.slots.at[:, other_lane]
    remote(ref, ref, s.xsend.at[2], s.xrecv.at[2], (r, pair)).wait_recv()

    def senders(k):
        rows = rows_of(k * TILE, TILE)
        index = s.scol[rows, :].astype(jnp.int32)
        table = hot(index == lax.broadcasted_iota(jnp.int32, (TILE, S), 1))
        s.xs[rows, :] = mm(table, s.slots[...]).astype(BF)

    loop(0, tiles, senders)
    weight_wait(2, 0)
    first_more(h, s.xs, L)
    weight_wait(1, 2)
    first_more(oh, s.xr, 2 * L)
    weight_forward(2)
    weight_forward(7)
    weight_forward(3)
    weight_wait(2, 2)
    first_more(oh, s.xs, L)
    weight_wait(7, 0)
    weight_wait(7, 2)
    weight_wait(3, 0)
    weight_wait(3, 2)

    s.aggp[...] = jnp.zeros_like(s.aggp)

    def out_copies(k, source, target, which):
        here = source.at[rows_of(k * TILE, TILE)]
        there = target.at[rows_of(edge0 + k * TILE, TILE)]
        keep = local(here, there, s.osem.at[which, k])
        send = remote(here, there, s.osend.at[which, k], s.orecv.at[which, k], (r, pair))
        return keep, send

    def out_start(k, source, target, which):
        keep, send = out_copies(k, source, target, which)
        keep.start()
        send.start()

    def out_wait(k, source, target, which):
        keep, send = out_copies(k, source, target, which)
        keep.wait()
        send.wait_send()
        ref = target.at[rows_of(oc * EH + k * TILE, TILE)]
        remote(ref, ref, s.osend.at[which, k], s.orecv.at[which, k], (r, pair)).wait_recv()

    def forward(k):
        rows = rows_of(k * TILE, TILE)
        hidden = []
        for p in (0, 1):
            pre = s.pre[p, rows, :] + s.bias[0:1, p * half : (p + 1) * half]
            sig = 1.0 / (1.0 + jnp.exp(-pre))
            value = (pre * sig).astype(BF)
            s.hid[p, rows, :] = value
            s.pre[p, rows, :] = sig * (1.0 + pre * (1.0 - sig))
            hidden.append(value)
        outer = mm(hidden[0], s.weo[0:half, :]) + mm(hidden[1], s.weo[half:H, :]) + s.fv[0:1, :]
        normed, inverse = normalize(outer)
        s.normed[rows, :] = normed
        s.inv[rows, :] = inverse
        masked = s.mcol[rows, :] * (normed * s.fv[1:2, :] + s.fv[2:3, :])
        s.ne[rows, :] = (s.ef[rows, :].astype(F32) + masked).astype(BF)
        out_start(k, s.ne, s.ne_h, 0)
        high, low = two(masked)
        table = s.rhot_t[:, pl.ds(pl.multiple_of(k * TILE, TILE), TILE)]
        s.aggp[...] += mm(table, high) + mm(table, low)

    loop(0, tiles, forward)
    swap = remote(s.aggp, s.aggr, s.xsend.at[0], s.xrecv.at[0], (r, pair))
    swap.start()
    weight_wait(5, 0)
    weight_forward(4)
    weight_forward(5)
    weight_wait(5, 2)
    own_term = mm(s.nf[...], s.wni[0:L, :])
    weight_wait(4, 0)
    weight_wait(4, 2)
    swap.wait()

    agg = (s.aggp[...] + s.aggr[...]).astype(BF)
    pre = own_term + mm(agg, s.wni[L : 2 * L, :]) + s.bias[1:2, :]
    sig = 1.0 / (1.0 + jnp.exp(-pre))
    node_hidden = (pre * sig).astype(BF)
    slope_of = sig * (1.0 + pre * (1.0 - sig))
    weight_forward(6)
    weight_wait(6, 0)
    weight_wait(6, 2)
    outer = mm(node_hidden, s.wno[...]) + s.fv[3:4, :]
    normed, inverse = normalize(outer)
    s.nn[...] = (s.nf[...].astype(F32) + (normed * s.fv[4:5, :] + s.fv[5:6, :])).astype(BF)
    nn_copy = local(s.nn, s.nn_h, s.nsem.at[0])
    nn_copy.start()
    loads[6].wait()
    up = s.ncot[...].astype(F32)
    node_outer_grad = norm_back(up * s.fv[4:5, :], normed, inverse).astype(BF)
    node_slope = (nt(node_outer_grad, s.wno[...]) * slope_of).astype(BF)
    agg_high, agg_low = two(nt(node_slope, s.wni[L : 2 * L, :]))
    s.agh[...] = agg_high
    s.agl[...] = agg_low

    for q in range(H // Q):
        s.nsl[q] = node_slope[:, q * Q : (q + 1) * Q]
        s.nhid[q] = node_hidden[:, q * Q : (q + 1) * Q]
    s.vsum[...] = jnp.zeros_like(s.vsum)
    s.vsum[3:4, :] = 0.5 * row_sum(node_outer_grad.astype(F32))
    s.vsum[4:5, :] = 0.5 * row_sum(up * normed)
    s.vsum[5:6, :] = 0.5 * row_sum(up)
    base_node, base_out, base_in, base_vec = d.base_node, d.base_out, d.base_in, d.base_in + 3 * L
    s.g[c, 0:L, :] = tn(s.nf[...], s.nsl[t])
    s.g[c, L : 2 * L, :] = tn(agg, s.nsl[t])
    node_out_grad = tn(s.nhid[t], node_outer_grad)
    for q in range(L // LANES):
        s.g[c, 2 * L + q * Q : 2 * L + (q + 1) * Q, :] = node_out_grad[:, q * LANES : (q + 1) * LANES]

    chunks = ((base_node, d.size_node), (base_out, d.size_out), (base_in, d.size_in))

    def piece(n, q, bb):
        base, size = chunks[n]
        count = size // R
        return rows_of(base + (q * nb + bb) * count, count)

    def pair_copy(n):
        at = pl.ds(*chunks[n])
        return remote(s.sb.at[at], s.rbp.at[at], s.psend.at[n], s.precv.at[n], (r, pair))

    def pair_start(n):
        at = pl.ds(*chunks[n])
        s.sb[at, :] = s.g[oc, at, :].astype(BF)
        pair_copy(n).start()

    def pair_finish(n):
        pair_copy(n).wait()
        at = pl.ds(*chunks[n])
        if n == 2:
            vec = pl.ds(base_vec, 32)
            s.g[c, vec, :] = s.g[c, vec, :].astype(BF).astype(F32)
        s.g[c, at, :] += s.rbp[at, :].astype(F32)

    def a_row(j):
        return b * 4 + lax.rem(a + j, 4)

    def b_row(j):
        return lax.rem(b + j, nb) * 4 + a

    def a_copy(n, jj, j, q):
        at = piece(n, q, lax.rem(b + jj, nb))
        return remote(s.sb.at[at], s.rba.at[j - 1, at], s.asend.at[n, jj, j], s.arecv.at[n, jj, j], (a_row(j), t))

    def b_slot(n):
        base, size = chunks[n]
        return pl.ds(base // R, size // R)

    def b_copy(n, jj, bb):
        return remote(
            s.sb.at[piece(n, a, bb)],
            s.rbb.at[jj - 1, b_slot(n)],
            s.bsend.at[n, jj],
            s.brecv.at[n, jj],
            (b_row(jj), t),
        )

    order = (*range(1, nb), 0)

    def a_send(n):
        at = pl.ds(*chunks[n])
        s.sb[at, :] = s.g[c, at, :].astype(BF)
        for jj in order:
            for j in (1, 2, 3):
                a_copy(n, jj, j, lax.rem(a + j, 4)).start()

    def a_sum(n, jj):
        at = piece(n, a, lax.rem(b + jj, nb))
        for j in (1, 2, 3):
            a_copy(n, jj, j, a).wait_recv()
        return s.g[c, at, :] + (
            s.rba[0, at, :].astype(F32) + s.rba[1, at, :].astype(F32) + s.rba[2, at, :].astype(F32)
        )

    def b_send(n):
        for jj in range(1, nb):
            at = piece(n, a, lax.rem(b + jj, nb))
            s.sb[at, :] = a_sum(n, jj).astype(BF)
            b_copy(n, jj, lax.rem(b + jj, nb)).start()

    def to_b(n, jj):
        ref = s.fin.at[piece(n, a, b)]
        return remote(ref, ref, s.fbsend.at[n, jj], s.fbrecv.at[n, jj], (b_row(jj), t))

    def to_a(n, jj, j):
        ref = s.fin.at[piece(n, a, lax.rem(b + nb - jj, nb))]
        return remote(ref, ref, s.fasend.at[n, jj, j], s.farecv.at[n, jj, j], (a_row(j), t))

    def b_finish(n):
        total = a_sum(n, 0)
        at = piece(n, a, b)
        for jj in range(1, nb):
            b_copy(n, jj, b).wait_recv()
            total = total + s.rbb[jj - 1, b_slot(n), :].astype(F32)
        final = total.astype(BF)
        s.fin[at, :] = final
        for jj in range(1, nb):
            to_b(n, jj).start()
        for j in (1, 2, 3):
            to_a(n, 0, j).start()
        final = final.astype(F32)
        squares = final * final
        count = squares.shape[0]
        if n == 2:
            index = lax.broadcasted_iota(jnp.int32, (count, LANES), 0) + (base_in + (a * nb + b) * count)
            copied = jnp.logical_and(index >= base_vec, index < base_vec + 24)
            squares = jnp.where(copied, 0.25 * squares, squares)
        s.norm_a[mine8, :] += jnp.sum(squares.reshape(count // 8, 8, LANES), axis=0)

    def spread(n):
        for jj in range(1, nb):
            ref = s.fin.at[piece(n, a, lax.rem(b + nb - jj, nb))]
            remote(ref, ref, s.fbsend.at[n, jj], s.fbrecv.at[n, jj], (b_row(jj), t)).wait_recv()
            for j in (1, 2, 3):
                to_a(n, jj, j).start()

    def spread_wait(n):
        for jj in range(nb):
            for j in (1, 2, 3):
                ref = s.fin.at[piece(n, lax.rem(a + 4 - j, 4), lax.rem(b + nb - jj, nb))]
                remote(ref, ref, s.fasend.at[n, jj, j], s.farecv.at[n, jj, j], (a_row(j), t)).wait_recv()

    def sums_done(n):
        for jj in range(nb):
            for j in (1, 2, 3):
                a_copy(n, jj, j, lax.rem(a + j, 4)).wait_send()
                to_a(n, jj, j).wait_send()
        for jj in range(1, nb):
            b_copy(n, jj, lax.rem(b + jj, nb)).wait_send()
            to_b(n, jj).wait_send()

    mine8 = rows_of(r * 8, 8, 8)
    s.norm_a[mine8, :] = jnp.zeros((8, LANES), F32)
    a_send(0)

    loads[7].wait()

    def backward_norm(k):
        rows = rows_of(k * TILE, TILE)
        table = s.rhot[rows, :]
        cot = s.ecot[rows, :].astype(F32)
        up = s.mcol[rows, :] * (cot + (mm(table, s.agh[...]) + mm(table, s.agl[...])))
        normed = s.normed[rows, :]
        grad = norm_back(up * s.fv[1:2, :], normed, s.inv[rows, :]).astype(BF)
        s.og[rows, :] = grad
        s.vsum[0:1, :] += row_sum(grad.astype(F32))
        s.vsum[1:2, :] += row_sum(up * normed)
        s.vsum[2:3, :] += row_sum(up)

    loop(0, tiles, backward_norm)
    out_part = tn(s.hid[h], s.og[...])
    for p in (0, 1):
        for q in range(L // LANES):
            at = base_out + q * Q
            s.g[p, at : at + Q, :] = out_part[p * Q : (p + 1) * Q, q * LANES : (q + 1) * LANES]
    pair_start(1)

    def slope_half(which, k):
        rows = rows_of(k * TILE, TILE)
        w_rows = rows_of(which * half, half)
        value = (nt(s.og[rows, :], s.weo[w_rows, :]) * s.pre[which, rows, :]).astype(BF)
        s.sl[which, rows, :] = value
        lanes = pl.ds(pl.multiple_of(k * TILE, TILE), TILE)
        s.rs[which] += mm(s.rhot_t[:, lanes], value)

        def slots(j):
            at = rows_of(j * TILE, TILE)
            s.ss[which, at, :] += mm(s.shot_t[at, lanes], value)

        loop(0, slot_tiles, slots)
        return value

    s.rs[...] = jnp.zeros_like(s.rs)
    s.ss[...] = jnp.zeros_like(s.ss)

    def backward_own(k):
        value = slope_half(h, k)
        s.vsum[6:7, 0:half] += row_sum(value.astype(F32))

    loop(0, tiles, backward_own)

    edge_part = tn(s.ef[...], s.sl[h])
    recv_part = tn(s.nf[...], s.rs[h].astype(BF))
    for p in (0, 1):
        cols = slice(p * Q, (p + 1) * Q)
        s.g[p, base_in : base_in + L, :] = edge_part[:, cols]
        s.g[p, base_in + 2 * L : base_in + 3 * L, :] = recv_part[:, cols]
        for j in range(6):
            for q in range(L // LANES):
                at = base_vec + j * (L // LANES) + q
                s.g[p, at : at + 1, :] = s.vsum[j : j + 1, q * LANES : (q + 1) * LANES]
        s.g[p, base_vec + 24 : base_vec + 25, :] = s.vsum[6:7, cols]
        s.g[p, base_vec + 25 : base_vec + 26, :] = 0.5 * row_sum(s.nsl[2 * h + p].astype(F32))

    def sender_part(k):
        at = rows_of(k * TILE, TILE)
        value = tn(s.slots[at, :], s.ss[h, at, :].astype(BF))
        for p in (0, 1):
            s.g[p, base_in + L : base_in + 2 * L, :] += value[:, p * Q : (p + 1) * Q]

    loop(0, slot_tiles, sender_part)
    pair_start(2)
    pair_finish(1)
    a_send(1)
    pair_finish(2)
    a_send(2)
    b_send(0)

    def backward_other(k):
        rows = rows_of(k * TILE, TILE)
        value = slope_half(oh, k)
        cot = s.ecot[rows, :].astype(F32)
        back = nt(s.sl[0, rows, :], s.wei[0, 0:L, :]) + nt(s.sl[1, rows, :], s.wei[1, 0:L, :])
        s.eg[rows, :] = (cot + back).astype(BF)
        out_start(k, s.eg, s.eg_h, 1)

    loop(0, tiles, backward_other)
    b_finish(0)
    b_send(1)
    b_send(2)

    def slot_grad(which, rows):
        at = rows_of(L + which * LH, LH)
        return nt(s.ss[0, rows, :].astype(BF), s.wei[0, at, :]) + nt(s.ss[1, rows, :].astype(BF), s.wei[1, at, :])

    def recv_grad(which):
        at = rows_of(2 * L + which * LH, LH)
        return nt(s.rs[0].astype(BF), s.wei[0, at, :]) + nt(s.rs[1].astype(BF), s.wei[1, at, :])

    def slot_other(k):
        rows = rows_of(k * TILE, TILE)
        s.tosend[rows, :] = slot_grad(oc, rows).astype(BF)

    loop(0, slot_tiles, slot_other)
    s.tosend[S : S + N, :] = recv_grad(oc).astype(BF)
    grad_swap = remote(s.tosend, s.torecv, s.xsend.at[1], s.xrecv.at[1], (r, pair))
    grad_swap.start()
    s.ntp[...] = (
        s.ncot[:, col_lane].astype(F32)
        + (nt(s.nsl[0], s.wni[rows_of(c * LH, LH), 0:Q]) + nt(s.nsl[1], s.wni[rows_of(c * LH, LH), Q : 2 * Q]))
        + (
            nt(s.nsl[2], s.wni[rows_of(c * LH, LH), 2 * Q : 3 * Q])
            + nt(s.nsl[3], s.wni[rows_of(c * LH, LH), 3 * Q : 4 * Q])
        )
        + recv_grad(c)
    )
    b_finish(1)
    grad_swap.wait_recv()

    def slot_own(k):
        rows = rows_of(k * TILE, TILE)
        s.served[rows, :] = (slot_grad(c, rows) + s.torecv[rows, :].astype(F32)).astype(BF)

    loop(1, R, lambda k: served_copy(k).wait_send())
    loop(0, slot_tiles, slot_own)

    def back_copy(k):
        to = lax.rem(r + k, R)
        return remote(s.served.at[rows_of(to * CAP, CAP)], s.ret.at[mine], s.ksend.at[k], s.krecv.at[k], (to, t))

    b_finish(2)

    def norm_row(k):
        to = lax.rem(r + k, R)
        ref = s.norm_a.at[mine8]
        return remote(ref, ref, s.qsend.at[k], s.qrecv.at[k], (to, t))

    loop(1, R, lambda k: norm_row(k).start())
    loop(1, R, lambda k: back_copy(k).start())
    s.ret[mine, :] = s.served[mine, :]
    s.ntp[...] += s.torecv[S : S + N, :].astype(F32)
    for n in (0, 1, 2):
        spread(n)

    def norm_row_wait(k):
        source = lax.rem(r + R - k, R)
        ref = s.norm_a.at[rows_of(source * 8, 8, 8)]
        remote(ref, ref, s.qsend.at[k], s.qrecv.at[k], (source, t)).wait_recv()
        norm_row(k).wait_send()

    loop(1, R, norm_row_wait)
    own_rows = rows_of(t * 8, 8, 8)
    s.nsq[own_rows, :] = jnp.sum(s.norm_a[...].reshape(R, 8, LANES), axis=0)
    for k, peer in enumerate((pair, far, diag)):
        ref = s.nsq.at[own_rows]
        remote(ref, ref, s.tsem.at[0, k], s.tsem.at[1, k], (r, peer)).start()

    def back_wait(k):
        source = lax.rem(r + R - k, R)
        ref = s.ret.at[rows_of(source * CAP, CAP)]
        remote(ref, ref, s.ksend.at[k], s.krecv.at[k], (source, t)).wait_recv()
        back_copy(k).wait_send()

    loop(1, R, back_wait)

    def gathered(k):
        lanes = pl.ds(pl.multiple_of(k * TILE, TILE), TILE)
        s.ntp[...] += mm(s.serve_t[:, lanes], s.ret[rows_of(k * TILE, TILE), :])

    loop(0, slot_tiles, gathered)
    s.ng[...] = s.ntp[...].astype(BF)
    ng_keep = local(s.ng, s.ng_h.at[:, col_lane], s.nsem.at[1])
    ng_keep.start()
    ng_send = remote(s.ng, s.ng_h.at[:, col_lane], s.xsend.at[3], s.xrecv.at[3], (r, pair))
    ng_send.start()

    for n in (0, 1, 2):
        spread_wait(n)
    s.fin_o[...] = s.fin[...]
    for k, peer in enumerate((pair, far, diag)):
        ref = s.nsq.at[rows_of(peer * 8, 8, 8)]
        remote(ref, ref, s.tsem.at[0, k], s.tsem.at[1, k], (r, peer)).wait()
    total = s.nsq[0:8, :] + s.nsq[8:16, :] + s.nsq[16:24, :] + s.nsq[24:32, :]
    s.norm_o[...] = jnp.sqrt(jnp.full((8, LANES), jnp.sum(total), F32))
    for n in (0, 1, 2):
        sums_done(n)
    for i in range(8):
        weight_copy(i, 0, t).wait_send()
        weight_copy(i, 1, t).wait_send()
        weight_copy(i, 2, far).wait_send()
    slot_swap.wait_send()
    grad_swap.wait_send()

    def finish(k):
        out_wait(k, s.ne, s.ne_h, 0)
        out_wait(k, s.eg, s.eg_h, 1)

    loop(0, tiles, finish)
    nn_copy.wait()
    ng_keep.wait()
    ng_send.wait_send()
    ref = s.ng_h.at[:, other_lane]
    remote(ref, ref, s.xsend.at[3], s.xrecv.at[3], (r, pair)).wait_recv()


def adam(weight, first, second, gradient, factor, rate):
    clipped = gradient * factor
    first_new = beta_one * first + (1.0 - beta_one) * clipped
    second_new = beta_two * second + (1.0 - beta_two) * clipped * clipped
    bias_one = 1.0 - beta_one**adam_step
    bias_two = 1.0 - beta_two**adam_step
    moved = first_new / bias_one / (jnp.sqrt(second_new / bias_two) + adam_eps) + decay_rate * weight
    return weight - rate * moved, first_new, second_new


def update(names, d, *refs):
    s = types.SimpleNamespace(**dict(zip(names, refs, strict=True)))
    L, Q = d.L, d.Q
    passes = [
        pltpu.make_async_copy(s.__dict__[f"pass{k}"], s.__dict__[f"out{k}"], s.psem.at[k]) for k in range(4)
    ]
    for copy in passes:
        copy.start()
    norm = s.norm[0:1, 0:1]
    s.norm_o[0] = s.norm[0, 0]
    factor = clip_level / jnp.maximum(norm, clip_level)
    copies = []

    def one(k, grad, at, rate):
        values = adam(
            s.__dict__[f"in{k}"][at], s.__dict__[f"in{6 + k}"][at], s.__dict__[f"in{12 + k}"][at], grad, factor, rate
        )
        for n, value in enumerate(values):
            s.__dict__[f"buf{6 * n + k}"][at] = value

    def send(k):
        for n in range(3):
            m = 6 * n + k
            copy = pltpu.make_async_copy(s.__dict__[f"buf{m}"], s.__dict__[f"new{m}"], s.osem.at[m])
            copy.start()
            copies.append(copy)

    everything = (slice(None), slice(None))
    for k, base in ((2, d.base_node), (0, d.base_in)):
        for low in range(0, (2 if k == 2 else 3) * L, 256):
            rows = slice(low, low + 256)
            one(k, s.fin[base + low : base + low + 256, :].astype(F32), (rows, slice(None)), learn_rate)
        send(k)
    for k, base in ((3, d.base_node + 2 * L), (1, d.base_out)):
        for q in range(L // LANES):
            at = (slice(None), slice(q * LANES, (q + 1) * LANES))
            one(k, s.fin[base + q * LANES : base + (q + 1) * LANES, :].astype(F32), at, learn_rate)
        send(k)
    vec = s.fin[d.base_in + 3 * L : d.base_in + 3 * L + 32, :].astype(F32)
    one(4, vec[24:26, :], everything, vector_rate)
    send(4)
    for j in range(6):
        for q in range(L // LANES):
            m = j * (L // LANES) + q
            at = (slice(j, j + 1), slice(q * LANES, (q + 1) * LANES))
            one(5, vec[m : m + 1, :], at, vector_rate)
    send(5)
    for copy in copies + passes:
        copy.wait()


def device_step(
    node_feats,
    edge_feats,
    edge_receiver,
    edge_slot,
    edge_mask,
    serve_rows,
    node_cot,
    edge_cot,
    *states,
):
    weights = states[:6]
    d = types.SimpleNamespace()
    d.R = lax.axis_size("rows")
    d.N, d.L = node_feats.shape
    d.E = edge_feats.shape[0]
    d.Q = weights[0].shape[1]
    d.H = d.Q * lax.axis_size("tp")
    d.CAP = serve_rows.shape[1]
    R, N, E, L, H, Q = d.R, d.N, d.E, d.L, d.H, d.Q
    EH, S, nb = E // 2, R * d.CAP, R // 4
    tiles = EH // TILE

    def padded(count):
        return -(-count // (16 * R)) * (16 * R)

    d.size_node, d.size_out, d.size_in = padded(3 * L), padded(L), padded(3 * L + 32)
    d.base_node, d.base_out, d.base_in = 0, d.size_node, d.size_node + d.size_out
    G = d.size_node + d.size_out + d.size_in
    any_spec = pl.BlockSpec(memory_space=pl.ANY)
    vmem_spec = pl.BlockSpec(memory_space=pltpu.VMEM)
    inputs = dict(
        nf_h=(node_feats, any_spec),
        ef_h=(edge_feats, any_spec),
        ncot_h=(node_cot, any_spec),
        ecot_h=(edge_cot, any_spec),
        wei_h=(weights[0], any_spec),
        weo_h=(weights[1], any_spec),
        wni_h=(weights[2], any_spec),
        wno_h=(weights[3], any_spec),
        hb=(weights[4], vmem_spec),
        fv=(weights[5], vmem_spec),
        rec2=(edge_receiver.reshape(-1, LANES), vmem_spec),
        slot2=(edge_slot.reshape(-1, LANES), vmem_spec),
        mask2=(edge_mask.reshape(-1, LANES), vmem_spec),
        rec1=(edge_receiver.reshape(1, -1), vmem_spec),
        slot1=(edge_slot.reshape(1, -1), vmem_spec),
        serve=(serve_rows, vmem_spec),
    )
    outputs = dict(
        nn_h=(jax.ShapeDtypeStruct((N, L), BF), any_spec),
        ne_h=(jax.ShapeDtypeStruct((E, L), BF), any_spec),
        ng_h=(jax.ShapeDtypeStruct((N, L), BF), any_spec),
        eg_h=(jax.ShapeDtypeStruct((E, L), BF), any_spec),
        fin_o=(jax.ShapeDtypeStruct((G, Q), BF), vmem_spec),
        norm_o=(jax.ShapeDtypeStruct((8, LANES), F32), vmem_spec),
    )
    dma = pltpu.SemaphoreType.DMA
    scratch = dict(
        wei32=pltpu.VMEM((3 * L, Q), F32),
        weo32=pltpu.VMEM((Q, L), F32),
        wni32=pltpu.VMEM((2 * L, Q), F32),
        wno32=pltpu.VMEM((Q, L), F32),
        nf=pltpu.VMEM((N, L), BF),
        ef=pltpu.VMEM((EH, L), BF),
        ncot=pltpu.VMEM((N, L), BF),
        ecot=pltpu.VMEM((EH, L), BF),
        wei=pltpu.VMEM((2, 3 * L, H // 2), BF),
        weo=pltpu.VMEM((H, L), BF),
        wni=pltpu.VMEM((2 * L, H), BF),
        wno=pltpu.VMEM((H, L), BF),
        bias=pltpu.VMEM((8, H), F32),
        serve_col=pltpu.VMEM((S, 1), F32),
        serve_t=pltpu.VMEM((N, S), BF),
        served=pltpu.VMEM((S, L // 2), BF),
        slots=pltpu.VMEM((S, L), BF),
        ret=pltpu.VMEM((S, L // 2), BF),
        rcol=pltpu.VMEM((EH, 1), F32),
        scol=pltpu.VMEM((EH, 1), F32),
        mcol=pltpu.VMEM((EH, 1), F32),
        rhot=pltpu.VMEM((EH, N), BF),
        rhot_t=pltpu.VMEM((N, EH), BF),
        shot_t=pltpu.VMEM((S, EH), BF),
        xr=pltpu.VMEM((EH, L), BF),
        xs=pltpu.VMEM((EH, L), BF),
        pre=pltpu.VMEM((2, EH, H // 2), F32),
        hid=pltpu.VMEM((2, EH, H // 2), BF),
        normed=pltpu.VMEM((EH, L), F32),
        inv=pltpu.VMEM((EH, 1), F32),
        ne=pltpu.VMEM((EH, L), BF),
        eg=pltpu.VMEM((EH, L), BF),
        aggp=pltpu.VMEM((N, L), F32),
        aggr=pltpu.VMEM((N, L), F32),
        nn=pltpu.VMEM((N, L), BF),
        ng=pltpu.VMEM((N, L // 2), BF),
        agh=pltpu.VMEM((N, L), BF),
        agl=pltpu.VMEM((N, L), BF),
        ntp=pltpu.VMEM((N, L // 2), F32),
        nsl=pltpu.VMEM((H // Q, N, Q), BF),
        nhid=pltpu.VMEM((H // Q, N, Q), BF),
        og=pltpu.VMEM((EH, L), BF),
        sl=pltpu.VMEM((2, EH, H // 2), BF),
        rs=pltpu.VMEM((2, N, H // 2), F32),
        ss=pltpu.VMEM((2, S, H // 2), F32),
        tosend=pltpu.VMEM((S + N, L // 2), BF),
        torecv=pltpu.VMEM((S + N, L // 2), BF),
        g=pltpu.VMEM((2, G, Q), F32),
        sb=pltpu.VMEM((G, Q), BF),
        rbp=pltpu.VMEM((G, Q), BF),
        rba=pltpu.VMEM((3, G, Q), BF),
        rbb=pltpu.VMEM((nb - 1, G // R, Q), BF),
        fin=pltpu.VMEM((G, Q), BF),
        vsum=pltpu.VMEM((8, L), F32),
        norm_a=pltpu.VMEM((8 * R, LANES), F32),
        nsq=pltpu.VMEM((32, LANES), F32),
        lsem=dma((8,)),
        wsend=dma((8, 3)),
        wrecv=dma((8, 3)),
        ssend=dma((R,)),
        srecv=dma((R,)),
        ksend=dma((R,)),
        krecv=dma((R,)),
        qsend=dma((R,)),
        qrecv=dma((R,)),
        osem=dma((2, tiles)),
        osend=dma((2, tiles)),
        orecv=dma((2, tiles)),
        xsend=dma((4,)),
        xrecv=dma((4,)),
        nsem=dma((2,)),
        psend=dma((3,)),
        precv=dma((3,)),
        asend=dma((3, nb, 4)),
        arecv=dma((3, nb, 4)),
        bsend=dma((3, nb)),
        brecv=dma((3, nb)),
        fbsend=dma((3, nb)),
        fbrecv=dma((3, nb)),
        fasend=dma((3, nb, 4)),
        farecv=dma((3, nb, 4)),
        tsem=dma((2, 3)),
    )
    names = (*inputs, *outputs, *scratch)
    limit = 6 * 1024 * 1024
    for x in scratch.values():
        if x.memory_space == pltpu.VMEM:
            *lead, rows, lanes = x.shape
            limit += math.prod(lead) * rows * -(-lanes // LANES) * LANES * jnp.dtype(x.dtype).itemsize
    new_nodes, new_edges, node_gradient, edge_gradient, fin, norm = pl.pallas_call(
        functools.partial(layer, names, d),
        out_shape=[shape for shape, _ in outputs.values()],
        in_specs=[spec for _, spec in inputs.values()],
        out_specs=[spec for _, spec in outputs.values()],
        scratch_shapes=list(scratch.values()),
        compiler_params=pltpu.CompilerParams(
            collective_id=0, has_side_effects=True, vmem_limit_bytes=limit
        ),
    )(*[value for value, _ in inputs.values()])

    passes = (new_nodes, new_edges, node_gradient, edge_gradient)
    names = (
        "fin",
        "norm",
        *(f"pass{k}" for k in range(4)),
        *(f"in{k}" for k in range(18)),
        *(f"out{k}" for k in range(4)),
        "norm_o",
        *(f"new{k}" for k in range(18)),
        *(f"buf{k}" for k in range(18)),
        "psem",
        "osem",
    )
    outs = pl.pallas_call(
        functools.partial(update, names, d),
        out_shape=[
            *(jax.ShapeDtypeStruct(x.shape, x.dtype) for x in passes),
            jax.ShapeDtypeStruct((1,), F32),
            *(jax.ShapeDtypeStruct(x.shape, F32) for x in states),
        ],
        in_specs=[vmem_spec, vmem_spec, *[any_spec] * 4, *[vmem_spec] * 18],
        out_specs=[*[any_spec] * 4, pl.BlockSpec(memory_space=pltpu.SMEM), *[any_spec] * 18],
        scratch_shapes=[*(pltpu.VMEM(x.shape, F32) for x in states), dma((4,)), dma((18,))],
        compiler_params=pltpu.CompilerParams(vmem_limit_bytes=32 * 1024 * 1024),
    )(fin, norm, *passes, *states)
    return tuple(outs)


def solution(mesh):
    split = [P(None, "tp"), P("tp", None), P(None, "tp"), P("tp", None), P(None, "tp"), P()]
    row = P("rows", None)
    return jax.shard_map(
        device_step,
        mesh=mesh,
        in_specs=(row, row, P("rows"), P("rows"), P("rows"), row, row, row, *split, *split, *split),
        out_specs=(row, row, row, row, P(), *split, *split, *split),
        check_vma=False,
    )
```

```python
import functools
import math
import types

import jax
import jax.numpy as jnp
from jax import lax
from jax.experimental import pallas as pl
from jax.experimental.pallas import tpu as pltpu
from jax.sharding import PartitionSpec as P

BF = jnp.bfloat16
F32 = jnp.float32
MESH = pl.DeviceIdType.MESH
LANES = 128
TILE = 256
ROWS = 512

beta_one = 0.9
beta_two = 0.999
adam_step = 7.0
adam_eps = 1e-08
learn_rate = 0.05
vector_rate = 0.3
decay_rate = 0.1
clip_level = 1.0


def mm(left, right):
    return jnp.dot(left, right, preferred_element_type=F32)


def nt(left, right):
    return lax.dot_general(left, right, (((1,), (1,)), ((), ())), preferred_element_type=F32)


def tn(left, right):
    return lax.dot_general(left, right, (((0,), (0,)), ((), ())), preferred_element_type=F32)


def two(values):
    high = values.astype(BF)
    return high, (values - high.astype(F32)).astype(BF)


def aligned(start, step):
    return start if isinstance(start, int) else pl.multiple_of(start, step)


def rows_of(start, size, step=16):
    return pl.ds(aligned(start, step), size)


def hot(cond):
    return jnp.where(cond, 1.0, 0.0).astype(BF)


def normalize(values):
    center = values - jnp.mean(values, axis=1, keepdims=True)
    inverse = lax.rsqrt(jnp.mean(center * center, axis=1, keepdims=True) + 1e-05)
    return center * inverse, inverse


def norm_back(scaled, normed, inverse):
    first = jnp.mean(scaled, axis=1, keepdims=True)
    second = jnp.mean(scaled * normed, axis=1, keepdims=True)
    return inverse * (scaled - first - normed * second)


def row_sum(values):
    return jnp.sum(values, axis=0, keepdims=True)


def layer(names, d, *refs):
    s = types.SimpleNamespace(**dict(zip(names, refs, strict=True)))
    R, N, E, L, H, Q, CAP = d.R, d.N, d.E, d.L, d.H, d.Q, d.CAP
    EH, S, half, LH = E // 2, R * CAP, H // 2, L // 2
    tiles, slot_tiles, nb = EH // ROWS, S // TILE, R // 4
    r = lax.axis_index("rows")
    t = lax.axis_index("tp")
    h, c = t // 2, lax.rem(t, 2)
    oh, oc = 1 - h, 1 - c
    pair = t + 1 - 2 * c
    far = t + 2 - 4 * h
    diag = pair + 2 - 4 * h
    a, b = lax.rem(r, 4), r // 4
    edge0 = c * EH
    own_lane = pl.ds(pl.multiple_of(t * Q, Q), Q)
    core_lane = pl.ds(pl.multiple_of(c * Q, Q), Q)
    col_lane = pl.ds(pl.multiple_of(c * LH, LH), LH)

    def local(src, dst, sem):
        return pltpu.make_async_copy(src, dst, sem)

    def remote(src, dst, send, recv, device):
        return pltpu.make_async_remote_copy(
            src_ref=src, dst_ref=dst, send_sem=send, recv_sem=recv, device_id=device, device_id_type=MESH
        )

    def loop(low, high, body):
        def step(k, carry):
            body(k)
            return carry

        if high - low <= 8:
            for k in range(low, high):
                body(k)
        else:
            lax.fori_loop(low, high, step, 0)

    loads = [
        local(s.wei_h, s.wei32, s.lsem.at[0]),
        local(s.nf_h, s.nf, s.lsem.at[1]),
        local(s.ef_h.at[rows_of(edge0, EH)], s.ef, s.lsem.at[2]),
        local(s.weo_h, s.weo32, s.lsem.at[3]),
        local(s.wni_h, s.wni32, s.lsem.at[4]),
        local(s.wno_h, s.wno32, s.lsem.at[5]),
        local(s.ncot_h, s.ncot, s.lsem.at[6]),
        local(s.ecot_h.at[rows_of(edge0, EH)], s.ecot, s.lsem.at[7]),
        local(s.serve_h, s.serve, s.lsem.at[8]),
        local(s.hb_h, s.hb, s.lsem.at[9]),
        local(s.fv_h, s.fv, s.lsem.at[10]),
        local(s.rec2_h, s.rec2, s.lsem.at[11]),
        local(s.slot2_h, s.slot2, s.lsem.at[12]),
        local(s.mask2_h, s.mask2, s.lsem.at[13]),
        local(s.rec1_h, s.rec1, s.lsem.at[14]),
        local(s.slot1_h, s.slot1, s.lsem.at[15]),
    ]
    for k in (0, 1, 8, 9, 3, 11, 12, 13, 14, 15, 2, 4, 5, 10, 6, 7):
        loads[k].start()

    barrier = pltpu.get_barrier_semaphore()
    for peer in (pair, far, diag):
        pl.semaphore_signal(barrier, inc=1, device_id=(r, peer), device_id_type=MESH)

    def greet(k):
        pl.semaphore_signal(barrier, inc=1, device_id=(lax.rem(r + k, R), t), device_id_type=MESH)

    loop(1, R, greet)

    shared = (1, 2, 4, 5)

    def block(i, tt, part=None):
        lane = pl.ds(pl.multiple_of(tt * Q, Q), Q)
        if i < 3:
            half_lane = pl.ds(pl.multiple_of(lax.rem(tt, 2) * Q, Q), Q)
            rows = pl.ds((0, 2 * L, L)[i], L) if part is None else rows_of((0, 2 * L, L)[i] + part * (L // 4), L // 4)
            return s.wei.at[tt // 2, rows, half_lane]
        if i == 3:
            return s.weo.at[lane, :]
        if i < 6:
            low = (L, 0)[i - 4]
            return s.wni.at[pl.ds(low, L) if part is None else rows_of(low + part * (L // 4), L // 4), lane]
        if i == 6:
            return s.wno.at[lane, :]
        return s.bias.at[:, lane]

    def weight_copy(i, way, who):
        ref = block(i, who, a if way == 1 and i in shared else None)
        return remote(ref, ref, s.wsend.at[i, way], s.wrecv.at[i, way], (r, (pair, far, pair)[way]))

    def part_copy(i, j, part):
        ref = block(i, far, part)
        device = (b * 4 + lax.rem(a + j, 4), t)
        return remote(ref, ref, s.wsend.at[i, 2 + j], s.wrecv.at[i, 2 + j], device)

    def weight_send(i, way):
        weight_copy(i, way, t).start()

    def weight_wait(i, way):
        weight_copy(i, way, (pair, far, diag)[way]).wait_recv()

    def part_spread(i):
        weight_wait(i, 1)
        for j in (1, 2, 3):
            part_copy(i, j, a).start()

    def weight_forward(i):
        if i in shared:
            for j in (1, 2, 3):
                part_copy(i, j, lax.rem(a + 4 - j, 4)).wait_recv()
        else:
            weight_wait(i, 1)
        weight_copy(i, 2, far).start()

    loads[0].wait()
    for i in range(3):
        at = pl.ds((0, 2 * L, L)[i], L)
        s.wei[h, at, core_lane] = s.wei32[at, :].astype(BF)
    loads[9].wait()
    s.bias[0:2, own_lane] = s.hb[...]
    s.bias[2:8, own_lane] = jnp.zeros((6, Q), F32)
    loads[1].wait()

    loads[8].wait()
    turned = jnp.transpose(s.serve[...].astype(F32))
    for k in range(R):
        s.serve_col[k * CAP : (k + 1) * CAP, :] = turned[:, k : k + 1]

    def serve(k):
        at = rows_of(k * TILE, TILE)
        table = s.serve_col[at, :].astype(jnp.int32) == lax.broadcasted_iota(jnp.int32, (TILE, N), 1)
        table = jnp.where(table, 1.0, 0.0)
        s.serve_t[:, pl.ds(pl.multiple_of(k * TILE, TILE), TILE)] = jnp.transpose(table).astype(BF)
        s.served[at, :] = mm(table.astype(BF), s.nf[:, col_lane]).astype(BF)

    loop(0, slot_tiles, serve)
    pl.semaphore_wait(barrier, R + 2)

    for i in (1, 2, 7, 0):
        weight_send(i, 1)
    mine = rows_of(r * CAP, CAP)

    def served_copy(k):
        to = lax.rem(r + k, R)
        return remote(
            s.served.at[rows_of(to * CAP, CAP)],
            s.slots.at[mine, col_lane],
            s.ssend.at[k],
            s.srecv.at[k],
            (to, t),
        )

    loop(1, R, lambda k: served_copy(k).start())
    s.slots[mine, col_lane] = s.served[mine, :]
    for i in (0, 1, 2, 7):
        weight_send(i, 0)
    loads[4].wait()
    for i in (4, 5):
        at = pl.ds((L, 0)[i - 4], L)
        s.wni[at, own_lane] = s.wni32[at, :].astype(BF)
        weight_send(i, 1)
    loads[3].wait()
    s.weo[own_lane, :] = s.weo32[...].astype(BF)
    loads[5].wait()
    s.wno[own_lane, :] = s.wno32[...].astype(BF)
    for i in (3, 6):
        weight_send(i, 1)
    for i in (3, 4, 5, 6):
        weight_send(i, 0)

    for k in (11, 12, 13, 14, 15):
        loads[k].wait()
    per = EH // LANES
    at = rows_of(c * per, per, 8)
    for source, target in ((s.rec2, s.rcol), (s.slot2, s.scol), (s.mask2, s.mcol)):
        turned = jnp.transpose(source[at, :].astype(F32))
        for k in range(per):
            target[k * LANES : (k + 1) * LANES, :] = turned[:, k : k + 1]
    lanes_here = pl.ds(pl.multiple_of(edge0, EH), EH)
    s.rhot_t[...] = hot(s.rec1[:, lanes_here] == lax.broadcasted_iota(jnp.int32, (N, EH), 0))
    part_spread(1)
    part_spread(2)

    def slot_table(k):
        rows = rows_of(k * TILE, TILE)
        s.shot_t[rows, :] = hot(
            s.slot1[:, lanes_here] == lax.broadcasted_iota(jnp.int32, (TILE, EH), 0) + k * TILE
        )

    loop(0, slot_tiles, slot_table)

    def receivers(k):
        rows = rows_of(k * ROWS, ROWS)
        index = s.rcol[rows, :].astype(jnp.int32)
        table = hot(index == lax.broadcasted_iota(jnp.int32, (ROWS, N), 1))
        s.rhot[rows, :] = table
        s.xr[rows, :] = mm(table, s.nf[...]).astype(BF)

    loop(0, tiles, receivers)
    loads[2].wait()

    def first_two(which):
        def body(k):
            rows = rows_of(k * ROWS, ROWS)
            value = mm(s.ef[rows, :], s.wei[which, 0:L, :])
            s.pre[which, rows, :] = value + mm(s.xr[rows, :], s.wei[which, 2 * L : 3 * L, :])

        loop(0, tiles, body)

    def hidden_of(which, k):
        rows = rows_of(k * ROWS, ROWS)
        lanes = pl.ds(pl.multiple_of(which * half, half), half)
        pre = s.pre[which, rows, :] + mm(s.xs[rows, :], s.wei[which, L : 2 * L, :]) + s.bias[0:1, lanes]
        sig = 0.5 + 0.5 * jnp.tanh(0.5 * pre)
        value = (pre * sig).astype(BF)
        s.hid[which, rows, :] = value
        s.pre[which, rows, :] = sig + (pre * sig) * (1.0 - sig)
        return mm(value, s.weo[rows_of(which * half, half), :])

    for i in (0, 1):
        weight_wait(i, 0)
    first_two(h)
    s.g[...] = jnp.zeros_like(s.g)
    weight_forward(0)

    def served_wait(k):
        source = lax.rem(r + R - k, R)
        ref = s.slots.at[rows_of(source * CAP, CAP), col_lane]
        remote(ref, ref, s.ssend.at[k], s.srecv.at[k], (source, t)).wait_recv()

    loop(1, R, served_wait)
    slot_swap = remote(s.slots.at[:, col_lane], s.slots.at[:, col_lane], s.xsend.at[2], s.xrecv.at[2], (r, pair))
    slot_swap.start()
    weight_forward(1)
    other_lane = pl.ds(pl.multiple_of(oc * LH, LH), LH)
    ref = s.slots.at[:, other_lane]
    remote(ref, ref, s.xsend.at[2], s.xrecv.at[2], (r, pair)).wait_recv()

    def senders(k):
        rows = rows_of(k * ROWS, ROWS)
        index = s.scol[rows, :].astype(jnp.int32)
        table = hot(index == lax.broadcasted_iota(jnp.int32, (ROWS, S), 1))
        s.xs[rows, :] = mm(table, s.slots[...]).astype(BF)

    loop(0, tiles, senders)
    weight_forward(2)
    part_spread(4)
    part_spread(5)
    for i in (2, 7, 3):
        weight_wait(i, 0)

    def own_half(k):
        s.part[rows_of(k * ROWS, ROWS), :] = hidden_of(h, k)

    loop(0, tiles, own_half)
    weight_forward(7)
    for i in (0, 1):
        weight_wait(i, 2)
    first_two(oh)
    weight_forward(3)
    for i in (2, 7, 3):
        weight_wait(i, 2)
    loads[10].wait()

    def out_copies(k, source, target, which):
        here = source.at[rows_of(k * ROWS, ROWS)]
        there = target.at[rows_of(edge0 + k * ROWS, ROWS)]
        keep = local(here, there, s.osem.at[which, k])
        send = remote(here, there, s.osend.at[which, k], s.orecv.at[which, k], (r, pair))
        return keep, send

    def out_start(k, source, target, which):
        keep, send = out_copies(k, source, target, which)
        keep.start()
        send.start()

    def out_wait(k, source, target, which):
        keep, send = out_copies(k, source, target, which)
        keep.wait()
        send.wait_send()
        ref = target.at[rows_of(oc * EH + k * ROWS, ROWS)]
        remote(ref, ref, s.osend.at[which, k], s.orecv.at[which, k], (r, pair)).wait_recv()

    def forward(k):
        rows = rows_of(k * ROWS, ROWS)
        outer = s.part[rows, :] + hidden_of(oh, k) + s.fv[0:1, :]
        normed, inverse = normalize(outer)
        s.normed[rows, :] = normed
        s.inv[rows, :] = inverse
        masked = s.mcol[rows, :] * (normed * s.fv[1:2, :] + s.fv[2:3, :])
        s.ne[rows, :] = (s.ef[rows, :].astype(F32) + masked).astype(BF)
        out_start(k, s.ne, s.ne_h, 0)
        s.mk[rows, :] = masked.astype(BF)

    loop(0, tiles, forward)
    s.aggp[...] = mm(s.rhot_t[...], s.mk[...])
    swap = remote(s.aggp, s.aggr, s.xsend.at[0], s.xrecv.at[0], (r, pair))
    swap.start()
    for i in (4, 5, 6):
        weight_forward(i)
    weight_wait(5, 0)
    weight_wait(5, 2)
    own_term = mm(s.nf[...], s.wni[0:L, :])
    weight_wait(4, 0)
    weight_wait(4, 2)
    swap.wait()

    agg = (s.aggp[...] + s.aggr[...]).astype(BF)
    pre = own_term + mm(agg, s.wni[L : 2 * L, :]) + s.bias[1:2, :]
    sig = 0.5 + 0.5 * jnp.tanh(0.5 * pre)
    node_hidden = (pre * sig).astype(BF)
    slope_of = sig + (pre * sig) * (1.0 - sig)
    weight_wait(6, 0)
    weight_wait(6, 2)
    outer = mm(node_hidden, s.wno[...]) + s.fv[3:4, :]
    normed, inverse = normalize(outer)
    s.nn[...] = (s.nf[...].astype(F32) + (normed * s.fv[4:5, :] + s.fv[5:6, :])).astype(BF)
    nn_copy = local(s.nn, s.nn_h, s.nsem.at[0])
    nn_copy.start()
    loads[6].wait()
    up = s.ncot[...].astype(F32)
    node_outer_grad = norm_back(up * s.fv[4:5, :], normed, inverse).astype(BF)
    node_slope = (nt(node_outer_grad, s.wno[...]) * slope_of).astype(BF)
    s.agh[...] = nt(node_slope, s.wni[L : 2 * L, :]).astype(BF)

    for q in range(H // Q):
        s.nsl[q] = node_slope[:, q * Q : (q + 1) * Q]
        s.nhid[q] = node_hidden[:, q * Q : (q + 1) * Q]
    s.vsum[...] = jnp.zeros_like(s.vsum)
    s.vsum[3:4, :] = 0.5 * row_sum(node_outer_grad.astype(F32))
    s.vsum[4:5, :] = 0.5 * row_sum(up * normed)
    s.vsum[5:6, :] = 0.5 * row_sum(up)
    base_node, base_out, base_in, base_vec = d.base_node, d.base_out, d.base_in, d.base_in + 3 * L
    s.g[c, 0:L, :] = tn(s.nf[...], s.nsl[t])
    s.g[c, L : 2 * L, :] = tn(agg, s.nsl[t])
    node_out_grad = tn(s.nhid[t], node_outer_grad)
    for q in range(L // LANES):
        s.g[c, 2 * L + q * Q : 2 * L + (q + 1) * Q, :] = node_out_grad[:, q * LANES : (q + 1) * LANES]

    chunks = ((base_node, d.size_node), (base_out, d.size_out), (base_in, d.size_in))

    def piece(n, q, bb):
        base, size = chunks[n]
        count = size // R
        return rows_of(base + (q * nb + bb) * count, count)

    def pair_copy(n):
        at = pl.ds(*chunks[n])
        return remote(s.sb.at[at], s.rbp.at[at], s.psend.at[n], s.precv.at[n], (r, pair))

    def pair_start(n):
        at = pl.ds(*chunks[n])
        s.sb[at, :] = s.g[oc, at, :].astype(BF)
        pair_copy(n).start()

    def pair_finish(n):
        pair_copy(n).wait()
        at = pl.ds(*chunks[n])
        if n == 2:
            vec = pl.ds(base_vec, 32)
            s.g[c, vec, :] = s.g[c, vec, :].astype(BF).astype(F32)
        s.g[c, at, :] += s.rbp[at, :].astype(F32)

    def a_row(j):
        return b * 4 + lax.rem(a + j, 4)

    def b_row(j):
        return lax.rem(b + j, nb) * 4 + a

    def a_copy(n, jj, j, q):
        at = piece(n, q, lax.rem(b + jj, nb))
        return remote(s.sb.at[at], s.rba.at[j - 1, at], s.asend.at[n, jj, j], s.arecv.at[n, jj, j], (a_row(j), t))

    def b_slot(n):
        base, size = chunks[n]
        return pl.ds(base // R, size // R)

    def b_copy(n, jj, bb):
        return remote(
            s.sb.at[piece(n, a, bb)],
            s.rbb.at[jj - 1, b_slot(n)],
            s.bsend.at[n, jj],
            s.brecv.at[n, jj],
            (b_row(jj), t),
        )

    order = (*range(1, nb), 0)

    def a_send(n):
        at = pl.ds(*chunks[n])
        s.sb[at, :] = s.g[c, at, :].astype(BF)
        for jj in order:
            for j in (1, 2, 3):
                a_copy(n, jj, j, lax.rem(a + j, 4)).start()

    def a_sum(n, jj):
        at = piece(n, a, lax.rem(b + jj, nb))
        for j in (1, 2, 3):
            a_copy(n, jj, j, a).wait_recv()
        return s.g[c, at, :] + (
            s.rba[0, at, :].astype(F32) + s.rba[1, at, :].astype(F32) + s.rba[2, at, :].astype(F32)
        )

    def b_send(n):
        for jj in range(1, nb):
            at = piece(n, a, lax.rem(b + jj, nb))
            s.sb[at, :] = a_sum(n, jj).astype(BF)
            b_copy(n, jj, lax.rem(b + jj, nb)).start()

    def to_b(n, jj):
        ref = s.fin_o.at[piece(n, a, b)]
        return remote(ref, ref, s.fbsend.at[n, jj], s.fbrecv.at[n, jj], (b_row(jj), t))

    def to_a(n, jj, j):
        ref = s.fin_o.at[piece(n, a, lax.rem(b + nb - jj, nb))]
        return remote(ref, ref, s.fasend.at[n, jj, j], s.farecv.at[n, jj, j], (a_row(j), t))

    def b_finish(n):
        total = a_sum(n, 0)
        at = piece(n, a, b)
        for jj in range(1, nb):
            b_copy(n, jj, b).wait_recv()
            total = total + s.rbb[jj - 1, b_slot(n), :].astype(F32)
        final = total.astype(BF)
        s.fin_o[at, :] = final
        for jj in range(1, nb):
            to_b(n, jj).start()
        for j in (1, 2, 3):
            to_a(n, 0, j).start()
        final = final.astype(F32)
        squares = final * final
        count = squares.shape[0]
        if n == 2:
            index = lax.broadcasted_iota(jnp.int32, (count, LANES), 0) + (base_in + (a * nb + b) * count)
            copied = jnp.logical_and(index >= base_vec, index < base_vec + 24)
            squares = jnp.where(copied, 0.25 * squares, squares)
        s.norm_a[mine8, :] += jnp.sum(squares.reshape(count // 8, 8, LANES), axis=0)

    def spread(n):
        for jj in range(1, nb):
            ref = s.fin_o.at[piece(n, a, lax.rem(b + nb - jj, nb))]
            remote(ref, ref, s.fbsend.at[n, jj], s.fbrecv.at[n, jj], (b_row(jj), t)).wait_recv()
            for j in (1, 2, 3):
                to_a(n, jj, j).start()

    def spread_wait(n):
        for jj in range(nb):
            for j in (1, 2, 3):
                ref = s.fin_o.at[piece(n, lax.rem(a + 4 - j, 4), lax.rem(b + nb - jj, nb))]
                remote(ref, ref, s.fasend.at[n, jj, j], s.farecv.at[n, jj, j], (a_row(j), t)).wait_recv()

    def sums_done(n):
        for jj in range(nb):
            for j in (1, 2, 3):
                a_copy(n, jj, j, lax.rem(a + j, 4)).wait_send()
                to_a(n, jj, j).wait_send()
        for jj in range(1, nb):
            b_copy(n, jj, lax.rem(b + jj, nb)).wait_send()
            to_b(n, jj).wait_send()

    mine8 = rows_of(r * 8, 8, 8)
    s.norm_a[mine8, :] = jnp.zeros((8, LANES), F32)
    a_send(0)

    loads[7].wait()

    def backward_norm(k):
        rows = rows_of(k * ROWS, ROWS)
        table = s.rhot[rows, :]
        cot = s.ecot[rows, :].astype(F32)
        up = s.mcol[rows, :] * (cot + mm(table, s.agh[...]))
        normed = s.normed[rows, :]
        grad = norm_back(up * s.fv[1:2, :], normed, s.inv[rows, :]).astype(BF)
        s.og[rows, :] = grad
        s.vsum[0:1, :] += row_sum(grad.astype(F32))
        s.vsum[1:2, :] += row_sum(up * normed)
        s.vsum[2:3, :] += row_sum(up)

    loop(0, tiles, backward_norm)
    out_part = tn(s.hid[h], s.og[...])
    for p in (0, 1):
        for q in range(L // LANES):
            at = base_out + q * Q
            s.g[p, at : at + Q, :] = out_part[p * Q : (p + 1) * Q, q * LANES : (q + 1) * LANES]
    pair_start(1)

    def slope_half(which, k):
        rows = rows_of(k * ROWS, ROWS)
        w_rows = rows_of(which * half, half)
        value = (nt(s.og[rows, :], s.weo[w_rows, :]) * s.pre[which, rows, :]).astype(BF)
        s.sl[which, rows, :] = value
        return value

    def slope_sums(which):
        s.rs[which] = mm(s.rhot_t[...], s.sl[which])

        def slots(j):
            at = rows_of(j * TILE, TILE)
            s.ss[which, at, :] = mm(s.shot_t[at, :], s.sl[which])

        loop(0, slot_tiles, slots)

    def backward_own(k):
        value = slope_half(h, k)
        s.vsum[6:7, 0:half] += row_sum(value.astype(F32))

    loop(0, tiles, backward_own)
    slope_sums(h)

    pair_finish(1)
    a_send(1)

    edge_part = tn(s.ef[...], s.sl[h])
    recv_part = tn(s.nf[...], s.rs[h].astype(BF))
    for p in (0, 1):
        cols = slice(p * Q, (p + 1) * Q)
        s.g[p, base_in : base_in + L, :] = edge_part[:, cols]
        s.g[p, base_in + 2 * L : base_in + 3 * L, :] = recv_part[:, cols]
        for j in range(6):
            for q in range(L // LANES):
                at = base_vec + j * (L // LANES) + q
                s.g[p, at : at + 1, :] = s.vsum[j : j + 1, q * LANES : (q + 1) * LANES]
        s.g[p, base_vec + 24 : base_vec + 25, :] = s.vsum[6:7, cols]
        s.g[p, base_vec + 25 : base_vec + 26, :] = 0.5 * row_sum(s.nsl[2 * h + p].astype(F32))

    def sender_part(k):
        at = rows_of(k * TILE, TILE)
        value = tn(s.slots[at, :], s.ss[h, at, :].astype(BF))
        for p in (0, 1):
            s.g[p, base_in + L : base_in + 2 * L, :] += value[:, p * Q : (p + 1) * Q]

    loop(0, slot_tiles, sender_part)
    pair_start(2)
    b_send(0)
    pair_finish(2)
    a_send(2)

    def backward_other(k):
        rows = rows_of(k * ROWS, ROWS)
        value = slope_half(oh, k)
        cot = s.ecot[rows, :].astype(F32)
        back = nt(s.sl[0, rows, :], s.wei[0, 0:L, :]) + nt(s.sl[1, rows, :], s.wei[1, 0:L, :])
        s.eg[rows, :] = (cot + back).astype(BF)
        out_start(k, s.eg, s.eg_h, 1)

    loop(0, tiles, backward_other)
    slope_sums(oh)
    b_send(1)
    b_finish(0)

    def slot_grad(which, rows):
        at = rows_of(L + which * LH, LH)
        return nt(s.ss[0, rows, :].astype(BF), s.wei[0, at, :]) + nt(s.ss[1, rows, :].astype(BF), s.wei[1, at, :])

    def recv_grad(which):
        at = rows_of(2 * L + which * LH, LH)
        return nt(s.rs[0].astype(BF), s.wei[0, at, :]) + nt(s.rs[1].astype(BF), s.wei[1, at, :])

    def slot_other(k):
        rows = rows_of(k * TILE, TILE)
        s.tosend[rows, :] = slot_grad(oc, rows).astype(BF)

    loop(0, slot_tiles, slot_other)
    s.tosend[S : S + N, :] = recv_grad(oc).astype(BF)
    grad_swap = remote(s.tosend, s.torecv, s.xsend.at[1], s.xrecv.at[1], (r, pair))
    grad_swap.start()
    b_send(2)
    s.ntp[...] = (
        s.ncot[:, col_lane].astype(F32)
        + (nt(s.nsl[0], s.wni[rows_of(c * LH, LH), 0:Q]) + nt(s.nsl[1], s.wni[rows_of(c * LH, LH), Q : 2 * Q]))
        + (
            nt(s.nsl[2], s.wni[rows_of(c * LH, LH), 2 * Q : 3 * Q])
            + nt(s.nsl[3], s.wni[rows_of(c * LH, LH), 3 * Q : 4 * Q])
        )
        + recv_grad(c)
    )
    grad_swap.wait_recv()

    def slot_own(k):
        rows = rows_of(k * TILE, TILE)
        s.served[rows, :] = (slot_grad(c, rows) + s.torecv[rows, :].astype(F32)).astype(BF)

    loop(1, R, lambda k: served_copy(k).wait_send())
    loop(0, slot_tiles, slot_own)

    def back_copy(k):
        to = lax.rem(r + k, R)
        return remote(s.served.at[rows_of(to * CAP, CAP)], s.ret.at[mine], s.ksend.at[k], s.krecv.at[k], (to, t))

    loop(1, R, lambda k: back_copy(k).start())
    b_finish(1)
    spread(0)
    b_finish(2)

    def norm_row(k):
        to = lax.rem(r + k, R)
        ref = s.norm_a.at[mine8]
        return remote(ref, ref, s.qsend.at[k], s.qrecv.at[k], (to, t))

    loop(1, R, lambda k: norm_row(k).start())
    s.ret[mine, :] = s.served[mine, :]
    s.ntp[...] += s.torecv[S : S + N, :].astype(F32)
    for n in (1, 2):
        spread(n)

    def norm_row_wait(k):
        source = lax.rem(r + R - k, R)
        ref = s.norm_a.at[rows_of(source * 8, 8, 8)]
        remote(ref, ref, s.qsend.at[k], s.qrecv.at[k], (source, t)).wait_recv()
        norm_row(k).wait_send()

    loop(1, R, norm_row_wait)
    own_rows = rows_of(t * 8, 8, 8)
    s.nsq[own_rows, :] = jnp.sum(s.norm_a[...].reshape(R, 8, LANES), axis=0)
    for k, peer in enumerate((pair, far, diag)):
        ref = s.nsq.at[own_rows]
        remote(ref, ref, s.tsem.at[0, k], s.tsem.at[1, k], (r, peer)).start()

    def back_wait(k):
        source = lax.rem(r + R - k, R)
        ref = s.ret.at[rows_of(source * CAP, CAP)]
        remote(ref, ref, s.ksend.at[k], s.krecv.at[k], (source, t)).wait_recv()
        back_copy(k).wait_send()

    loop(1, R, back_wait)

    def gathered(k):
        lanes = pl.ds(pl.multiple_of(k * TILE, TILE), TILE)
        s.ntp[...] += mm(s.serve_t[:, lanes], s.ret[rows_of(k * TILE, TILE), :])

    loop(0, slot_tiles, gathered)
    s.ng[...] = s.ntp[...].astype(BF)
    ng_keep = local(s.ng, s.ng_h.at[:, col_lane], s.nsem.at[1])
    ng_keep.start()
    ng_send = remote(s.ng, s.ng_h.at[:, col_lane], s.xsend.at[3], s.xrecv.at[3], (r, pair))
    ng_send.start()

    for n in (0, 1, 2):
        spread_wait(n)
    for k, peer in enumerate((pair, far, diag)):
        ref = s.nsq.at[rows_of(peer * 8, 8, 8)]
        remote(ref, ref, s.tsem.at[0, k], s.tsem.at[1, k], (r, peer)).wait()
    total = s.nsq[0:8, :] + s.nsq[8:16, :] + s.nsq[16:24, :] + s.nsq[24:32, :]
    s.norm_o[...] = jnp.sqrt(jnp.full((8, LANES), jnp.sum(total), F32))
    for n in (0, 1, 2):
        sums_done(n)
    for i in range(8):
        weight_copy(i, 0, t).wait_send()
        weight_copy(i, 1, t).wait_send()
        weight_copy(i, 2, far).wait_send()
        if i in shared:
            for j in (1, 2, 3):
                part_copy(i, j, a).wait_send()
    slot_swap.wait_send()
    grad_swap.wait_send()

    def finish(k):
        out_wait(k, s.ne, s.ne_h, 0)
        out_wait(k, s.eg, s.eg_h, 1)

    loop(0, tiles, finish)
    nn_copy.wait()
    ng_keep.wait()
    ng_send.wait_send()
    ref = s.ng_h.at[:, other_lane]
    remote(ref, ref, s.xsend.at[3], s.xrecv.at[3], (r, pair)).wait_recv()


def adam(weight, first, second, gradient, factor, rate):
    clipped = gradient * factor
    first_new = beta_one * first + (1.0 - beta_one) * clipped
    second_new = beta_two * second + (1.0 - beta_two) * clipped * clipped
    bias_one = 1.0 - beta_one**adam_step
    bias_two = 1.0 - beta_two**adam_step
    moved = first_new / bias_one / (jnp.sqrt(second_new / bias_two) + adam_eps) + decay_rate * weight
    return weight - rate * moved, first_new, second_new


def update(names, d, *refs):
    s = types.SimpleNamespace(**dict(zip(names, refs, strict=True)))
    L, Q = d.L, d.Q
    passes = [
        pltpu.make_async_copy(s.__dict__[f"pass{k}"], s.__dict__[f"out{k}"], s.psem.at[k]) for k in range(4)
    ]
    for copy in passes:
        copy.start()
    norm = s.norm[0:1, 0:1]
    s.norm_o[0] = s.norm[0, 0]
    factor = clip_level / jnp.maximum(norm, clip_level)
    copies = []

    def one(k, grad, at, rate):
        values = adam(
            s.__dict__[f"in{k}"][at], s.__dict__[f"in{6 + k}"][at], s.__dict__[f"in{12 + k}"][at], grad, factor, rate
        )
        for n, value in enumerate(values):
            s.__dict__[f"buf{6 * n + k}"][at] = value

    def send(k):
        for n in range(3):
            m = 6 * n + k
            copy = pltpu.make_async_copy(s.__dict__[f"buf{m}"], s.__dict__[f"new{m}"], s.osem.at[m])
            copy.start()
            copies.append(copy)

    everything = (slice(None), slice(None))
    for k, base in ((2, d.base_node), (0, d.base_in)):
        for low in range(0, (2 if k == 2 else 3) * L, 256):
            rows = slice(low, low + 256)
            one(k, s.fin[base + low : base + low + 256, :].astype(F32), (rows, slice(None)), learn_rate)
        send(k)
    for k, base in ((3, d.base_node + 2 * L), (1, d.base_out)):
        for q in range(L // LANES):
            at = (slice(None), slice(q * LANES, (q + 1) * LANES))
            one(k, s.fin[base + q * LANES : base + (q + 1) * LANES, :].astype(F32), at, learn_rate)
        send(k)
    vec = s.fin[d.base_in + 3 * L : d.base_in + 3 * L + 32, :].astype(F32)
    one(4, vec[24:26, :], everything, vector_rate)
    send(4)
    for j in range(6):
        for q in range(L // LANES):
            m = j * (L // LANES) + q
            at = (slice(j, j + 1), slice(q * LANES, (q + 1) * LANES))
            one(5, vec[m : m + 1, :], at, vector_rate)
    send(5)
    for copy in copies + passes:
        copy.wait()


def device_step(
    node_feats,
    edge_feats,
    edge_receiver,
    edge_slot,
    edge_mask,
    serve_rows,
    node_cot,
    edge_cot,
    *states,
):
    weights = states[:6]
    d = types.SimpleNamespace()
    d.R = lax.axis_size("rows")
    d.N, d.L = node_feats.shape
    d.E = edge_feats.shape[0]
    d.Q = weights[0].shape[1]
    d.H = d.Q * lax.axis_size("tp")
    d.CAP = serve_rows.shape[1]
    R, N, E, L, H, Q = d.R, d.N, d.E, d.L, d.H, d.Q
    EH, S, nb = E // 2, R * d.CAP, R // 4
    tiles = EH // ROWS

    def padded(count):
        return -(-count // (16 * R)) * (16 * R)

    d.size_node, d.size_out, d.size_in = padded(3 * L), padded(L), padded(3 * L + 32)
    d.base_node, d.base_out, d.base_in = 0, d.size_node, d.size_node + d.size_out
    G = d.size_node + d.size_out + d.size_in
    vmem_spec = pl.BlockSpec(memory_space=pltpu.VMEM)
    inputs = dict(
        nf_h=node_feats,
        ef_h=edge_feats,
        ncot_h=node_cot,
        ecot_h=edge_cot,
        wei_h=weights[0],
        weo_h=weights[1],
        wni_h=weights[2],
        wno_h=weights[3],
        hb_h=weights[4],
        fv_h=weights[5],
        rec2_h=edge_receiver.reshape(-1, LANES),
        slot2_h=edge_slot.reshape(-1, LANES),
        mask2_h=edge_mask.reshape(-1, LANES),
        rec1_h=edge_receiver.reshape(1, -1),
        slot1_h=edge_slot.reshape(1, -1),
        serve_h=serve_rows,
    )
    hbm_spec = pl.BlockSpec(memory_space=pltpu.HBM)
    outputs = dict(
        nn_h=(jax.ShapeDtypeStruct((N, L), BF), hbm_spec),
        ne_h=(jax.ShapeDtypeStruct((E, L), BF), hbm_spec),
        ng_h=(jax.ShapeDtypeStruct((N, L), BF), hbm_spec),
        eg_h=(jax.ShapeDtypeStruct((E, L), BF), hbm_spec),
        fin_o=(jax.ShapeDtypeStruct((G, Q), BF), vmem_spec),
        norm_o=(jax.ShapeDtypeStruct((8, LANES), F32), vmem_spec),
    )
    dma = pltpu.SemaphoreType.DMA
    scratch = dict(
        hb=pltpu.VMEM((2, Q), F32),
        fv=pltpu.VMEM((6, L), F32),
        rec2=pltpu.VMEM((E // LANES, LANES), jnp.int32),
        slot2=pltpu.VMEM((E // LANES, LANES), jnp.int32),
        mask2=pltpu.VMEM((E // LANES, LANES), jnp.int32),
        rec1=pltpu.VMEM((1, E), jnp.int32),
        slot1=pltpu.VMEM((1, E), jnp.int32),
        serve=pltpu.VMEM((R, d.CAP), jnp.int32),
        wei32=pltpu.VMEM((3 * L, Q), F32),
        weo32=pltpu.VMEM((Q, L), F32),
        wni32=pltpu.VMEM((2 * L, Q), F32),
        wno32=pltpu.VMEM((Q, L), F32),
        nf=pltpu.VMEM((N, L), BF),
        ef=pltpu.VMEM((EH, L), BF),
        ncot=pltpu.VMEM((N, L), BF),
        ecot=pltpu.VMEM((EH, L), BF),
        wei=pltpu.VMEM((2, 3 * L, H // 2), BF),
        weo=pltpu.VMEM((H, L), BF),
        wni=pltpu.VMEM((2 * L, H), BF),
        wno=pltpu.VMEM((H, L), BF),
        bias=pltpu.VMEM((8, H), F32),
        serve_col=pltpu.VMEM((S, 1), F32),
        serve_t=pltpu.VMEM((N, S), BF),
        served=pltpu.VMEM((S, L // 2), BF),
        slots=pltpu.VMEM((S, L), BF),
        ret=pltpu.VMEM((S, L // 2), BF),
        rcol=pltpu.VMEM((EH, 1), F32),
        scol=pltpu.VMEM((EH, 1), F32),
        mcol=pltpu.VMEM((EH, 1), F32),
        rhot=pltpu.VMEM((EH, N), BF),
        rhot_t=pltpu.VMEM((N, EH), BF),
        shot_t=pltpu.VMEM((S, EH), BF),
        xr=pltpu.VMEM((EH, L), BF),
        xs=pltpu.VMEM((EH, L), BF),
        part=pltpu.VMEM((EH, L), F32),
        mk=pltpu.VMEM((EH, L), BF),
        pre=pltpu.VMEM((2, EH, H // 2), F32),
        hid=pltpu.VMEM((2, EH, H // 2), BF),
        normed=pltpu.VMEM((EH, L), F32),
        inv=pltpu.VMEM((EH, 1), F32),
        ne=pltpu.VMEM((EH, L), BF),
        eg=pltpu.VMEM((EH, L), BF),
        aggp=pltpu.VMEM((N, L), F32),
        aggr=pltpu.VMEM((N, L), F32),
        nn=pltpu.VMEM((N, L), BF),
        ng=pltpu.VMEM((N, L // 2), BF),
        agh=pltpu.VMEM((N, L), BF),
        ntp=pltpu.VMEM((N, L // 2), F32),
        nsl=pltpu.VMEM((H // Q, N, Q), BF),
        nhid=pltpu.VMEM((H // Q, N, Q), BF),
        og=pltpu.VMEM((EH, L), BF),
        sl=pltpu.VMEM((2, EH, H // 2), BF),
        rs=pltpu.VMEM((2, N, H // 2), F32),
        ss=pltpu.VMEM((2, S, H // 2), F32),
        tosend=pltpu.VMEM((S + N, L // 2), BF),
        torecv=pltpu.VMEM((S + N, L // 2), BF),
        g=pltpu.VMEM((2, G, Q), F32),
        sb=pltpu.VMEM((G, Q), BF),
        rbp=pltpu.VMEM((G, Q), BF),
        rba=pltpu.VMEM((3, G, Q), BF),
        rbb=pltpu.VMEM((nb - 1, G // R, Q), BF),
        vsum=pltpu.VMEM((8, L), F32),
        norm_a=pltpu.VMEM((8 * R, LANES), F32),
        nsq=pltpu.VMEM((32, LANES), F32),
        lsem=dma((16,)),
        wsend=dma((8, 6)),
        wrecv=dma((8, 6)),
        ssend=dma((R,)),
        srecv=dma((R,)),
        ksend=dma((R,)),
        krecv=dma((R,)),
        qsend=dma((R,)),
        qrecv=dma((R,)),
        osem=dma((2, tiles)),
        osend=dma((2, tiles)),
        orecv=dma((2, tiles)),
        xsend=dma((4,)),
        xrecv=dma((4,)),
        nsem=dma((2,)),
        psend=dma((3,)),
        precv=dma((3,)),
        asend=dma((3, nb, 4)),
        arecv=dma((3, nb, 4)),
        bsend=dma((3, nb)),
        brecv=dma((3, nb)),
        fbsend=dma((3, nb)),
        fbrecv=dma((3, nb)),
        fasend=dma((3, nb, 4)),
        farecv=dma((3, nb, 4)),
        tsem=dma((2, 3)),
    )
    names = (*inputs, *outputs, *scratch)
    limit = 6 * 1024 * 1024
    for x in scratch.values():
        if x.memory_space == pltpu.VMEM:
            *lead, rows, lanes = x.shape
            limit += math.prod(lead) * rows * -(-lanes // LANES) * LANES * jnp.dtype(x.dtype).itemsize
    new_nodes, new_edges, node_gradient, edge_gradient, fin, norm = pl.pallas_call(
        functools.partial(layer, names, d),
        out_shape=[shape for shape, _ in outputs.values()],
        in_specs=[hbm_spec] * len(inputs),
        out_specs=[spec for _, spec in outputs.values()],
        scratch_shapes=list(scratch.values()),
        compiler_params=pltpu.CompilerParams(
            collective_id=0, has_side_effects=True, vmem_limit_bytes=limit
        ),
    )(*(pltpu.with_memory_space_constraint(x, pltpu.HBM) for x in inputs.values()))

    passes = (new_nodes, new_edges, node_gradient, edge_gradient)
    names = (
        "fin",
        "norm",
        *(f"pass{k}" for k in range(4)),
        *(f"in{k}" for k in range(18)),
        *(f"out{k}" for k in range(4)),
        "norm_o",
        *(f"new{k}" for k in range(18)),
        *(f"buf{k}" for k in range(18)),
        "psem",
        "osem",
    )
    outs = pl.pallas_call(
        functools.partial(update, names, d),
        out_shape=[
            *(jax.ShapeDtypeStruct(x.shape, x.dtype) for x in passes),
            jax.ShapeDtypeStruct((1,), F32),
            *(jax.ShapeDtypeStruct(x.shape, F32) for x in states),
        ],
        in_specs=[vmem_spec, vmem_spec, *[hbm_spec] * 4, *[vmem_spec] * 18],
        out_specs=[*[hbm_spec] * 4, pl.BlockSpec(memory_space=pltpu.SMEM), *[hbm_spec] * 18],
        scratch_shapes=[*(pltpu.VMEM(x.shape, F32) for x in states), dma((4,)), dma((18,))],
        compiler_params=pltpu.CompilerParams(vmem_limit_bytes=12 * 1024 * 1024),
    )(fin, norm, *passes, *states)
    return tuple(outs)


def solution(mesh):
    split = [P(None, "tp"), P("tp", None), P(None, "tp"), P("tp", None), P(None, "tp"), P()]
    row = P("rows", None)
    return jax.shard_map(
        device_step,
        mesh=mesh,
        in_specs=(row, row, P("rows"), P("rows"), P("rows"), row, row, row, *split, *split, *split),
        out_specs=(row, row, row, row, P(), *split, *split, *split),
        check_vma=False,
    )
```

```python
import functools
import math
import types

import jax
import jax.numpy as jnp
from jax import lax
from jax.experimental import pallas as pl
from jax.experimental.pallas import tpu as pltpu
from jax.sharding import PartitionSpec as P

BF = jnp.bfloat16
F32 = jnp.float32
MESH = pl.DeviceIdType.MESH
LANES = 128
TILE = 256
ROWS = 512
DOWN = (4, 4, 4)
UP = (4, 4, 4)

beta_one = 0.9
beta_two = 0.999
adam_step = 7.0
adam_eps = 1e-08
learn_rate = 0.05
vector_rate = 0.3
decay_rate = 0.1
clip_level = 1.0


def mm(left, right):
    return jnp.dot(left, right, preferred_element_type=F32)


def nt(left, right):
    return lax.dot_general(left, right, (((1,), (1,)), ((), ())), preferred_element_type=F32)


def tn(left, right):
    return lax.dot_general(left, right, (((0,), (0,)), ((), ())), preferred_element_type=F32)


def two(values):
    high = values.astype(BF)
    return high, (values - high.astype(F32)).astype(BF)


def aligned(start, step):
    return start if isinstance(start, int) else pl.multiple_of(start, step)


def rows_of(start, size, step=16):
    return pl.ds(aligned(start, step), size)


def hot(cond):
    return jnp.where(cond, 1.0, 0.0).astype(BF)


def normalize(values):
    center = values - jnp.mean(values, axis=1, keepdims=True)
    inverse = lax.rsqrt(jnp.mean(center * center, axis=1, keepdims=True) + 1e-05)
    return center * inverse, inverse


def norm_back(scaled, normed, inverse):
    first = jnp.mean(scaled, axis=1, keepdims=True)
    second = jnp.mean(scaled * normed, axis=1, keepdims=True)
    return inverse * (scaled - first - normed * second)


def row_sum(values):
    return jnp.sum(values, axis=0, keepdims=True)


def layer(names, d, *refs):
    s = types.SimpleNamespace(**dict(zip(names, refs, strict=True)))
    R, N, E, L, H, Q, CAP = d.R, d.N, d.E, d.L, d.H, d.Q, d.CAP
    EH, S, half, LH = E // 2, R * CAP, H // 2, L // 2
    tiles, slot_tiles, nb = EH // ROWS, S // TILE, R // 4
    r = lax.axis_index("rows")
    t = lax.axis_index("tp")
    h, c = t // 2, lax.rem(t, 2)
    oh, oc = 1 - h, 1 - c
    pair = t + 1 - 2 * c
    far = t + 2 - 4 * h
    diag = pair + 2 - 4 * h
    a, b = lax.rem(r, 4), r // 4
    edge0 = c * EH
    near_row = lax.rem(r + 1, R)
    own_lane = pl.ds(pl.multiple_of(t * Q, Q), Q)
    core_lane = pl.ds(pl.multiple_of(c * Q, Q), Q)
    far_lane = pl.ds(pl.multiple_of(far * Q, Q), Q)
    col_lane = pl.ds(pl.multiple_of(c * LH, LH), LH)

    def local(src, dst, sem):
        return pltpu.make_async_copy(src, dst, sem)

    def remote(src, dst, send, recv, device):
        return pltpu.make_async_remote_copy(
            src_ref=src, dst_ref=dst, send_sem=send, recv_sem=recv, device_id=device, device_id_type=MESH
        )

    def loop(low, high, body):
        def step(k, carry):
            body(k)
            return carry

        if high - low <= 8:
            for k in range(low, high):
                body(k)
        else:
            lax.fori_loop(low, high, step, 0)

    loads = [
        local(s.wei_h, s.wei32, s.lsem.at[0]),
        local(s.nf_h, s.nf, s.lsem.at[1]),
        local(s.ef_h.at[rows_of(edge0, EH)], s.ef, s.lsem.at[2]),
        local(s.weo_h, s.weo32, s.lsem.at[3]),
        local(s.wni_h, s.wni32, s.lsem.at[4]),
        local(s.wno_h, s.wno32, s.lsem.at[5]),
        local(s.ncot_h, s.ncot, s.lsem.at[6]),
        local(s.ecot_h.at[rows_of(edge0, EH)], s.ecot, s.lsem.at[7]),
        local(s.serve_h, s.serve, s.lsem.at[8]),
        local(s.hb_h, s.hb, s.lsem.at[9]),
        local(s.fv_h, s.fv, s.lsem.at[10]),
        local(s.rec2_h, s.rec2, s.lsem.at[11]),
        local(s.slot2_h, s.slot2, s.lsem.at[12]),
        local(s.mask2_h, s.mask2, s.lsem.at[13]),
        local(s.rec1_h, s.rec1, s.lsem.at[14]),
        local(s.slot1_h, s.slot1, s.lsem.at[15]),
    ]
    for k in (0, 1, 8, 9, 3, 11, 12, 13, 14, 15, 2, 4, 5, 10, 6, 7):
        loads[k].start()

    barrier = pltpu.get_barrier_semaphore()
    for peer in (pair, far, diag):
        pl.semaphore_signal(barrier, inc=1, device_id=(r, peer), device_id_type=MESH)

    def greet(k):
        pl.semaphore_signal(barrier, inc=1, device_id=(lax.rem(r + k, R), t), device_id_type=MESH)

    loop(1, R, greet)

    shared = (1, 2, 4, 5)

    def block(i, tt, part=None):
        lane = pl.ds(pl.multiple_of(tt * Q, Q), Q)
        if i < 3:
            half_lane = pl.ds(pl.multiple_of(lax.rem(tt, 2) * Q, Q), Q)
            rows = pl.ds((0, 2 * L, L)[i], L) if part is None else rows_of((0, 2 * L, L)[i] + part * (L // 4), L // 4)
            return s.wei.at[tt // 2, rows, half_lane]
        if i == 3:
            return s.weo.at[lane, :]
        if i < 6:
            low = (L, 0)[i - 4]
            return s.wni.at[pl.ds(low, L) if part is None else rows_of(low + part * (L // 4), L // 4), lane]
        if i == 6:
            return s.wno.at[lane, :]
        return s.bias.at[:, lane]

    groups = (0, 0, 0, 1, 2, 2, 3, 4)

    def weight_copy(i, way, who):
        ref = block(i, who, a if way == 1 and i in shared else None)
        sent = 10 + i if way == 1 else groups[i] + 5 * (way // 2)
        return remote(ref, ref, s.wsend.at[sent], s.wrecv.at[8 * way + i], (r, (pair, far, pair)[way]))

    def part_copy(i, j, ref):
        at = shared.index(i)
        device = (b * 4 + lax.rem(a + j, 4), t)
        return remote(ref, ref, s.wsend.at[18 + at], s.wrecv.at[24 + at], device)

    def three_parts(i):
        low, size = (0, 2 * L, L, 0, L, 0)[i], 3 * (L // 4)
        if i < 3:
            return s.wei.at[oh, pl.ds(low, size), core_lane]
        return s.wni.at[pl.ds(low, size), far_lane]

    def weights_sent():
        for way, tt, th, lane in ((0, t, h, own_lane), (2, far, oh, far_lane)):
            for k, ref in enumerate(
                (s.wei.at[th, :, core_lane], block(3, tt), s.wni.at[:, lane], block(6, tt), block(7, tt))
            ):
                remote(ref, ref, s.wsend.at[k + 5 * (way // 2)], s.wrecv.at[0], (r, pair)).wait_send()
        for i in range(8):
            weight_copy(i, 1, t).wait_send()
        for i in shared:
            part_copy(i, 1, three_parts(i)).wait_send()

    def weight_send(i, way):
        weight_copy(i, way, t).start()

    def weight_wait(i, way):
        weight_copy(i, way, (pair, far, diag)[way]).wait_recv()

    def part_spread(i):
        weight_wait(i, 1)
        for j in (1, 2, 3):
            part_copy(i, j, block(i, far, a)).start()

    def weight_forward(i):
        if i in shared:
            part_copy(i, 1, three_parts(i)).wait_recv()
        else:
            weight_wait(i, 1)
        weight_copy(i, 2, far).start()

    loads[0].wait()
    for i in range(3):
        at = pl.ds((0, 2 * L, L)[i], L)
        s.wei[h, at, core_lane] = s.wei32[at, :].astype(BF)
    loads[9].wait()
    s.bias[0:2, own_lane] = s.hb[...]
    s.bias[2:8, own_lane] = jnp.zeros((6, Q), F32)
    loads[1].wait()

    loads[8].wait()
    turned = jnp.transpose(s.serve[...].astype(F32))
    for k in range(R):
        s.serve_col[k * CAP : (k + 1) * CAP, :] = turned[:, k : k + 1]

    def serve(k):
        at = rows_of(k * TILE, TILE)
        table = s.serve_col[at, :].astype(jnp.int32) == lax.broadcasted_iota(jnp.int32, (TILE, N), 1)
        table = jnp.where(table, 1.0, 0.0)
        s.serve_t[:, pl.ds(pl.multiple_of(k * TILE, TILE), TILE)] = jnp.transpose(table).astype(BF)
        s.served[at, :] = mm(table.astype(BF), s.nf[:, col_lane]).astype(BF)

    loop(0, slot_tiles, serve)
    pl.semaphore_wait(barrier, R + 2)

    for i in (1, 2, 7, 0):
        weight_send(i, 1)
    mine = rows_of(r * CAP, CAP)

    def served_copy(k):
        to = lax.rem(r + k, R)
        return remote(
            s.served.at[rows_of(to * CAP, CAP)],
            s.slots.at[mine, col_lane],
            s.ssend.at[0],
            s.srecv.at[0],
            (to, t),
        )

    loop(1, R, lambda k: served_copy(k).start())
    s.slots[mine, col_lane] = s.served[mine, :]
    for i in (0, 1, 2, 7):
        weight_send(i, 0)
    loads[4].wait()
    for i in (4, 5):
        at = pl.ds((L, 0)[i - 4], L)
        s.wni[at, own_lane] = s.wni32[at, :].astype(BF)
        weight_send(i, 1)
    loads[3].wait()
    s.weo[own_lane, :] = s.weo32[...].astype(BF)
    loads[5].wait()
    s.wno[own_lane, :] = s.wno32[...].astype(BF)
    for i in (3, 6):
        weight_send(i, 1)
    for i in (3, 4, 5, 6):
        weight_send(i, 0)

    for k in (11, 12, 13, 14, 15):
        loads[k].wait()
    per = EH // LANES
    at = rows_of(c * per, per, 8)
    for source, target in ((s.rec2, s.rcol), (s.slot2, s.scol), (s.mask2, s.mcol)):
        turned = jnp.transpose(source[at, :].astype(F32))
        for k in range(per):
            target[k * LANES : (k + 1) * LANES, :] = turned[:, k : k + 1]
    lanes_here = pl.ds(pl.multiple_of(edge0, EH), EH)
    s.rhot_t[...] = hot(s.rec1[:, lanes_here] == lax.broadcasted_iota(jnp.int32, (N, EH), 0))
    part_spread(1)
    part_spread(2)

    def slot_table(k):
        rows = rows_of(k * TILE, TILE)
        s.shot_t[rows, :] = hot(
            s.slot1[:, lanes_here] == lax.broadcasted_iota(jnp.int32, (TILE, EH), 0) + k * TILE
        )

    loop(0, slot_tiles, slot_table)

    def receivers(k):
        rows = rows_of(k * ROWS, ROWS)
        index = s.rcol[rows, :].astype(jnp.int32)
        table = hot(index == lax.broadcasted_iota(jnp.int32, (ROWS, N), 1))
        s.rhot[rows, :] = table
        s.xr[rows, :] = mm(table, s.nf[...]).astype(BF)

    loop(0, tiles, receivers)
    loads[2].wait()

    def first_two(which):
        def body(k):
            rows = rows_of(k * ROWS, ROWS)
            value = mm(s.ef[rows, :], s.wei[which, 0:L, :])
            s.pre[which, rows, :] = value + mm(s.xr[rows, :], s.wei[which, 2 * L : 3 * L, :])

        loop(0, tiles, body)

    def hidden_of(which, k):
        rows = rows_of(k * ROWS, ROWS)
        lanes = pl.ds(pl.multiple_of(which * half, half), half)
        pre = s.pre[which, rows, :] + mm(s.xs[rows, :], s.wei[which, L : 2 * L, :]) + s.bias[0:1, lanes]
        sig = 0.5 + 0.5 * jnp.tanh(0.5 * pre)
        value = (pre * sig).astype(BF)
        s.hid[which, rows, :] = value
        s.pre[which, rows, :] = sig + (pre * sig) * (1.0 - sig)

    def outer_of(which, k):
        return mm(s.hid[which, rows_of(k * ROWS, ROWS), :], s.weo[rows_of(which * half, half), :])

    for i in (0, 1):
        weight_wait(i, 0)
    first_two(h)
    s.g[...] = jnp.zeros_like(s.g)
    weight_forward(0)

    others = pl.ds(0, (R - 1) * CAP)
    ref = s.slots.at[others, col_lane]
    remote(ref, ref, s.ssend.at[0], s.srecv.at[0], (near_row, t)).wait_recv()
    slot_swap = remote(s.slots.at[:, col_lane], s.slots.at[:, col_lane], s.xsend.at[2], s.xrecv.at[2], (r, pair))
    slot_swap.start()
    weight_forward(1)
    other_lane = pl.ds(pl.multiple_of(oc * LH, LH), LH)
    ref = s.slots.at[:, other_lane]
    remote(ref, ref, s.xsend.at[2], s.xrecv.at[2], (r, pair)).wait_recv()

    def senders(k):
        rows = rows_of(k * ROWS, ROWS)
        index = s.scol[rows, :].astype(jnp.int32)
        table = hot(index == lax.broadcasted_iota(jnp.int32, (ROWS, S), 1))
        s.xs[rows, :] = mm(table, s.slots[...]).astype(BF)

    loop(0, tiles, senders)
    weight_forward(2)
    part_spread(4)
    part_spread(5)
    for i in (2, 7, 3):
        weight_wait(i, 0)

    def own_half(k):
        hidden_of(h, k)
        s.part[rows_of(k * ROWS, ROWS), :] = outer_of(h, k)

    loop(0, tiles, own_half)
    weight_forward(7)
    for i in (0, 1):
        weight_wait(i, 2)
    first_two(oh)
    for i in (2, 7):
        weight_wait(i, 2)
    weight_forward(3)
    loop(0, tiles, lambda k: hidden_of(oh, k))
    weight_wait(3, 2)
    loads[10].wait()

    def out_copies(rows, source, target, which):
        here = source.at[rows]
        there = target.at[rows_of(edge0 + rows.start, rows.size)]
        keep = local(here, there, s.osem.at[which])
        send = remote(here, there, s.osend.at[which], s.orecv.at[which], (r, pair))
        return keep, send

    def out_start(k, source, target, which):
        keep, send = out_copies(pl.ds(k * ROWS, ROWS), source, target, which)
        keep.start()
        send.start()

    def out_wait(source, target, which):
        keep, send = out_copies(pl.ds(0, EH), source, target, which)
        keep.wait()
        send.wait_send()
        ref = target.at[rows_of(oc * EH, EH)]
        remote(ref, ref, s.osend.at[which], s.orecv.at[which], (r, pair)).wait_recv()

    def forward(k):
        rows = rows_of(k * ROWS, ROWS)
        outer = s.part[rows, :] + outer_of(oh, k) + s.fv[0:1, :]
        normed, inverse = normalize(outer)
        s.normed[rows, :] = normed
        s.inv[rows, :] = inverse
        masked = s.mcol[rows, :] * (normed * s.fv[1:2, :] + s.fv[2:3, :])
        s.ne[rows, :] = (s.ef[rows, :].astype(F32) + masked).astype(BF)
        out_start(k, s.ne, s.ne_h, 0)
        s.mk[rows, :] = masked.astype(BF)

    loop(0, tiles, forward)
    swaps = []
    for k in (0, 1):
        at = pl.ds(k * (N // 2), N // 2)
        s.aggp[at, :] = mm(s.rhot_t[at, :], s.mk[...])
        swap = remote(s.aggp.at[at], s.aggr.at[at], s.xsend.at[4 * k], s.xrecv.at[4 * k], (r, pair))
        swap.start()
        swaps.append(swap)
    for i in (4, 5, 6):
        weight_forward(i)
    weight_wait(5, 0)
    weight_wait(5, 2)
    own_term = mm(s.nf[...], s.wni[0:L, :])
    weight_wait(4, 0)
    weight_wait(4, 2)
    for swap in swaps:
        swap.wait()

    agg = (s.aggp[...] + s.aggr[...]).astype(BF)
    pre = own_term + mm(agg, s.wni[L : 2 * L, :]) + s.bias[1:2, :]
    sig = 0.5 + 0.5 * jnp.tanh(0.5 * pre)
    node_hidden = (pre * sig).astype(BF)
    slope_of = sig + (pre * sig) * (1.0 - sig)
    weight_wait(6, 0)
    weight_wait(6, 2)
    outer = mm(node_hidden, s.wno[...]) + s.fv[3:4, :]
    normed, inverse = normalize(outer)
    s.nn[...] = (s.nf[...].astype(F32) + (normed * s.fv[4:5, :] + s.fv[5:6, :])).astype(BF)
    nn_copy = local(s.nn, s.nn_h, s.nsem.at[0])
    nn_copy.start()
    loads[6].wait()
    up = s.ncot[...].astype(F32)
    node_outer_grad = norm_back(up * s.fv[4:5, :], normed, inverse).astype(BF)
    node_slope = (nt(node_outer_grad, s.wno[...]) * slope_of).astype(BF)
    s.agh[...] = nt(node_slope, s.wni[L : 2 * L, :]).astype(BF)

    for q in range(H // Q):
        s.nsl[q] = node_slope[:, q * Q : (q + 1) * Q]
        s.nhid[q] = node_hidden[:, q * Q : (q + 1) * Q]
    s.vsum[...] = jnp.zeros_like(s.vsum)
    s.vsum[3:4, :] = 0.5 * row_sum(node_outer_grad.astype(F32))
    s.vsum[4:5, :] = 0.5 * row_sum(up * normed)
    s.vsum[5:6, :] = 0.5 * row_sum(up)
    base_node, base_out, base_in, base_vec = d.base_node, d.base_out, d.base_in, d.base_in + 3 * L
    s.g[c, 0:L, :] = tn(s.nf[...], s.nsl[t])
    s.g[c, L : 2 * L, :] = tn(agg, s.nsl[t])
    node_out_grad = tn(s.nhid[t], node_outer_grad)
    for q in range(L // LANES):
        s.g[c, 2 * L + q * Q : 2 * L + (q + 1) * Q, :] = node_out_grad[:, q * LANES : (q + 1) * LANES]

    chunks = ((base_node, d.size_node), (base_out, d.size_out), (base_in, d.size_in))

    down, up_ways = d.down, d.up

    def piece(n, row):
        base, size = chunks[n]
        m = down[n]
        return rows_of(base + (lax.rem(row, m) * (R // m) + row // m) * (size // R), size // R)

    v = r

    def placed(row):
        return row

    def near(m, j):
        return (v // m) * m + lax.rem(v + j, m)

    def across(m, j):
        return lax.rem(v // m + j, R // m) * m + lax.rem(v, m)

    def crossed(m, row, j):
        return lax.rem(row // m + j, R // m) * m + lax.rem(row, m)

    def pair_copy(n):
        at = pl.ds(*chunks[n])
        return remote(s.sb.at[at], s.rbp.at[at], s.psend.at[n], s.precv.at[n], (r, pair))

    def pair_start(n):
        at = pl.ds(*chunks[n])
        s.sb[at, :] = s.g[oc, at, :].astype(BF)
        pair_copy(n).start()

    def pair_finish(n):
        pair_copy(n).wait()
        at = pl.ds(*chunks[n])
        if n == 2:
            vec = pl.ds(base_vec, 32)
            s.g[c, vec, :] = s.g[c, vec, :].astype(BF).astype(F32)
        s.g[c, at, :] += s.rbp[at, :].astype(F32)

    def a_copy(n, jj, j, target):
        at = piece(n, crossed(down[n], target, jj))
        return remote(
            s.sb.at[at], s.rba.at[j - 1, at], s.asend.at[n], s.arecv.at[n, jj], (placed(near(down[n], j)), t)
        )

    def b_slot(n):
        base, size = chunks[n]
        return pl.ds(base // R, size // R)

    def b_copy(n, jj, row):
        return remote(
            s.sb.at[piece(n, row)],
            s.rbb.at[jj - 1, b_slot(n)],
            s.bsend.at[n, jj - 1],
            s.brecv.at[n, jj - 1],
            (placed(across(down[n], jj)), t),
        )

    def a_send(n):
        at = pl.ds(*chunks[n])
        s.sb[at, :] = s.g[c, at, :].astype(BF)
        for jj in (*range(1, R // down[n]), 0):
            for j in range(1, down[n]):
                a_copy(n, jj, j, near(down[n], j)).start()

    def a_sum(n, jj):
        at = piece(n, across(down[n], jj))
        total = s.g[c, at, :]
        ref = s.rba.at[pl.ds(0, down[n] - 1), at]
        remote(ref, ref, s.asend.at[n], s.arecv.at[n, jj], (near_row, t)).wait_recv()
        for j in range(1, down[n]):
            total = total + s.rba[j - 1, at, :].astype(F32)
        return total

    def b_send(n):
        for jj in range(1, R // down[n]):
            row = across(down[n], jj)
            s.sb[piece(n, row), :] = a_sum(n, jj).astype(BF)
            b_copy(n, jj, row).start()

    def to_b(n, jj, row):
        ref = s.fin_o.at[piece(n, row)]
        return remote(ref, ref, s.fbsend.at[n, jj - 1], s.fbrecv.at[n, jj - 1], (placed(across(up_ways[n], jj)), t))

    def to_a(n, jj, j, row):
        ref = s.fin_o.at[piece(n, row)]
        return remote(ref, ref, s.fasend.at[n], s.farecv.at[n], (placed(near(up_ways[n], j)), t))

    def b_finish(n):
        total = a_sum(n, 0)
        at = piece(n, v)
        for jj in range(1, R // down[n]):
            b_copy(n, jj, v).wait_recv()
            total = total + s.rbb[jj - 1, b_slot(n), :].astype(F32)
        final = total.astype(BF)
        s.fin_o[at, :] = final
        for jj in range(1, R // up_ways[n]):
            to_b(n, jj, v).start()
        for j in range(1, up_ways[n]):
            to_a(n, 0, j, v).start()
        final = final.astype(F32)
        squares = final * final
        count = squares.shape[0]
        if n == 2:
            m = down[n]
            low = base_in + (lax.rem(v, m) * (R // m) + v // m) * count
            index = lax.broadcasted_iota(jnp.int32, (count, LANES), 0) + low
            copied = jnp.logical_and(index >= base_vec, index < base_vec + 24)
            squares = jnp.where(copied, 0.25 * squares, squares)
        s.norm_a[mine8, :] += jnp.sum(squares.reshape(count // 8, 8, LANES), axis=0)

    def spread(n):
        m = up_ways[n]
        for jj in range(1, R // m):
            row = crossed(m, v, R // m - jj)
            to_b(n, jj, row).wait_recv()
            for j in range(1, m):
                to_a(n, jj, j, row).start()

    def all_but_own(n, m):
        base, size = chunks[n]
        return pl.ds(base, (R - R // m) * (size // R))

    def spread_wait(n):
        ref = s.fin_o.at[all_but_own(n, up_ways[n])]
        remote(ref, ref, s.fasend.at[n], s.farecv.at[n], (near_row, t)).wait()

    def sums_done(n):
        m = down[n]
        ref = s.sb.at[all_but_own(n, m)]
        remote(ref, ref, s.asend.at[n], s.arecv.at[n, 0], (near_row, t)).wait_send()
        for jj in range(1, R // m):
            b_copy(n, jj, across(m, jj)).wait_send()
        for jj in range(1, R // up_ways[n]):
            to_b(n, jj, v).wait_send()

    mine8 = rows_of(r * 8, 8, 8)
    s.norm_a[mine8, :] = jnp.zeros((8, LANES), F32)
    a_send(0)

    loads[7].wait()

    def backward_norm(k):
        rows = rows_of(k * ROWS, ROWS)
        table = s.rhot[rows, :]
        cot = s.ecot[rows, :].astype(F32)
        up = s.mcol[rows, :] * (cot + mm(table, s.agh[...]))
        normed = s.normed[rows, :]
        grad = norm_back(up * s.fv[1:2, :], normed, s.inv[rows, :]).astype(BF)
        s.og[rows, :] = grad
        s.vsum[0:1, :] += row_sum(grad.astype(F32))
        s.vsum[1:2, :] += row_sum(up * normed)
        s.vsum[2:3, :] += row_sum(up)

    loop(0, tiles, backward_norm)
    out_part = tn(s.hid[h], s.og[...])
    for p in (0, 1):
        for q in range(L // LANES):
            at = base_out + q * Q
            s.g[p, at : at + Q, :] = out_part[p * Q : (p + 1) * Q, q * LANES : (q + 1) * LANES]
    pair_start(1)

    def slope_half(which, k):
        rows = rows_of(k * ROWS, ROWS)
        w_rows = rows_of(which * half, half)
        value = (nt(s.og[rows, :], s.weo[w_rows, :]) * s.pre[which, rows, :]).astype(BF)
        s.sl[which, rows, :] = value
        return value

    def slope_sums(which):
        s.rs[which] = mm(s.rhot_t[...], s.sl[which])

        def slots(j):
            at = rows_of(j * TILE, TILE)
            s.ss[which, at, :] = mm(s.shot_t[at, :], s.sl[which])

        loop(0, slot_tiles, slots)

    def backward_own(k):
        value = slope_half(h, k)
        s.vsum[6:7, 0:half] += row_sum(value.astype(F32))

    loop(0, tiles, backward_own)
    slope_sums(h)

    pair_finish(1)
    a_send(1)

    edge_part = tn(s.ef[...], s.sl[h])
    recv_part = tn(s.nf[...], s.rs[h].astype(BF))
    for p in (0, 1):
        cols = slice(p * Q, (p + 1) * Q)
        s.g[p, base_in : base_in + L, :] = edge_part[:, cols]
        s.g[p, base_in + 2 * L : base_in + 3 * L, :] = recv_part[:, cols]
        for j in range(6):
            for q in range(L // LANES):
                at = base_vec + j * (L // LANES) + q
                s.g[p, at : at + 1, :] = s.vsum[j : j + 1, q * LANES : (q + 1) * LANES]
        s.g[p, base_vec + 24 : base_vec + 25, :] = s.vsum[6:7, cols]
        s.g[p, base_vec + 25 : base_vec + 26, :] = 0.5 * row_sum(s.nsl[2 * h + p].astype(F32))

    def sender_part(k):
        at = rows_of(k * TILE, TILE)
        value = tn(s.slots[at, :], s.ss[h, at, :].astype(BF))
        for p in (0, 1):
            s.g[p, base_in + L : base_in + 2 * L, :] += value[:, p * Q : (p + 1) * Q]

    loop(0, slot_tiles, sender_part)
    pair_start(2)
    b_send(0)
    pair_finish(2)
    a_send(2)

    def backward_other(k):
        rows = rows_of(k * ROWS, ROWS)
        value = slope_half(oh, k)
        cot = s.ecot[rows, :].astype(F32)
        back = nt(s.sl[0, rows, :], s.wei[0, 0:L, :]) + nt(s.sl[1, rows, :], s.wei[1, 0:L, :])
        s.eg[rows, :] = (cot + back).astype(BF)
        out_start(k, s.eg, s.eg_h, 1)

    loop(0, tiles, backward_other)
    slope_sums(oh)
    b_send(1)
    b_finish(0)

    def slot_grad(which, rows):
        at = rows_of(L + which * LH, LH)
        return nt(s.ss[0, rows, :].astype(BF), s.wei[0, at, :]) + nt(s.ss[1, rows, :].astype(BF), s.wei[1, at, :])

    def recv_grad(which):
        at = rows_of(2 * L + which * LH, LH)
        return nt(s.rs[0].astype(BF), s.wei[0, at, :]) + nt(s.rs[1].astype(BF), s.wei[1, at, :])

    def slot_other(k):
        rows = rows_of(k * TILE, TILE)
        s.tosend[rows, :] = slot_grad(oc, rows).astype(BF)

    loop(0, slot_tiles, slot_other)
    s.tosend[S : S + N, :] = recv_grad(oc).astype(BF)
    grad_swap = remote(s.tosend, s.torecv, s.xsend.at[1], s.xrecv.at[1], (r, pair))
    grad_swap.start()
    b_send(2)
    s.ntp[...] = (
        s.ncot[:, col_lane].astype(F32)
        + (nt(s.nsl[0], s.wni[rows_of(c * LH, LH), 0:Q]) + nt(s.nsl[1], s.wni[rows_of(c * LH, LH), Q : 2 * Q]))
        + (
            nt(s.nsl[2], s.wni[rows_of(c * LH, LH), 2 * Q : 3 * Q])
            + nt(s.nsl[3], s.wni[rows_of(c * LH, LH), 3 * Q : 4 * Q])
        )
        + recv_grad(c)
    )
    grad_swap.wait_recv()

    def slot_own(k):
        rows = rows_of(k * TILE, TILE)
        s.served[rows, :] = (slot_grad(c, rows) + s.torecv[rows, :].astype(F32)).astype(BF)

    ref = s.served.at[others]
    remote(ref, ref, s.ssend.at[0], s.srecv.at[0], (near_row, t)).wait_send()
    loop(0, slot_tiles, slot_own)

    def back_copy(k):
        to = lax.rem(r + k, R)
        return remote(s.served.at[rows_of(to * CAP, CAP)], s.ret.at[mine], s.ksend.at[0], s.krecv.at[0], (to, t))

    loop(1, R, lambda k: back_copy(k).start())
    b_finish(1)
    spread(0)
    b_finish(2)

    def norm_row(k):
        to = lax.rem(r + k, R)
        ref = s.norm_a.at[mine8]
        return remote(ref, ref, s.qsend.at[0], s.qrecv.at[0], (to, t))

    loop(1, R, lambda k: norm_row(k).start())
    s.ret[mine, :] = s.served[mine, :]
    s.ntp[...] += s.torecv[S : S + N, :].astype(F32)
    for n in (1, 2):
        spread(n)

    ref = s.norm_a.at[pl.ds(0, (R - 1) * 8)]
    remote(ref, ref, s.qsend.at[0], s.qrecv.at[0], (near_row, t)).wait()
    own_rows = rows_of(t * 8, 8, 8)
    s.nsq[own_rows, :] = jnp.sum(s.norm_a[...].reshape(R, 8, LANES), axis=0)
    for peer in (pair, far, diag):
        ref = s.nsq.at[own_rows]
        remote(ref, ref, s.tsem.at[0], s.tsem.at[1], (r, peer)).start()

    ref = s.ret.at[others]
    remote(ref, ref, s.ksend.at[0], s.krecv.at[0], (near_row, t)).wait()

    def gathered(k):
        lanes = pl.ds(pl.multiple_of(k * TILE, TILE), TILE)
        s.ntp[...] += mm(s.serve_t[:, lanes], s.ret[rows_of(k * TILE, TILE), :])

    loop(0, slot_tiles, gathered)
    s.ng[...] = s.ntp[...].astype(BF)
    ng_keep = local(s.ng, s.ng_h.at[:, col_lane], s.nsem.at[1])
    ng_keep.start()
    ng_send = remote(s.ng, s.ng_h.at[:, col_lane], s.xsend.at[3], s.xrecv.at[3], (r, pair))
    ng_send.start()

    for n in (0, 1, 2):
        spread_wait(n)
    ref = s.nsq.at[pl.ds(0, 24)]
    remote(ref, ref, s.tsem.at[0], s.tsem.at[1], (r, pair)).wait()
    total = s.nsq[0:8, :] + s.nsq[8:16, :] + s.nsq[16:24, :] + s.nsq[24:32, :]
    s.norm_o[...] = jnp.sqrt(jnp.full((8, LANES), jnp.sum(total), F32))
    for n in (0, 1, 2):
        sums_done(n)
    weights_sent()
    slot_swap.wait_send()
    grad_swap.wait_send()

    out_wait(s.ne, s.ne_h, 0)
    out_wait(s.eg, s.eg_h, 1)
    nn_copy.wait()
    ng_keep.wait()
    ng_send.wait_send()
    ref = s.ng_h.at[:, other_lane]
    remote(ref, ref, s.xsend.at[3], s.xrecv.at[3], (r, pair)).wait_recv()


def adam(weight, first, second, gradient, factor, rate):
    clipped = gradient * factor
    first_new = beta_one * first + (1.0 - beta_one) * clipped
    second_new = beta_two * second + (1.0 - beta_two) * clipped * clipped
    bias_one = 1.0 - beta_one**adam_step
    bias_two = 1.0 - beta_two**adam_step
    moved = first_new / bias_one / (jnp.sqrt(second_new / bias_two) + adam_eps) + decay_rate * weight
    return weight - rate * moved, first_new, second_new


def update(names, d, *refs):
    s = types.SimpleNamespace(**dict(zip(names, refs, strict=True)))
    L, Q = d.L, d.Q
    passes = [
        pltpu.make_async_copy(s.__dict__[f"pass{k}"], s.__dict__[f"out{k}"], s.psem.at[k]) for k in range(4)
    ]
    for copy in passes:
        copy.start()
    norm = s.norm[0:1, 0:1]
    s.norm_o[0] = s.norm[0, 0]
    factor = clip_level / jnp.maximum(norm, clip_level)
    copies = []

    def one(k, grad, at, rate):
        values = adam(
            s.__dict__[f"in{k}"][at], s.__dict__[f"in{6 + k}"][at], s.__dict__[f"in{12 + k}"][at], grad, factor, rate
        )
        for n, value in enumerate(values):
            s.__dict__[f"buf{6 * n + k}"][at] = value

    def send(k):
        for n in range(3):
            m = 6 * n + k
            copy = pltpu.make_async_copy(s.__dict__[f"buf{m}"], s.__dict__[f"new{m}"], s.osem.at[m])
            copy.start()
            copies.append(copy)

    everything = (slice(None), slice(None))
    for k, base in ((2, d.base_node), (0, d.base_in)):
        for low in range(0, (2 if k == 2 else 3) * L, 256):
            rows = slice(low, low + 256)
            one(k, s.fin[base + low : base + low + 256, :].astype(F32), (rows, slice(None)), learn_rate)
        send(k)
    for k, base in ((3, d.base_node + 2 * L), (1, d.base_out)):
        for q in range(L // LANES):
            at = (slice(None), slice(q * LANES, (q + 1) * LANES))
            one(k, s.fin[base + q * LANES : base + (q + 1) * LANES, :].astype(F32), at, learn_rate)
        send(k)
    vec = s.fin[d.base_in + 3 * L : d.base_in + 3 * L + 32, :].astype(F32)
    one(4, vec[24:26, :], everything, vector_rate)
    send(4)
    for j in range(6):
        for q in range(L // LANES):
            m = j * (L // LANES) + q
            at = (slice(j, j + 1), slice(q * LANES, (q + 1) * LANES))
            one(5, vec[m : m + 1, :], at, vector_rate)
    send(5)
    for copy in copies + passes:
        copy.wait()


def device_step(
    node_feats,
    edge_feats,
    edge_receiver,
    edge_slot,
    edge_mask,
    serve_rows,
    node_cot,
    edge_cot,
    *states,
):
    weights = states[:6]
    d = types.SimpleNamespace()
    d.R = lax.axis_size("rows")
    d.N, d.L = node_feats.shape
    d.E = edge_feats.shape[0]
    d.Q = weights[0].shape[1]
    d.H = d.Q * lax.axis_size("tp")
    d.CAP = serve_rows.shape[1]
    R, N, E, L, H, Q = d.R, d.N, d.E, d.L, d.H, d.Q
    EH, S = E // 2, R * d.CAP
    tiles = EH // ROWS

    def padded(count):
        return -(-count // (16 * R)) * (16 * R)

    d.size_node, d.size_out, d.size_in = padded(3 * L), padded(L), padded(3 * L + 32)
    d.base_node, d.base_out, d.base_in = 0, d.size_node, d.size_node + d.size_out
    G = d.size_node + d.size_out + d.size_in
    d.down, d.up = DOWN, UP
    most = R // min(*DOWN, *UP)
    vmem_spec = pl.BlockSpec(memory_space=pltpu.VMEM)
    inputs = dict(
        nf_h=node_feats,
        ef_h=edge_feats,
        ncot_h=node_cot,
        ecot_h=edge_cot,
        wei_h=weights[0],
        weo_h=weights[1],
        wni_h=weights[2],
        wno_h=weights[3],
        hb_h=weights[4],
        fv_h=weights[5],
        rec2_h=edge_receiver.reshape(-1, LANES),
        slot2_h=edge_slot.reshape(-1, LANES),
        mask2_h=edge_mask.reshape(-1, LANES),
        rec1_h=edge_receiver.reshape(1, -1),
        slot1_h=edge_slot.reshape(1, -1),
        serve_h=serve_rows,
    )
    hbm_spec = pl.BlockSpec(memory_space=pltpu.HBM)
    outputs = dict(
        nn_h=(jax.ShapeDtypeStruct((N, L), BF), hbm_spec),
        ne_h=(jax.ShapeDtypeStruct((E, L), BF), hbm_spec),
        ng_h=(jax.ShapeDtypeStruct((N, L), BF), hbm_spec),
        eg_h=(jax.ShapeDtypeStruct((E, L), BF), hbm_spec),
        fin_o=(jax.ShapeDtypeStruct((G, Q), BF), vmem_spec),
        norm_o=(jax.ShapeDtypeStruct((8, LANES), F32), vmem_spec),
    )
    dma = pltpu.SemaphoreType.DMA
    scratch = dict(
        hb=pltpu.VMEM((2, Q), F32),
        fv=pltpu.VMEM((6, L), F32),
        rec2=pltpu.VMEM((E // LANES, LANES), jnp.int32),
        slot2=pltpu.VMEM((E // LANES, LANES), jnp.int32),
        mask2=pltpu.VMEM((E // LANES, LANES), jnp.int32),
        rec1=pltpu.VMEM((1, E), jnp.int32),
        slot1=pltpu.VMEM((1, E), jnp.int32),
        serve=pltpu.VMEM((R, d.CAP), jnp.int32),
        wei32=pltpu.VMEM((3 * L, Q), F32),
        weo32=pltpu.VMEM((Q, L), F32),
        wni32=pltpu.VMEM((2 * L, Q), F32),
        wno32=pltpu.VMEM((Q, L), F32),
        nf=pltpu.VMEM((N, L), BF),
        ef=pltpu.VMEM((EH, L), BF),
        ncot=pltpu.VMEM((N, L), BF),
        ecot=pltpu.VMEM((EH, L), BF),
        wei=pltpu.VMEM((2, 3 * L, H // 2), BF),
        weo=pltpu.VMEM((H, L), BF),
        wni=pltpu.VMEM((2 * L, H), BF),
        wno=pltpu.VMEM((H, L), BF),
        bias=pltpu.VMEM((8, H), F32),
        serve_col=pltpu.VMEM((S, 1), F32),
        serve_t=pltpu.VMEM((N, S), BF),
        served=pltpu.VMEM((S, L // 2), BF),
        slots=pltpu.VMEM((S, L), BF),
        ret=pltpu.VMEM((S, L // 2), BF),
        rcol=pltpu.VMEM((EH, 1), F32),
        scol=pltpu.VMEM((EH, 1), F32),
        mcol=pltpu.VMEM((EH, 1), F32),
        rhot=pltpu.VMEM((EH, N), BF),
        rhot_t=pltpu.VMEM((N, EH), BF),
        shot_t=pltpu.VMEM((S, EH), BF),
        xr=pltpu.VMEM((EH, L), BF),
        xs=pltpu.VMEM((EH, L), BF),
        part=pltpu.VMEM((EH, L), F32),
        mk=pltpu.VMEM((EH, L), BF),
        pre=pltpu.VMEM((2, EH, H // 2), F32),
        hid=pltpu.VMEM((2, EH, H // 2), BF),
        normed=pltpu.VMEM((EH, L), F32),
        inv=pltpu.VMEM((EH, 1), F32),
        ne=pltpu.VMEM((EH, L), BF),
        eg=pltpu.VMEM((EH, L), BF),
        aggp=pltpu.VMEM((N, L), F32),
        aggr=pltpu.VMEM((N, L), F32),
        nn=pltpu.VMEM((N, L), BF),
        ng=pltpu.VMEM((N, L // 2), BF),
        agh=pltpu.VMEM((N, L), BF),
        ntp=pltpu.VMEM((N, L // 2), F32),
        nsl=pltpu.VMEM((H // Q, N, Q), BF),
        nhid=pltpu.VMEM((H // Q, N, Q), BF),
        og=pltpu.VMEM((EH, L), BF),
        sl=pltpu.VMEM((2, EH, H // 2), BF),
        rs=pltpu.VMEM((2, N, H // 2), F32),
        ss=pltpu.VMEM((2, S, H // 2), F32),
        tosend=pltpu.VMEM((S + N, L // 2), BF),
        torecv=pltpu.VMEM((S + N, L // 2), BF),
        g=pltpu.VMEM((2, G, Q), F32),
        sb=pltpu.VMEM((G, Q), BF),
        rbp=pltpu.VMEM((G, Q), BF),
        rba=pltpu.VMEM((3, G, Q), BF),
        rbb=pltpu.VMEM((most - 1, G // R, Q), BF),
        vsum=pltpu.VMEM((8, L), F32),
        norm_a=pltpu.VMEM((8 * R, LANES), F32),
        nsq=pltpu.VMEM((32, LANES), F32),
        lsem=dma((16,)),
        wsend=dma((22,)),
        wrecv=dma((28,)),
        ssend=dma((1,)),
        srecv=dma((1,)),
        ksend=dma((1,)),
        krecv=dma((1,)),
        qsend=dma((1,)),
        qrecv=dma((1,)),
        osem=dma((2,)),
        osend=dma((2,)),
        orecv=dma((2,)),
        xsend=dma((5,)),
        xrecv=dma((5,)),
        nsem=dma((2,)),
        psend=dma((3,)),
        precv=dma((3,)),
        asend=dma((3,)),
        arecv=dma((3, most)),
        bsend=dma((3, most - 1)),
        brecv=dma((3, most - 1)),
        fbsend=dma((3, most - 1)),
        fbrecv=dma((3, most - 1)),
        fasend=dma((3,)),
        farecv=dma((3,)),
        tsem=dma((2,)),
    )
    names = (*inputs, *outputs, *scratch)
    limit = 6 * 1024 * 1024
    for x in scratch.values():
        if x.memory_space == pltpu.VMEM:
            *lead, rows, lanes = x.shape
            limit += math.prod(lead) * rows * -(-lanes // LANES) * LANES * jnp.dtype(x.dtype).itemsize
    new_nodes, new_edges, node_gradient, edge_gradient, fin, norm = pl.pallas_call(
        functools.partial(layer, names, d),
        out_shape=[shape for shape, _ in outputs.values()],
        in_specs=[hbm_spec] * len(inputs),
        out_specs=[spec for _, spec in outputs.values()],
        scratch_shapes=list(scratch.values()),
        compiler_params=pltpu.CompilerParams(
            collective_id=0, has_side_effects=True, vmem_limit_bytes=limit
        ),
    )(*(pltpu.with_memory_space_constraint(x, pltpu.HBM) for x in inputs.values()))

    passes = (new_nodes, new_edges, node_gradient, edge_gradient)
    names = (
        "fin",
        "norm",
        *(f"pass{k}" for k in range(4)),
        *(f"in{k}" for k in range(18)),
        *(f"out{k}" for k in range(4)),
        "norm_o",
        *(f"new{k}" for k in range(18)),
        *(f"buf{k}" for k in range(18)),
        "psem",
        "osem",
    )
    outs = pl.pallas_call(
        functools.partial(update, names, d),
        out_shape=[
            *(jax.ShapeDtypeStruct(x.shape, x.dtype) for x in passes),
            jax.ShapeDtypeStruct((1,), F32),
            *(jax.ShapeDtypeStruct(x.shape, F32) for x in states),
        ],
        in_specs=[vmem_spec, vmem_spec, *[hbm_spec] * 4, *[vmem_spec] * 18],
        out_specs=[*[hbm_spec] * 4, pl.BlockSpec(memory_space=pltpu.SMEM), *[hbm_spec] * 18],
        scratch_shapes=[*(pltpu.VMEM(x.shape, F32) for x in states), dma((4,)), dma((18,))],
        compiler_params=pltpu.CompilerParams(vmem_limit_bytes=12 * 1024 * 1024),
    )(fin, norm, *passes, *states)
    return tuple(outs)


def solution(mesh):
    split = [P(None, "tp"), P("tp", None), P(None, "tp"), P("tp", None), P(None, "tp"), P()]
    row = P("rows", None)
    return jax.shard_map(
        device_step,
        mesh=mesh,
        in_specs=(row, row, P("rows"), P("rows"), P("rows"), row, row, row, *split, *split, *split),
        out_specs=(row, row, row, row, P(), *split, *split, *split),
        check_vma=False,
    )
```

```python
import functools
import math
import types

import jax
import jax.numpy as jnp
from jax import lax
from jax.experimental import pallas as pl
from jax.experimental.pallas import tpu as pltpu
from jax.sharding import PartitionSpec as P

BF = jnp.bfloat16
F32 = jnp.float32
MESH = pl.DeviceIdType.MESH
LANES = 128
TILE = 256
ROWS = 512
DOWN = (4, 4, 4)
UP = (4, 4, 4)

beta_one = 0.9
beta_two = 0.999
adam_step = 7.0
adam_eps = 1e-08
learn_rate = 0.05
vector_rate = 0.3
decay_rate = 0.1
clip_level = 1.0


def mm(left, right):
    return jnp.dot(left, right, preferred_element_type=F32)


def nt(left, right):
    return lax.dot_general(left, right, (((1,), (1,)), ((), ())), preferred_element_type=F32)


def tn(left, right):
    return lax.dot_general(left, right, (((0,), (0,)), ((), ())), preferred_element_type=F32)


def two(values):
    high = values.astype(BF)
    return high, (values - high.astype(F32)).astype(BF)


def aligned(start, step):
    return start if isinstance(start, int) else pl.multiple_of(start, step)


def rows_of(start, size, step=16):
    return pl.ds(aligned(start, step), size)


def hot(cond):
    return jnp.where(cond, 1.0, 0.0).astype(BF)


def normalize(values):
    center = values - jnp.mean(values, axis=1, keepdims=True)
    inverse = lax.rsqrt(jnp.mean(center * center, axis=1, keepdims=True) + 1e-05)
    return center * inverse, inverse


def norm_back(scaled, normed, inverse):
    first = jnp.mean(scaled, axis=1, keepdims=True)
    second = jnp.mean(scaled * normed, axis=1, keepdims=True)
    return inverse * (scaled - first - normed * second)


def row_sum(values):
    return jnp.sum(values, axis=0, keepdims=True)


def layer(names, d, *refs):
    s = types.SimpleNamespace(**dict(zip(names, refs, strict=True)))
    R, N, E, L, H, Q, CAP = d.R, d.N, d.E, d.L, d.H, d.Q, d.CAP
    EH, S, half, LH, LQ = E // 2, R * CAP, H // 2, L // 2, L // 4
    tiles, slot_tiles, nb = EH // ROWS, S // TILE, R // 4
    r = lax.axis_index("rows")
    t = lax.axis_index("tp")
    h, c = t // 2, lax.rem(t, 2)
    oh, oc = 1 - h, 1 - c
    pair = t + 1 - 2 * c
    far = t + 2 - 4 * h
    diag = pair + 2 - 4 * h
    a, b = lax.rem(r, 4), r // 4
    edge0 = c * EH
    near_row = lax.rem(r + 1, R)
    own_lane = pl.ds(pl.multiple_of(t * Q, Q), Q)
    core_lane = pl.ds(pl.multiple_of(c * Q, Q), Q)
    far_lane = pl.ds(pl.multiple_of(far * Q, Q), Q)
    col_lane = pl.ds(pl.multiple_of(c * LH, LH), LH)

    def local(src, dst, sem):
        return pltpu.make_async_copy(src, dst, sem)

    def remote(src, dst, send, recv, device):
        return pltpu.make_async_remote_copy(
            src_ref=src, dst_ref=dst, send_sem=send, recv_sem=recv, device_id=device, device_id_type=MESH
        )

    def loop(low, high, body):
        def step(k, carry):
            body(k)
            return carry

        if high - low <= 8:
            for k in range(low, high):
                body(k)
        else:
            lax.fori_loop(low, high, step, 0)

    loads = [
        local(s.wei_h, s.wei32, s.lsem.at[0]),
        local(s.nf_h, s.nf, s.lsem.at[1]),
        local(s.ef_h.at[rows_of(edge0, EH)], s.ef, s.lsem.at[2]),
        local(s.weo_h, s.weo32, s.lsem.at[3]),
        local(s.wni_h, s.wni32, s.lsem.at[4]),
        local(s.wno_h, s.wno32, s.lsem.at[5]),
        local(s.ncot_h, s.ncot, s.lsem.at[6]),
        local(s.ecot_h.at[rows_of(edge0, EH)], s.ecot, s.lsem.at[7]),
        local(s.serve_h, s.serve, s.lsem.at[8]),
        local(s.hb_h, s.hb, s.lsem.at[9]),
        local(s.fv_h, s.fv, s.lsem.at[10]),
        local(s.rec2_h, s.rec2, s.lsem.at[11]),
        local(s.slot2_h, s.slot2, s.lsem.at[12]),
        local(s.mask2_h, s.mask2, s.lsem.at[13]),
        local(s.rec1_h, s.rec1, s.lsem.at[14]),
        local(s.slot1_h, s.slot1, s.lsem.at[15]),
    ]
    for k in (0, 1, 8, 9, 3, 11, 12, 13, 14, 15, 2, 4, 5, 10, 6, 7):
        loads[k].start()

    barrier = pltpu.get_barrier_semaphore()
    for peer in (pair, far, diag):
        pl.semaphore_signal(barrier, inc=1, device_id=(r, peer), device_id_type=MESH)

    def greet(k):
        pl.semaphore_signal(barrier, inc=1, device_id=(lax.rem(r + k, R), t), device_id_type=MESH)

    loop(1, R, greet)

    shared = (1, 2, 4, 5)

    def block(i, tt, part=None):
        lane = pl.ds(pl.multiple_of(tt * Q, Q), Q)
        if i < 3:
            half_lane = pl.ds(pl.multiple_of(lax.rem(tt, 2) * Q, Q), Q)
            rows = pl.ds((0, 2 * L, L)[i], L) if part is None else rows_of((0, 2 * L, L)[i] + part * (L // 4), L // 4)
            return s.wei.at[tt // 2, rows, half_lane]
        if i == 3:
            return s.weo.at[lane, :]
        if i < 6:
            low = (L, 0)[i - 4]
            return s.wni.at[pl.ds(low, L) if part is None else rows_of(low + part * (L // 4), L // 4), lane]
        if i == 6:
            return s.wno.at[lane, :]
        return s.bias.at[:, lane]

    groups = (0, 0, 0, 1, 2, 2, 3, 4)

    def weight_copy(i, way, who):
        ref = block(i, who, a if way == 1 and i in shared else None)
        sent = 10 + i if way == 1 else groups[i] + 5 * (way // 2)
        return remote(ref, ref, s.wsend.at[sent], s.wrecv.at[8 * way + i], (r, (pair, far, pair)[way]))

    def part_copy(i, j, ref):
        at = shared.index(i)
        device = (b * 4 + lax.rem(a + j, 4), t)
        return remote(ref, ref, s.wsend.at[18 + at], s.wrecv.at[24 + at], device)

    def three_parts(i):
        low, size = (0, 2 * L, L, 0, L, 0)[i], 3 * (L // 4)
        if i < 3:
            return s.wei.at[oh, pl.ds(low, size), core_lane]
        return s.wni.at[pl.ds(low, size), far_lane]

    def weights_sent():
        for way, tt, th, lane in ((0, t, h, own_lane), (2, far, oh, far_lane)):
            for k, ref in enumerate(
                (s.wei.at[th, :, core_lane], block(3, tt), s.wni.at[:, lane], block(6, tt), block(7, tt))
            ):
                remote(ref, ref, s.wsend.at[k + 5 * (way // 2)], s.wrecv.at[0], (r, pair)).wait_send()
        for i in range(8):
            weight_copy(i, 1, t).wait_send()
        for i in shared:
            part_copy(i, 1, three_parts(i)).wait_send()

    def weight_send(i, way):
        weight_copy(i, way, t).start()

    def weight_wait(i, way):
        weight_copy(i, way, (pair, far, diag)[way]).wait_recv()

    def part_spread(i):
        weight_wait(i, 1)
        for j in (1, 2, 3):
            part_copy(i, j, block(i, far, a)).start()

    def weight_forward(i):
        if i in shared:
            part_copy(i, 1, three_parts(i)).wait_recv()
        else:
            weight_wait(i, 1)
        weight_copy(i, 2, far).start()

    loads[0].wait()
    for i in range(3):
        at = pl.ds((0, 2 * L, L)[i], L)
        s.wei[h, at, core_lane] = s.wei32[at, :].astype(BF)
    loads[9].wait()
    s.bias[0:2, own_lane] = s.hb[...]
    s.bias[2:8, own_lane] = jnp.zeros((6, Q), F32)
    loads[1].wait()

    loads[8].wait()
    turned = jnp.transpose(s.serve[...].astype(F32))
    for k in range(R):
        s.serve_col[k * CAP : (k + 1) * CAP, :] = turned[:, k : k + 1]

    def serve(k):
        at = rows_of(k * TILE, TILE)
        table = s.serve_col[at, :].astype(jnp.int32) == lax.broadcasted_iota(jnp.int32, (TILE, N), 1)
        table = jnp.where(table, 1.0, 0.0)
        s.serve_t[:, pl.ds(pl.multiple_of(k * TILE, TILE), TILE)] = jnp.transpose(table).astype(BF)
        s.served[at, :] = mm(table.astype(BF), s.nf[:, col_lane]).astype(BF)

    loop(0, slot_tiles, serve)
    pl.semaphore_wait(barrier, R + 2)

    for i in (1, 2, 7, 0):
        weight_send(i, 1)
    mine = rows_of(r * CAP, CAP)

    def served_copy(k):
        to = lax.rem(r + k, R)
        return remote(
            s.served.at[rows_of(to * CAP, CAP)],
            s.slots.at[mine, col_lane],
            s.ssend.at[0],
            s.srecv.at[0],
            (to, t),
        )

    loop(1, R, lambda k: served_copy(k).start())
    s.slots[mine, col_lane] = s.served[mine, :]
    for i in (0, 1, 2, 7):
        weight_send(i, 0)
    loads[4].wait()
    for i in (4, 5):
        at = pl.ds((L, 0)[i - 4], L)
        s.wni[at, own_lane] = s.wni32[at, :].astype(BF)
        weight_send(i, 1)
    loads[3].wait()
    s.weo[own_lane, :] = s.weo32[...].astype(BF)
    loads[5].wait()
    s.wno[own_lane, :] = s.wno32[...].astype(BF)
    for i in (3, 6):
        weight_send(i, 1)
    for i in (3, 4, 5, 6):
        weight_send(i, 0)

    for k in (11, 12, 13, 14, 15):
        loads[k].wait()
    per = EH // LANES
    at = rows_of(c * per, per, 8)
    for source, target in ((s.rec2, s.rcol), (s.slot2, s.scol), (s.mask2, s.mcol)):
        turned = jnp.transpose(source[at, :].astype(F32))
        for k in range(per):
            target[k * LANES : (k + 1) * LANES, :] = turned[:, k : k + 1]
    lanes_here = pl.ds(pl.multiple_of(edge0, EH), EH)
    s.rhot_t[...] = hot(s.rec1[:, lanes_here] == lax.broadcasted_iota(jnp.int32, (N, EH), 0))
    part_spread(1)
    part_spread(2)

    def slot_table(k):
        rows = rows_of(k * TILE, TILE)
        s.shot_t[rows, :] = hot(
            s.slot1[:, lanes_here] == lax.broadcasted_iota(jnp.int32, (TILE, EH), 0) + k * TILE
        )

    loop(0, slot_tiles, slot_table)

    def receivers(k):
        rows = rows_of(k * ROWS, ROWS)
        index = s.rcol[rows, :].astype(jnp.int32)
        table = hot(index == lax.broadcasted_iota(jnp.int32, (ROWS, N), 1))
        s.rhot[rows, :] = table
        s.xr[rows, :] = mm(table, s.nf[...]).astype(BF)

    loop(0, tiles, receivers)
    loads[2].wait()

    def first_two(which):
        def body(k):
            rows = rows_of(k * ROWS, ROWS)
            value = mm(s.ef[rows, :], s.wei[which, 0:L, :])
            s.pre[which, rows, :] = value + mm(s.xr[rows, :], s.wei[which, 2 * L : 3 * L, :])

        loop(0, tiles, body)

    def hidden_of(which, k):
        rows = rows_of(k * ROWS, ROWS)
        lanes = pl.ds(pl.multiple_of(which * half, half), half)
        pre = s.pre[which, rows, :] + mm(s.xs[rows, :], s.wei[which, L : 2 * L, :]) + s.bias[0:1, lanes]
        sig = 0.5 + 0.5 * jnp.tanh(0.5 * pre)
        value = (pre * sig).astype(BF)
        s.hid[which, rows, :] = value
        s.pre[which, rows, :] = sig + (pre * sig) * (1.0 - sig)

    def outer_of(which, k):
        return mm(s.hid[which, rows_of(k * ROWS, ROWS), :], s.weo[rows_of(which * half, half), :])

    for i in (0, 1):
        weight_wait(i, 0)
    first_two(h)
    for low, high in (
        (d.base_node + 3 * L, d.base_out),
        (d.base_out + L, d.base_in),
        (d.base_in + L, d.base_in + 2 * L),
        (d.base_in + 3 * L, d.base_in + d.size_in),
    ):
        if high > low:
            s.g[:, low:high, :] = jnp.zeros((2, high - low, Q), F32)
    weight_forward(0)

    others = pl.ds(0, (R - 1) * CAP)
    ref = s.slots.at[others, col_lane]
    remote(ref, ref, s.ssend.at[0], s.srecv.at[0], (near_row, t)).wait_recv()
    slot_swap = remote(s.slots.at[:, col_lane], s.slots.at[:, col_lane], s.xsend.at[2], s.xrecv.at[2], (r, pair))
    slot_swap.start()
    weight_forward(1)
    other_lane = pl.ds(pl.multiple_of(oc * LH, LH), LH)
    ref = s.slots.at[:, other_lane]
    remote(ref, ref, s.xsend.at[2], s.xrecv.at[2], (r, pair)).wait_recv()

    def senders(k):
        rows = rows_of(k * ROWS, ROWS)
        index = s.scol[rows, :].astype(jnp.int32)
        table = hot(index == lax.broadcasted_iota(jnp.int32, (ROWS, S), 1))
        s.xs[rows, :] = mm(table, s.slots[...]).astype(BF)

    loop(0, tiles, senders)
    weight_forward(2)
    part_spread(4)
    part_spread(5)
    for i in (2, 7, 3):
        weight_wait(i, 0)

    def own_half(k):
        hidden_of(h, k)
        s.part[rows_of(k * ROWS, ROWS), :] = outer_of(h, k)

    loop(0, tiles, own_half)
    weight_forward(7)
    for i in (0, 1):
        weight_wait(i, 2)
    first_two(oh)
    for i in (2, 7):
        weight_wait(i, 2)
    weight_forward(3)
    loop(0, tiles, lambda k: hidden_of(oh, k))
    weight_wait(3, 2)
    loads[10].wait()

    def out_copies(rows, source, target, which):
        here = source.at[rows]
        there = target.at[rows_of(edge0 + rows.start, rows.size)]
        keep = local(here, there, s.osem.at[which])
        send = remote(here, there, s.osend.at[which], s.orecv.at[which], (r, pair))
        return keep, send

    def out_start(k, source, target, which):
        keep, send = out_copies(pl.ds(k * ROWS, ROWS), source, target, which)
        keep.start()
        send.start()

    def out_wait(source, target, which):
        keep, send = out_copies(pl.ds(0, EH), source, target, which)
        keep.wait()
        send.wait_send()
        ref = target.at[rows_of(oc * EH, EH)]
        remote(ref, ref, s.osend.at[which], s.orecv.at[which], (r, pair)).wait_recv()

    def forward(k):
        rows = rows_of(k * ROWS, ROWS)
        outer = s.part[rows, :] + outer_of(oh, k) + s.fv[0:1, :]
        normed, inverse = normalize(outer)
        s.normed[rows, :] = normed
        s.inv[rows, :] = inverse
        masked = s.mcol[rows, :] * (normed * s.fv[1:2, :] + s.fv[2:3, :])
        s.ne[rows, :] = (s.ef[rows, :].astype(F32) + masked).astype(BF)
        out_start(k, s.ne, s.ne_h, 0)
        s.mk[rows, :] = masked.astype(BF)

    loop(0, tiles, forward)
    swaps = []
    for k in (0, 1):
        at = pl.ds(k * (N // 2), N // 2)
        s.aggp[at, :] = mm(s.rhot_t[at, :], s.mk[...])
        swap = remote(s.aggp.at[at], s.aggr.at[at], s.xsend.at[4 * k], s.xrecv.at[4 * k], (r, pair))
        swap.start()
        swaps.append(swap)
    for i in (4, 5, 6):
        weight_forward(i)
    weight_wait(5, 0)
    weight_wait(5, 2)
    own_term = mm(s.nf[...], s.wni[0:L, :])
    weight_wait(4, 0)
    weight_wait(4, 2)
    for swap in swaps:
        swap.wait()

    agg = (s.aggp[...] + s.aggr[...]).astype(BF)
    pre = own_term + mm(agg, s.wni[L : 2 * L, :]) + s.bias[1:2, :]
    sig = 0.5 + 0.5 * jnp.tanh(0.5 * pre)
    node_hidden = (pre * sig).astype(BF)
    slope_of = sig + (pre * sig) * (1.0 - sig)
    weight_wait(6, 0)
    weight_wait(6, 2)
    outer = mm(node_hidden, s.wno[...]) + s.fv[3:4, :]
    normed, inverse = normalize(outer)
    s.nn[...] = (s.nf[...].astype(F32) + (normed * s.fv[4:5, :] + s.fv[5:6, :])).astype(BF)
    nn_copy = local(s.nn, s.nn_h, s.nsem.at[0])
    nn_copy.start()
    loads[6].wait()
    up = s.ncot[...].astype(F32)
    node_outer_grad = norm_back(up * s.fv[4:5, :], normed, inverse).astype(BF)
    node_slope = (nt(node_outer_grad, s.wno[...]) * slope_of).astype(BF)
    s.agh[...] = nt(node_slope, s.wni[L : 2 * L, :]).astype(BF)

    for q in range(H // Q):
        s.nsl[q] = node_slope[:, q * Q : (q + 1) * Q]
        s.nhid[q] = node_hidden[:, q * Q : (q + 1) * Q]
    s.vsum[...] = jnp.zeros_like(s.vsum)
    s.vsum[3:4, :] = 0.5 * row_sum(node_outer_grad.astype(F32))
    s.vsum[4:5, :] = 0.5 * row_sum(up * normed)
    s.vsum[5:6, :] = 0.5 * row_sum(up)
    base_node, base_out, base_in, base_vec = d.base_node, d.base_out, d.base_in, d.base_in + 3 * L
    s.g[c, 0:L, :] = tn(s.nf[...], s.nsl[t])
    s.g[c, L : 2 * L, :] = tn(agg, s.nsl[t])
    node_out_grad = tn(s.nhid[t], node_outer_grad)
    for q in range(L // LANES):
        s.g[c, 2 * L + q * Q : 2 * L + (q + 1) * Q, :] = node_out_grad[:, q * LANES : (q + 1) * LANES]

    chunks = ((base_node, d.size_node), (base_out, d.size_out), (base_in, d.size_in))

    down, up_ways = d.down, d.up

    def piece(n, row):
        base, size = chunks[n]
        m = down[n]
        return rows_of(base + (lax.rem(row, m) * (R // m) + row // m) * (size // R), size // R)

    v = r

    def placed(row):
        return row

    def near(m, j):
        return (v // m) * m + lax.rem(v + j, m)

    def across(m, j):
        return lax.rem(v // m + j, R // m) * m + lax.rem(v, m)

    def crossed(m, row, j):
        return lax.rem(row // m + j, R // m) * m + lax.rem(row, m)

    def pair_copy(n):
        at = pl.ds(*chunks[n])
        return remote(s.sb.at[at], s.rbp.at[at], s.psend.at[n], s.precv.at[n], (r, pair))

    def pair_start(n):
        at = pl.ds(*chunks[n])
        s.sb[at, :] = s.g[oc, at, :].astype(BF)
        pair_copy(n).start()

    def pair_finish(n):
        pair_copy(n).wait()
        at = pl.ds(*chunks[n])
        if n == 2:
            vec = pl.ds(base_vec, 32)
            s.g[c, vec, :] = s.g[c, vec, :].astype(BF).astype(F32)
        s.g[c, at, :] += s.rbp[at, :].astype(F32)

    def a_copy(n, jj, j, target):
        at = piece(n, crossed(down[n], target, jj))
        return remote(
            s.sb.at[at], s.rba.at[j - 1, at], s.asend.at[n], s.arecv.at[n, jj], (placed(near(down[n], j)), t)
        )

    def b_slot(n):
        base, size = chunks[n]
        return pl.ds(base // R, size // R)

    def b_copy(n, jj, row):
        return remote(
            s.sb.at[piece(n, row)],
            s.rbb.at[jj - 1, b_slot(n)],
            s.bsend.at[n, jj - 1],
            s.brecv.at[n, jj - 1],
            (placed(across(down[n], jj)), t),
        )

    def a_send(n):
        at = pl.ds(*chunks[n])
        s.sb[at, :] = s.g[c, at, :].astype(BF)
        for jj in (*range(1, R // down[n]), 0):
            for j in range(1, down[n]):
                a_copy(n, jj, j, near(down[n], j)).start()

    def a_sum(n, jj):
        at = piece(n, across(down[n], jj))
        total = s.g[c, at, :]
        ref = s.rba.at[pl.ds(0, down[n] - 1), at]
        remote(ref, ref, s.asend.at[n], s.arecv.at[n, jj], (near_row, t)).wait_recv()
        for j in range(1, down[n]):
            total = total + s.rba[j - 1, at, :].astype(F32)
        return total

    def b_send(n):
        for jj in range(1, R // down[n]):
            row = across(down[n], jj)
            s.sb[piece(n, row), :] = a_sum(n, jj).astype(BF)
            b_copy(n, jj, row).start()

    def to_b(n, jj, row):
        ref = s.fin_o.at[piece(n, row)]
        return remote(ref, ref, s.fbsend.at[n, jj - 1], s.fbrecv.at[n, jj - 1], (placed(across(up_ways[n], jj)), t))

    def to_a(n, jj, j, row):
        ref = s.fin_o.at[piece(n, row)]
        return remote(ref, ref, s.fasend.at[n], s.farecv.at[n], (placed(near(up_ways[n], j)), t))

    def b_finish(n):
        total = a_sum(n, 0)
        at = piece(n, v)
        for jj in range(1, R // down[n]):
            b_copy(n, jj, v).wait_recv()
            total = total + s.rbb[jj - 1, b_slot(n), :].astype(F32)
        final = total.astype(BF)
        s.fin_o[at, :] = final
        for jj in range(1, R // up_ways[n]):
            to_b(n, jj, v).start()
        for j in range(1, up_ways[n]):
            to_a(n, 0, j, v).start()
        final = final.astype(F32)
        squares = final * final
        count = squares.shape[0]
        if n == 2:
            m = down[n]
            low = base_in + (lax.rem(v, m) * (R // m) + v // m) * count
            index = lax.broadcasted_iota(jnp.int32, (count, LANES), 0) + low
            copied = jnp.logical_and(index >= base_vec, index < base_vec + 24)
            squares = jnp.where(copied, 0.25 * squares, squares)
        s.norm_a[mine8, :] += jnp.sum(squares.reshape(count // 8, 8, LANES), axis=0)

    def spread(n):
        m = up_ways[n]
        for jj in range(1, R // m):
            row = crossed(m, v, R // m - jj)
            to_b(n, jj, row).wait_recv()
            for j in range(1, m):
                to_a(n, jj, j, row).start()

    def all_but_own(n, m):
        base, size = chunks[n]
        return pl.ds(base, (R - R // m) * (size // R))

    def spread_wait(n):
        ref = s.fin_o.at[all_but_own(n, up_ways[n])]
        remote(ref, ref, s.fasend.at[n], s.farecv.at[n], (near_row, t)).wait()

    def sums_done(n):
        m = down[n]
        ref = s.sb.at[all_but_own(n, m)]
        remote(ref, ref, s.asend.at[n], s.arecv.at[n, 0], (near_row, t)).wait_send()
        for jj in range(1, R // m):
            b_copy(n, jj, across(m, jj)).wait_send()
        for jj in range(1, R // up_ways[n]):
            to_b(n, jj, v).wait_send()

    mine8 = rows_of(r * 8, 8, 8)
    s.norm_a[mine8, :] = jnp.zeros((8, LANES), F32)
    a_send(0)

    loads[7].wait()

    def backward_norm(k):
        rows = rows_of(k * ROWS, ROWS)
        table = s.rhot[rows, :]
        cot = s.ecot[rows, :].astype(F32)
        up = s.mcol[rows, :] * (cot + mm(table, s.agh[...]))
        normed = s.normed[rows, :]
        grad = norm_back(up * s.fv[1:2, :], normed, s.inv[rows, :]).astype(BF)
        s.og[rows, :] = grad
        s.vsum[0:1, :] += row_sum(grad.astype(F32))
        s.vsum[1:2, :] += row_sum(up * normed)
        s.vsum[2:3, :] += row_sum(up)

    loop(0, tiles, backward_norm)
    out_part = tn(s.hid[h], s.og[...])
    for p in (0, 1):
        for q in range(L // LANES):
            at = base_out + q * Q
            s.g[p, at : at + Q, :] = out_part[p * Q : (p + 1) * Q, q * LANES : (q + 1) * LANES]
    pair_start(1)

    def slope_half(which, k):
        rows = rows_of(k * ROWS, ROWS)
        w_rows = rows_of(which * half, half)
        value = (nt(s.og[rows, :], s.weo[w_rows, :]) * s.pre[which, rows, :]).astype(BF)
        s.sl[which, rows, :] = value
        return value

    def slope_sums(which):
        s.rs[which] = mm(s.rhot_t[...], s.sl[which])

        def slots(j):
            at = rows_of(j * TILE, TILE)
            s.ss[which, at, :] = mm(s.shot_t[at, :], s.sl[which])

        loop(0, slot_tiles, slots)

    def backward_own(k):
        value = slope_half(h, k)
        s.vsum[6:7, 0:half] += row_sum(value.astype(F32))

    loop(0, tiles, backward_own)
    slope_sums(h)

    pair_finish(1)
    a_send(1)

    edge_part = tn(s.ef[...], s.sl[h])
    recv_part = tn(s.nf[...], s.rs[h].astype(BF))
    for p in (0, 1):
        cols = slice(p * Q, (p + 1) * Q)
        s.g[p, base_in : base_in + L, :] = edge_part[:, cols]
        s.g[p, base_in + 2 * L : base_in + 3 * L, :] = recv_part[:, cols]
        for j in range(6):
            for q in range(L // LANES):
                at = base_vec + j * (L // LANES) + q
                s.g[p, at : at + 1, :] = s.vsum[j : j + 1, q * LANES : (q + 1) * LANES]
        s.g[p, base_vec + 24 : base_vec + 25, :] = s.vsum[6:7, cols]
        s.g[p, base_vec + 25 : base_vec + 26, :] = 0.5 * row_sum(s.nsl[2 * h + p].astype(F32))

    def sender_part(k):
        at = rows_of(k * TILE, TILE)
        value = tn(s.slots[at, :], s.ss[h, at, :].astype(BF))
        for p in (0, 1):
            s.g[p, base_in + L : base_in + 2 * L, :] += value[:, p * Q : (p + 1) * Q]

    loop(0, slot_tiles, sender_part)
    pair_start(2)
    b_send(0)
    pair_finish(2)
    a_send(2)

    def backward_other(k):
        rows = rows_of(k * ROWS, ROWS)
        value = slope_half(oh, k)
        cot = s.ecot[rows, :].astype(F32)
        back = nt(s.sl[0, rows, :], s.wei[0, 0:L, :]) + nt(s.sl[1, rows, :], s.wei[1, 0:L, :])
        s.eg[rows, :] = (cot + back).astype(BF)
        out_start(k, s.eg, s.eg_h, 1)

    loop(0, tiles, backward_other)
    slope_sums(oh)
    b_send(1)
    b_finish(0)

    def quarter(hh, cc):
        return pl.ds(pl.multiple_of(cc * LH + hh * LQ, LQ), LQ)

    quarter_rows = rows_of(c * LH + h * LQ, LQ)

    def slot_grad(which, rows):
        at = rows_of(L + which * LH + h * LQ, LQ)
        return nt(s.ss[0, rows, :].astype(BF), s.wei[0, at, :]) + nt(s.ss[1, rows, :].astype(BF), s.wei[1, at, :])

    def recv_grad(which):
        at = rows_of(2 * L + which * LH + h * LQ, LQ)
        return nt(s.rs[0].astype(BF), s.wei[0, at, :]) + nt(s.rs[1].astype(BF), s.wei[1, at, :])

    def slot_other(k):
        rows = rows_of(k * TILE, TILE)
        s.tosend[rows, :] = slot_grad(oc, rows).astype(BF)

    loop(0, slot_tiles, slot_other)
    s.tosend[S : S + N, :] = recv_grad(oc).astype(BF)
    grad_swap = remote(s.tosend, s.torecv, s.xsend.at[1], s.xrecv.at[1], (r, pair))
    grad_swap.start()
    b_send(2)
    s.ntp[...] = (
        s.ncot[:, quarter(h, c)].astype(F32)
        + (nt(s.nsl[0], s.wni[quarter_rows, 0:Q]) + nt(s.nsl[1], s.wni[quarter_rows, Q : 2 * Q]))
        + (
            nt(s.nsl[2], s.wni[quarter_rows, 2 * Q : 3 * Q])
            + nt(s.nsl[3], s.wni[quarter_rows, 3 * Q : 4 * Q])
        )
        + recv_grad(c)
    )
    grad_swap.wait_recv()

    def slot_own(k):
        rows = rows_of(k * TILE, TILE)
        s.back[rows, :] = (slot_grad(c, rows) + s.torecv[rows, :].astype(F32)).astype(BF)

    ref = s.served.at[others]
    remote(ref, ref, s.ssend.at[0], s.srecv.at[0], (near_row, t)).wait_send()
    loop(0, slot_tiles, slot_own)

    def back_copy(k):
        to = lax.rem(r + k, R)
        return remote(s.back.at[rows_of(to * CAP, CAP)], s.ret.at[mine], s.ksend.at[0], s.krecv.at[0], (to, t))

    loop(1, R, lambda k: back_copy(k).start())
    b_finish(1)
    spread(0)
    b_finish(2)

    def norm_row(k):
        to = lax.rem(r + k, R)
        ref = s.norm_a.at[mine8]
        return remote(ref, ref, s.qsend.at[0], s.qrecv.at[0], (to, t))

    loop(1, R, lambda k: norm_row(k).start())
    s.ret[mine, :] = s.back[mine, :]
    s.ntp[...] += s.torecv[S : S + N, :].astype(F32)
    for n in (1, 2):
        spread(n)

    ref = s.norm_a.at[pl.ds(0, (R - 1) * 8)]
    remote(ref, ref, s.qsend.at[0], s.qrecv.at[0], (near_row, t)).wait()
    own_rows = rows_of(t * 8, 8, 8)
    s.nsq[own_rows, :] = jnp.sum(s.norm_a[...].reshape(R, 8, LANES), axis=0)
    for peer in (pair, far, diag):
        ref = s.nsq.at[own_rows]
        remote(ref, ref, s.tsem.at[0], s.tsem.at[1], (r, peer)).start()

    ref = s.ret.at[others]
    remote(ref, ref, s.ksend.at[0], s.krecv.at[0], (near_row, t)).wait()

    def gathered(k):
        lanes = pl.ds(pl.multiple_of(k * TILE, TILE), TILE)
        s.ntp[...] += mm(s.serve_t[:, lanes], s.ret[rows_of(k * TILE, TILE), :])

    loop(0, slot_tiles, gathered)
    s.ng[...] = s.ntp[...].astype(BF)
    ng_at = s.ng_h.at[:, quarter(h, c)]
    ng_keep = local(s.ng, ng_at, s.nsem.at[1])
    ng_keep.start()
    takers = ((3, pair, h, oc), (5, far, oh, c), (6, diag, oh, oc))
    for k, peer, _, _ in takers:
        remote(s.ng, ng_at, s.xsend.at[k], s.xrecv.at[k], (r, peer)).start()

    for n in (0, 1, 2):
        spread_wait(n)
    ref = s.nsq.at[pl.ds(0, 24)]
    remote(ref, ref, s.tsem.at[0], s.tsem.at[1], (r, pair)).wait()
    total = s.nsq[0:8, :] + s.nsq[8:16, :] + s.nsq[16:24, :] + s.nsq[24:32, :]
    s.norm_o[...] = jnp.sqrt(jnp.full((8, LANES), jnp.sum(total), F32))
    for n in (0, 1, 2):
        sums_done(n)
    weights_sent()
    slot_swap.wait_send()
    grad_swap.wait_send()

    out_wait(s.ne, s.ne_h, 0)
    out_wait(s.eg, s.eg_h, 1)
    nn_copy.wait()
    ng_keep.wait()
    for k, peer, hh, cc in takers:
        remote(s.ng, s.ng_h.at[:, quarter(hh, cc)], s.xsend.at[k], s.xrecv.at[k], (r, peer)).wait()


def adam(weight, first, second, gradient, factor, rate):
    clipped = gradient * factor
    first_new = beta_one * first + (1.0 - beta_one) * clipped
    second_new = beta_two * second + (1.0 - beta_two) * clipped * clipped
    bias_one = 1.0 - beta_one**adam_step
    bias_two = 1.0 - beta_two**adam_step
    moved = first_new / bias_one / (jnp.sqrt(second_new / bias_two) + adam_eps) + decay_rate * weight
    return weight - rate * moved, first_new, second_new


def update(names, d, *refs):
    s = types.SimpleNamespace(**dict(zip(names, refs, strict=True)))
    L, Q = d.L, d.Q
    passes = [
        pltpu.make_async_copy(s.__dict__[f"pass{k}"], s.__dict__[f"out{k}"], s.psem.at[k]) for k in range(4)
    ]
    for copy in passes:
        copy.start()
    norm = s.norm[0:1, 0:1]
    s.norm_o[0] = s.norm[0, 0]
    factor = clip_level / jnp.maximum(norm, clip_level)
    copies = []

    def one(k, grad, at, rate):
        values = adam(
            s.__dict__[f"in{k}"][at], s.__dict__[f"in{6 + k}"][at], s.__dict__[f"in{12 + k}"][at], grad, factor, rate
        )
        for n, value in enumerate(values):
            s.__dict__[f"buf{6 * n + k}"][at] = value

    def send(k):
        for n in range(3):
            m = 6 * n + k
            copy = pltpu.make_async_copy(s.__dict__[f"buf{m}"], s.__dict__[f"new{m}"], s.osem.at[m])
            copy.start()
            copies.append(copy)

    everything = (slice(None), slice(None))
    for k, base in ((2, d.base_node), (0, d.base_in)):
        for low in range(0, (2 if k == 2 else 3) * L, 256):
            rows = slice(low, low + 256)
            one(k, s.fin[base + low : base + low + 256, :].astype(F32), (rows, slice(None)), learn_rate)
        send(k)
    for k, base in ((3, d.base_node + 2 * L), (1, d.base_out)):
        for q in range(L // LANES):
            at = (slice(None), slice(q * LANES, (q + 1) * LANES))
            one(k, s.fin[base + q * LANES : base + (q + 1) * LANES, :].astype(F32), at, learn_rate)
        send(k)
    vec = s.fin[d.base_in + 3 * L : d.base_in + 3 * L + 32, :].astype(F32)
    one(4, vec[24:26, :], everything, vector_rate)
    send(4)
    for j in range(6):
        for q in range(L // LANES):
            m = j * (L // LANES) + q
            at = (slice(j, j + 1), slice(q * LANES, (q + 1) * LANES))
            one(5, vec[m : m + 1, :], at, vector_rate)
    send(5)
    for copy in copies + passes:
        copy.wait()


def device_step(
    node_feats,
    edge_feats,
    edge_receiver,
    edge_slot,
    edge_mask,
    serve_rows,
    node_cot,
    edge_cot,
    *states,
):
    weights = states[:6]
    d = types.SimpleNamespace()
    d.R = lax.axis_size("rows")
    d.N, d.L = node_feats.shape
    d.E = edge_feats.shape[0]
    d.Q = weights[0].shape[1]
    d.H = d.Q * lax.axis_size("tp")
    d.CAP = serve_rows.shape[1]
    R, N, E, L, H, Q = d.R, d.N, d.E, d.L, d.H, d.Q
    EH, S = E // 2, R * d.CAP
    tiles = EH // ROWS

    def padded(count):
        return -(-count // (16 * R)) * (16 * R)

    d.size_node, d.size_out, d.size_in = padded(3 * L), padded(L), padded(3 * L + 32)
    d.base_node, d.base_out, d.base_in = 0, d.size_node, d.size_node + d.size_out
    G = d.size_node + d.size_out + d.size_in
    d.down, d.up = DOWN, UP
    most = R // min(*DOWN, *UP)
    vmem_spec = pl.BlockSpec(memory_space=pltpu.VMEM)
    inputs = dict(
        nf_h=node_feats,
        ef_h=edge_feats,
        ncot_h=node_cot,
        ecot_h=edge_cot,
        wei_h=weights[0],
        weo_h=weights[1],
        wni_h=weights[2],
        wno_h=weights[3],
        hb_h=weights[4],
        fv_h=weights[5],
        rec2_h=edge_receiver.reshape(-1, LANES),
        slot2_h=edge_slot.reshape(-1, LANES),
        mask2_h=edge_mask.reshape(-1, LANES),
        rec1_h=edge_receiver.reshape(1, -1),
        slot1_h=edge_slot.reshape(1, -1),
        serve_h=serve_rows,
    )
    hbm_spec = pl.BlockSpec(memory_space=pltpu.HBM)
    outputs = dict(
        nn_h=(jax.ShapeDtypeStruct((N, L), BF), hbm_spec),
        ne_h=(jax.ShapeDtypeStruct((E, L), BF), hbm_spec),
        ng_h=(jax.ShapeDtypeStruct((N, L), BF), hbm_spec),
        eg_h=(jax.ShapeDtypeStruct((E, L), BF), hbm_spec),
        fin_o=(jax.ShapeDtypeStruct((G, Q), BF), vmem_spec),
        norm_o=(jax.ShapeDtypeStruct((8, LANES), F32), vmem_spec),
    )
    dma = pltpu.SemaphoreType.DMA
    scratch = dict(
        hb=pltpu.VMEM((2, Q), F32),
        fv=pltpu.VMEM((6, L), F32),
        rec2=pltpu.VMEM((E // LANES, LANES), jnp.int32),
        slot2=pltpu.VMEM((E // LANES, LANES), jnp.int32),
        mask2=pltpu.VMEM((E // LANES, LANES), jnp.int32),
        rec1=pltpu.VMEM((1, E), jnp.int32),
        slot1=pltpu.VMEM((1, E), jnp.int32),
        serve=pltpu.VMEM((R, d.CAP), jnp.int32),
        wei32=pltpu.VMEM((3 * L, Q), F32),
        weo32=pltpu.VMEM((Q, L), F32),
        wni32=pltpu.VMEM((2 * L, Q), F32),
        wno32=pltpu.VMEM((Q, L), F32),
        nf=pltpu.VMEM((N, L), BF),
        ef=pltpu.VMEM((EH, L), BF),
        ncot=pltpu.VMEM((N, L), BF),
        ecot=pltpu.VMEM((EH, L), BF),
        wei=pltpu.VMEM((2, 3 * L, H // 2), BF),
        weo=pltpu.VMEM((H, L), BF),
        wni=pltpu.VMEM((2 * L, H), BF),
        wno=pltpu.VMEM((H, L), BF),
        bias=pltpu.VMEM((8, H), F32),
        serve_col=pltpu.VMEM((S, 1), F32),
        serve_t=pltpu.VMEM((N, S), BF),
        served=pltpu.VMEM((S, L // 2), BF),
        slots=pltpu.VMEM((S, L), BF),
        ret=pltpu.VMEM((S, L // 4), BF),
        back=pltpu.VMEM((S, L // 4), BF),
        rcol=pltpu.VMEM((EH, 1), F32),
        scol=pltpu.VMEM((EH, 1), F32),
        mcol=pltpu.VMEM((EH, 1), F32),
        rhot=pltpu.VMEM((EH, N), BF),
        rhot_t=pltpu.VMEM((N, EH), BF),
        shot_t=pltpu.VMEM((S, EH), BF),
        xr=pltpu.VMEM((EH, L), BF),
        xs=pltpu.VMEM((EH, L), BF),
        part=pltpu.VMEM((EH, L), F32),
        mk=pltpu.VMEM((EH, L), BF),
        pre=pltpu.VMEM((2, EH, H // 2), F32),
        hid=pltpu.VMEM((2, EH, H // 2), BF),
        normed=pltpu.VMEM((EH, L), F32),
        inv=pltpu.VMEM((EH, 1), F32),
        ne=pltpu.VMEM((EH, L), BF),
        eg=pltpu.VMEM((EH, L), BF),
        aggp=pltpu.VMEM((N, L), F32),
        aggr=pltpu.VMEM((N, L), F32),
        nn=pltpu.VMEM((N, L), BF),
        ng=pltpu.VMEM((N, L // 4), BF),
        agh=pltpu.VMEM((N, L), BF),
        ntp=pltpu.VMEM((N, L // 4), F32),
        nsl=pltpu.VMEM((H // Q, N, Q), BF),
        nhid=pltpu.VMEM((H // Q, N, Q), BF),
        og=pltpu.VMEM((EH, L), BF),
        sl=pltpu.VMEM((2, EH, H // 2), BF),
        rs=pltpu.VMEM((2, N, H // 2), F32),
        ss=pltpu.VMEM((2, S, H // 2), F32),
        tosend=pltpu.VMEM((S + N, L // 4), BF),
        torecv=pltpu.VMEM((S + N, L // 4), BF),
        g=pltpu.VMEM((2, G, Q), F32),
        sb=pltpu.VMEM((G, Q), BF),
        rbp=pltpu.VMEM((G, Q), BF),
        rba=pltpu.VMEM((3, G, Q), BF),
        rbb=pltpu.VMEM((most - 1, G // R, Q), BF),
        vsum=pltpu.VMEM((8, L), F32),
        norm_a=pltpu.VMEM((8 * R, LANES), F32),
        nsq=pltpu.VMEM((32, LANES), F32),
        lsem=dma((16,)),
        wsend=dma((22,)),
        wrecv=dma((28,)),
        ssend=dma((1,)),
        srecv=dma((1,)),
        ksend=dma((1,)),
        krecv=dma((1,)),
        qsend=dma((1,)),
        qrecv=dma((1,)),
        osem=dma((2,)),
        osend=dma((2,)),
        orecv=dma((2,)),
        xsend=dma((7,)),
        xrecv=dma((7,)),
        nsem=dma((2,)),
        psend=dma((3,)),
        precv=dma((3,)),
        asend=dma((3,)),
        arecv=dma((3, most)),
        bsend=dma((3, most - 1)),
        brecv=dma((3, most - 1)),
        fbsend=dma((3, most - 1)),
        fbrecv=dma((3, most - 1)),
        fasend=dma((3,)),
        farecv=dma((3,)),
        tsem=dma((2,)),
    )
    names = (*inputs, *outputs, *scratch)
    limit = 6 * 1024 * 1024
    for x in scratch.values():
        if x.memory_space == pltpu.VMEM:
            *lead, rows, lanes = x.shape
            limit += math.prod(lead) * rows * -(-lanes // LANES) * LANES * jnp.dtype(x.dtype).itemsize
    new_nodes, new_edges, node_gradient, edge_gradient, fin, norm = pl.pallas_call(
        functools.partial(layer, names, d),
        out_shape=[shape for shape, _ in outputs.values()],
        in_specs=[hbm_spec] * len(inputs),
        out_specs=[spec for _, spec in outputs.values()],
        scratch_shapes=list(scratch.values()),
        compiler_params=pltpu.CompilerParams(
            collective_id=0, has_side_effects=True, vmem_limit_bytes=limit
        ),
    )(*(pltpu.with_memory_space_constraint(x, pltpu.HBM) for x in inputs.values()))

    passes = (new_nodes, new_edges, node_gradient, edge_gradient)
    names = (
        "fin",
        "norm",
        *(f"pass{k}" for k in range(4)),
        *(f"in{k}" for k in range(18)),
        *(f"out{k}" for k in range(4)),
        "norm_o",
        *(f"new{k}" for k in range(18)),
        *(f"buf{k}" for k in range(18)),
        "psem",
        "osem",
    )
    outs = pl.pallas_call(
        functools.partial(update, names, d),
        out_shape=[
            *(jax.ShapeDtypeStruct(x.shape, x.dtype) for x in passes),
            jax.ShapeDtypeStruct((1,), F32),
            *(jax.ShapeDtypeStruct(x.shape, F32) for x in states),
        ],
        in_specs=[vmem_spec, vmem_spec, *[hbm_spec] * 4, *[vmem_spec] * 18],
        out_specs=[*[hbm_spec] * 4, pl.BlockSpec(memory_space=pltpu.SMEM), *[hbm_spec] * 18],
        scratch_shapes=[*(pltpu.VMEM(x.shape, F32) for x in states), dma((4,)), dma((18,))],
        compiler_params=pltpu.CompilerParams(vmem_limit_bytes=12 * 1024 * 1024),
    )(fin, norm, *passes, *states)
    return tuple(outs)


def solution(mesh):
    split = [P(None, "tp"), P("tp", None), P(None, "tp"), P("tp", None), P(None, "tp"), P()]
    row = P("rows", None)
    return jax.shard_map(
        device_step,
        mesh=mesh,
        in_specs=(row, row, P("rows"), P("rows"), P("rows"), row, row, row, *split, *split, *split),
        out_specs=(row, row, row, row, P(), *split, *split, *split),
        check_vma=False,
    )
```

```python
import functools
import math
import types

import jax
import jax.numpy as jnp
from jax import lax
from jax.experimental import pallas as pl
from jax.experimental.pallas import tpu as pltpu
from jax.sharding import PartitionSpec as P

BF = jnp.bfloat16
F32 = jnp.float32
MESH = pl.DeviceIdType.MESH
LANES = 128
TILE = 256
ROWS = 512
DOWN = (4, 4, 4)
UP = (4, 4, 4)

beta_one = 0.9
beta_two = 0.999
adam_step = 7.0
adam_eps = 1e-08
learn_rate = 0.05
vector_rate = 0.3
decay_rate = 0.1
clip_level = 1.0


def mm(left, right):
    return jnp.dot(left, right, preferred_element_type=F32)


def nt(left, right):
    return lax.dot_general(left, right, (((1,), (1,)), ((), ())), preferred_element_type=F32)


def tn(left, right):
    return lax.dot_general(left, right, (((0,), (0,)), ((), ())), preferred_element_type=F32)


def two(values):
    high = values.astype(BF)
    return high, (values - high.astype(F32)).astype(BF)


def aligned(start, step):
    return start if isinstance(start, int) else pl.multiple_of(start, step)


def rows_of(start, size, step=16):
    return pl.ds(aligned(start, step), size)


def hot(cond):
    return jnp.where(cond, 1.0, 0.0).astype(BF)


def normalize(values):
    center = values - jnp.mean(values, axis=1, keepdims=True)
    inverse = lax.rsqrt(jnp.mean(center * center, axis=1, keepdims=True) + 1e-05)
    return center * inverse, inverse


def norm_back(scaled, normed, inverse):
    first = jnp.mean(scaled, axis=1, keepdims=True)
    second = jnp.mean(scaled * normed, axis=1, keepdims=True)
    return inverse * (scaled - first - normed * second)


def row_sum(values):
    return jnp.sum(values, axis=0, keepdims=True)


def layer(names, d, *refs):
    s = types.SimpleNamespace(**dict(zip(names, refs, strict=True)))
    R, N, E, L, H, Q, CAP = d.R, d.N, d.E, d.L, d.H, d.Q, d.CAP
    EH, S, half, LH, LQ = E // 2, R * CAP, H // 2, L // 2, L // 4
    tiles, slot_tiles, nb = EH // ROWS, S // TILE, R // 4
    r = lax.axis_index("rows")
    t = lax.axis_index("tp")
    h, c = t // 2, lax.rem(t, 2)
    oh, oc = 1 - h, 1 - c
    pair = t + 1 - 2 * c
    far = t + 2 - 4 * h
    diag = pair + 2 - 4 * h
    a, b = lax.rem(r, 4), r // 4
    edge0 = c * EH
    near_row = lax.rem(r + 1, R)
    own_lane = pl.ds(pl.multiple_of(t * Q, Q), Q)
    core_lane = pl.ds(pl.multiple_of(c * Q, Q), Q)
    far_lane = pl.ds(pl.multiple_of(far * Q, Q), Q)
    col_lane = pl.ds(pl.multiple_of(c * LH, LH), LH)

    def local(src, dst, sem):
        return pltpu.make_async_copy(src, dst, sem)

    def remote(src, dst, send, recv, device):
        return pltpu.make_async_remote_copy(
            src_ref=src, dst_ref=dst, send_sem=send, recv_sem=recv, device_id=device, device_id_type=MESH
        )

    def loop(low, high, body):
        def step(k, carry):
            body(k)
            return carry

        if high - low <= 8:
            for k in range(low, high):
                body(k)
        else:
            lax.fori_loop(low, high, step, 0)

    loads = [
        local(s.wei_h, s.wei32, s.lsem.at[0]),
        local(s.nf_h, s.nf, s.lsem.at[1]),
        local(s.ef_h.at[rows_of(edge0, EH)], s.ef, s.lsem.at[2]),
        local(s.weo_h, s.weo32, s.lsem.at[3]),
        local(s.wni_h, s.wni32, s.lsem.at[4]),
        local(s.wno_h, s.wno32, s.lsem.at[5]),
        local(s.ncot_h, s.ncot, s.lsem.at[6]),
        local(s.ecot_h.at[rows_of(edge0, EH)], s.ecot, s.lsem.at[7]),
        local(s.serve_h, s.serve, s.lsem.at[8]),
        local(s.hb_h, s.hb, s.lsem.at[9]),
        local(s.fv_h, s.fv, s.lsem.at[10]),
        local(s.rec2_h, s.rec2, s.lsem.at[11]),
        local(s.slot2_h, s.slot2, s.lsem.at[12]),
        local(s.mask2_h, s.mask2, s.lsem.at[13]),
        local(s.rec1_h, s.rec1, s.lsem.at[14]),
        local(s.slot1_h, s.slot1, s.lsem.at[15]),
    ]
    for k in (0, 1, 8, 9, 3, 11, 12, 13, 14, 15, 2, 4, 5, 10, 6, 7):
        loads[k].start()

    barrier = pltpu.get_barrier_semaphore()
    for peer in (pair, far, diag):
        pl.semaphore_signal(barrier, inc=1, device_id=(r, peer), device_id_type=MESH)

    def greet(k):
        pl.semaphore_signal(barrier, inc=1, device_id=(lax.rem(r + k, R), t), device_id_type=MESH)

    loop(1, R, greet)

    shared = (1, 2, 4, 5)

    def block(i, tt, part=None):
        lane = pl.ds(pl.multiple_of(tt * Q, Q), Q)
        if i < 3:
            half_lane = pl.ds(pl.multiple_of(lax.rem(tt, 2) * Q, Q), Q)
            rows = pl.ds((0, 2 * L, L)[i], L) if part is None else rows_of((0, 2 * L, L)[i] + part * (L // 4), L // 4)
            return s.wei.at[tt // 2, rows, half_lane]
        if i == 3:
            return s.weo.at[lane, :]
        if i < 6:
            low = (L, 0)[i - 4]
            return s.wni.at[pl.ds(low, L) if part is None else rows_of(low + part * (L // 4), L // 4), lane]
        if i == 6:
            return s.wno.at[lane, :]
        return s.bias.at[:, lane]

    groups = (0, 0, 0, 1, 2, 2, 3, 4)

    def weight_copy(i, way, who):
        ref = block(i, who, a if way == 1 and i in shared else None)
        sent = 10 + i if way == 1 else groups[i] + 5 * (way // 2)
        return remote(ref, ref, s.wsend.at[sent], s.wrecv.at[8 * way + i], (r, (pair, far, pair)[way]))

    def part_copy(i, j, ref):
        at = shared.index(i)
        device = (b * 4 + lax.rem(a + j, 4), t)
        return remote(ref, ref, s.wsend.at[18 + at], s.wrecv.at[24 + at], device)

    def three_parts(i):
        low, size = (0, 2 * L, L, 0, L, 0)[i], 3 * (L // 4)
        if i < 3:
            return s.wei.at[oh, pl.ds(low, size), core_lane]
        return s.wni.at[pl.ds(low, size), far_lane]

    def weights_sent():
        for way, tt, th, lane in ((0, t, h, own_lane), (2, far, oh, far_lane)):
            for k, ref in enumerate(
                (s.wei.at[th, :, core_lane], block(3, tt), s.wni.at[:, lane], block(6, tt), block(7, tt))
            ):
                remote(ref, ref, s.wsend.at[k + 5 * (way // 2)], s.wrecv.at[0], (r, pair)).wait_send()
        for i in range(8):
            weight_copy(i, 1, t).wait_send()
        for i in shared:
            part_copy(i, 1, three_parts(i)).wait_send()

    def weight_send(i, way):
        weight_copy(i, way, t).start()

    def weight_wait(i, way):
        weight_copy(i, way, (pair, far, diag)[way]).wait_recv()

    def part_spread(i):
        weight_wait(i, 1)
        for j in (1, 2, 3):
            part_copy(i, j, block(i, far, a)).start()

    def weight_forward(i):
        if i in shared:
            part_copy(i, 1, three_parts(i)).wait_recv()
        else:
            weight_wait(i, 1)
        weight_copy(i, 2, far).start()

    loads[0].wait()
    for i in range(3):
        at = pl.ds((0, 2 * L, L)[i], L)
        s.wei[h, at, core_lane] = s.wei32[at, :].astype(BF)
    loads[9].wait()
    s.bias[0:2, own_lane] = s.hb[...]
    s.bias[2:8, own_lane] = jnp.zeros((6, Q), F32)
    loads[1].wait()

    loads[8].wait()
    turned = jnp.transpose(s.serve[...].astype(F32))
    for k in range(R):
        s.serve_col[k * CAP : (k + 1) * CAP, :] = turned[:, k : k + 1]

    def serve(k):
        at = rows_of(k * TILE, TILE)
        table = s.serve_col[at, :].astype(jnp.int32) == lax.broadcasted_iota(jnp.int32, (TILE, N), 1)
        table = jnp.where(table, 1.0, 0.0)
        s.serve_t[:, pl.ds(pl.multiple_of(k * TILE, TILE), TILE)] = jnp.transpose(table).astype(BF)
        s.served[at, :] = mm(table.astype(BF), s.nf[:, col_lane]).astype(BF)

    loop(0, slot_tiles, serve)
    pl.semaphore_wait(barrier, R + 2)

    for i in (1, 2, 7, 0):
        weight_send(i, 1)
    mine = rows_of(r * CAP, CAP)

    def served_copy(k):
        to = lax.rem(r + k, R)
        return remote(
            s.served.at[rows_of(to * CAP, CAP)],
            s.slots.at[mine, col_lane],
            s.ssend.at[0],
            s.srecv.at[0],
            (to, t),
        )

    loop(1, R, lambda k: served_copy(k).start())
    s.slots[mine, col_lane] = s.served[mine, :]
    for i in (0, 1, 2, 7):
        weight_send(i, 0)
    loads[4].wait()
    for i in (4, 5):
        at = pl.ds((L, 0)[i - 4], L)
        s.wni[at, own_lane] = s.wni32[at, :].astype(BF)
        weight_send(i, 1)
    loads[3].wait()
    s.weo[own_lane, :] = s.weo32[...].astype(BF)
    loads[5].wait()
    s.wno[own_lane, :] = s.wno32[...].astype(BF)
    for i in (3, 6):
        weight_send(i, 1)
    for i in (3, 4, 5, 6):
        weight_send(i, 0)

    for k in (11, 12, 13, 14, 15):
        loads[k].wait()
    per = EH // LANES
    at = rows_of(c * per, per, 8)
    for source, target in ((s.rec2, s.rcol), (s.slot2, s.scol), (s.mask2, s.mcol)):
        turned = jnp.transpose(source[at, :].astype(F32))
        for k in range(per):
            target[k * LANES : (k + 1) * LANES, :] = turned[:, k : k + 1]
    lanes_here = pl.ds(pl.multiple_of(edge0, EH), EH)
    s.rhot_t[...] = hot(s.rec1[:, lanes_here] == lax.broadcasted_iota(jnp.int32, (N, EH), 0))
    part_spread(1)
    part_spread(2)

    def slot_table(k):
        rows = rows_of(k * TILE, TILE)
        s.shot_t[rows, :] = hot(
            s.slot1[:, lanes_here] == lax.broadcasted_iota(jnp.int32, (TILE, EH), 0) + k * TILE
        )

    loop(0, slot_tiles, slot_table)

    def receivers(k):
        rows = rows_of(k * ROWS, ROWS)
        index = s.rcol[rows, :].astype(jnp.int32)
        table = hot(index == lax.broadcasted_iota(jnp.int32, (ROWS, N), 1))
        s.rhot[rows, :] = table
        s.xr[rows, :] = mm(table, s.nf[...]).astype(BF)

    loop(0, tiles, receivers)
    loads[2].wait()

    def first_two(which):
        def body(k):
            rows = rows_of(k * ROWS, ROWS)
            value = mm(s.ef[rows, :], s.wei[which, 0:L, :])
            s.pre[which, rows, :] = value + mm(s.xr[rows, :], s.wei[which, 2 * L : 3 * L, :])

        loop(0, tiles, body)

    def hidden_of(which, k):
        rows = rows_of(k * ROWS, ROWS)
        lanes = pl.ds(pl.multiple_of(which * half, half), half)
        pre = s.pre[which, rows, :] + mm(s.xs[rows, :], s.wei[which, L : 2 * L, :]) + s.bias[0:1, lanes]
        sig = 0.5 + 0.5 * jnp.tanh(0.5 * pre)
        value = (pre * sig).astype(BF)
        s.hid[which, rows, :] = value
        s.pre[which, rows, :] = sig + (pre * sig) * (1.0 - sig)

    def outer_of(which, k):
        return mm(s.hid[which, rows_of(k * ROWS, ROWS), :], s.weo[rows_of(which * half, half), :])

    for i in (0, 1):
        weight_wait(i, 0)
    first_two(h)
    for low, high in (
        (d.base_node + 3 * L, d.base_out),
        (d.base_out + L, d.base_in),
        (d.base_in + L, d.base_in + 2 * L),
        (d.base_in + 3 * L, d.base_in + d.size_in),
    ):
        if high > low:
            s.g[:, low:high, :] = jnp.zeros((2, high - low, Q), F32)
    weight_forward(0)

    others = pl.ds(0, (R - 1) * CAP)
    ref = s.slots.at[others, col_lane]
    remote(ref, ref, s.ssend.at[0], s.srecv.at[0], (near_row, t)).wait_recv()
    slot_swap = remote(s.slots.at[:, col_lane], s.slots.at[:, col_lane], s.xsend.at[2], s.xrecv.at[2], (r, pair))
    slot_swap.start()
    weight_forward(1)
    other_lane = pl.ds(pl.multiple_of(oc * LH, LH), LH)
    ref = s.slots.at[:, other_lane]
    remote(ref, ref, s.xsend.at[2], s.xrecv.at[2], (r, pair)).wait_recv()

    def senders(k):
        rows = rows_of(k * ROWS, ROWS)
        index = s.scol[rows, :].astype(jnp.int32)
        table = hot(index == lax.broadcasted_iota(jnp.int32, (ROWS, S), 1))
        s.xs[rows, :] = mm(table, s.slots[...]).astype(BF)

    loop(0, tiles, senders)
    weight_forward(2)
    part_spread(4)
    part_spread(5)
    for i in (2, 7, 3):
        weight_wait(i, 0)

    def own_half(k):
        hidden_of(h, k)
        s.part[rows_of(k * ROWS, ROWS), :] = outer_of(h, k)

    loop(0, tiles, own_half)
    weight_forward(7)
    for i in (0, 1):
        weight_wait(i, 2)
    first_two(oh)
    for i in (2, 7):
        weight_wait(i, 2)
    weight_forward(3)
    loop(0, tiles, lambda k: hidden_of(oh, k))
    weight_wait(3, 2)
    loads[10].wait()

    def out_copies(rows, source, target, which):
        here = source.at[rows]
        there = target.at[rows_of(edge0 + rows.start, rows.size)]
        keep = local(here, there, s.osem.at[which])
        send = remote(here, there, s.osend.at[which], s.orecv.at[which], (r, pair))
        return keep, send

    def out_start(k, source, target, which):
        keep, send = out_copies(pl.ds(k * ROWS, ROWS), source, target, which)
        keep.start()
        send.start()

    def out_wait(source, target, which):
        keep, send = out_copies(pl.ds(0, EH), source, target, which)
        keep.wait()
        send.wait_send()
        ref = target.at[rows_of(oc * EH, EH)]
        remote(ref, ref, s.osend.at[which], s.orecv.at[which], (r, pair)).wait_recv()

    def forward(k):
        rows = rows_of(k * ROWS, ROWS)
        outer = s.part[rows, :] + outer_of(oh, k) + s.fv[0:1, :]
        normed, inverse = normalize(outer)
        s.normed[rows, :] = normed
        s.inv[rows, :] = inverse
        masked = s.mcol[rows, :] * (normed * s.fv[1:2, :] + s.fv[2:3, :])
        s.ne[rows, :] = (s.ef[rows, :].astype(F32) + masked).astype(BF)
        out_start(k, s.ne, s.ne_h, 0)
        s.mk[rows, :] = masked.astype(BF)

    loop(0, tiles, forward)
    swaps = []
    for k in (0, 1):
        at = pl.ds(k * (N // 2), N // 2)
        s.aggp[at, :] = mm(s.rhot_t[at, :], s.mk[...])
        swap = remote(s.aggp.at[at], s.aggr.at[at], s.xsend.at[4 * k], s.xrecv.at[4 * k], (r, pair))
        swap.start()
        swaps.append(swap)
    for i in (4, 5, 6):
        weight_forward(i)
    weight_wait(5, 0)
    weight_wait(5, 2)
    own_term = mm(s.nf[...], s.wni[0:L, :])
    weight_wait(4, 0)
    weight_wait(4, 2)
    for swap in swaps:
        swap.wait()

    agg = (s.aggp[...] + s.aggr[...]).astype(BF)
    pre = own_term + mm(agg, s.wni[L : 2 * L, :]) + s.bias[1:2, :]
    sig = 0.5 + 0.5 * jnp.tanh(0.5 * pre)
    node_hidden = (pre * sig).astype(BF)
    slope_of = sig + (pre * sig) * (1.0 - sig)
    weight_wait(6, 0)
    weight_wait(6, 2)
    outer = mm(node_hidden, s.wno[...]) + s.fv[3:4, :]
    normed, inverse = normalize(outer)
    s.nn[...] = (s.nf[...].astype(F32) + (normed * s.fv[4:5, :] + s.fv[5:6, :])).astype(BF)
    nn_copy = local(s.nn, s.nn_h, s.nsem.at[0])
    nn_copy.start()
    loads[6].wait()
    up = s.ncot[...].astype(F32)
    node_outer_grad = norm_back(up * s.fv[4:5, :], normed, inverse).astype(BF)
    node_slope = (nt(node_outer_grad, s.wno[...]) * slope_of).astype(BF)
    s.agh[...] = nt(node_slope, s.wni[L : 2 * L, :]).astype(BF)

    for q in range(H // Q):
        s.nsl[q] = node_slope[:, q * Q : (q + 1) * Q]
        s.nhid[q] = node_hidden[:, q * Q : (q + 1) * Q]
    s.vsum[...] = jnp.zeros_like(s.vsum)
    s.vsum[3:4, :] = 0.5 * row_sum(node_outer_grad.astype(F32))
    s.vsum[4:5, :] = 0.5 * row_sum(up * normed)
    s.vsum[5:6, :] = 0.5 * row_sum(up)
    base_node, base_out, base_in, base_vec = d.base_node, d.base_out, d.base_in, d.base_in + 3 * L
    s.g[c, 0:L, :] = tn(s.nf[...], s.nsl[t])
    s.g[c, L : 2 * L, :] = tn(agg, s.nsl[t])
    node_out_grad = tn(s.nhid[t], node_outer_grad)
    for q in range(L // LANES):
        s.g[c, 2 * L + q * Q : 2 * L + (q + 1) * Q, :] = node_out_grad[:, q * LANES : (q + 1) * LANES]

    chunks = ((base_node, d.size_node), (base_out, d.size_out), (base_in, d.size_in))

    down, up_ways = d.down, d.up

    def piece(n, row):
        base, size = chunks[n]
        m = down[n]
        return rows_of(base + (lax.rem(row, m) * (R // m) + row // m) * (size // R), size // R)

    v = r

    def placed(row):
        return row

    def near(m, j):
        return (v // m) * m + lax.rem(v + j, m)

    def across(m, j):
        return lax.rem(v // m + j, R // m) * m + lax.rem(v, m)

    def crossed(m, row, j):
        return lax.rem(row // m + j, R // m) * m + lax.rem(row, m)

    spans = (*chunks[:2], (base_in + L, d.size_in - L), (base_in, L))

    def pair_copy(n):
        at = pl.ds(*spans[n])
        return remote(s.sb.at[at], s.rbp.at[at], s.psend.at[n], s.precv.at[n], (r, pair))

    def pair_start(n):
        at = pl.ds(*spans[n])
        s.sb[at, :] = s.g[oc, at, :].astype(BF)
        pair_copy(n).start()

    def pair_finish(n):
        pair_copy(n).wait()
        at = pl.ds(*spans[n])
        if n == 2:
            vec = pl.ds(base_vec, 32)
            s.g[c, vec, :] = s.g[c, vec, :].astype(BF).astype(F32)
        s.g[c, at, :] += s.rbp[at, :].astype(F32)

    def a_copy(n, jj, j, target):
        at = piece(n, crossed(down[n], target, jj))
        return remote(
            s.sb.at[at], s.rba.at[j - 1, at], s.asend.at[n], s.arecv.at[n, jj], (placed(near(down[n], j)), t)
        )

    def b_slot(n):
        base, size = chunks[n]
        return pl.ds(base // R, size // R)

    def b_copy(n, jj, row):
        return remote(
            s.sb.at[piece(n, row)],
            s.rbb.at[jj - 1, b_slot(n)],
            s.bsend.at[n, jj - 1],
            s.brecv.at[n, jj - 1],
            (placed(across(down[n], jj)), t),
        )

    def a_send(n):
        at = pl.ds(*chunks[n])
        s.sb[at, :] = s.g[c, at, :].astype(BF)
        for jj in (*range(1, R // down[n]), 0):
            for j in range(1, down[n]):
                a_copy(n, jj, j, near(down[n], j)).start()

    def a_sum(n, jj):
        at = piece(n, across(down[n], jj))
        total = s.g[c, at, :]
        ref = s.rba.at[pl.ds(0, down[n] - 1), at]
        remote(ref, ref, s.asend.at[n], s.arecv.at[n, jj], (near_row, t)).wait_recv()
        for j in range(1, down[n]):
            total = total + s.rba[j - 1, at, :].astype(F32)
        return total

    def b_send(n):
        for jj in range(1, R // down[n]):
            row = across(down[n], jj)
            s.sb[piece(n, row), :] = a_sum(n, jj).astype(BF)
            b_copy(n, jj, row).start()

    def to_b(n, jj, row):
        ref = s.fin_o.at[piece(n, row)]
        return remote(ref, ref, s.fbsend.at[n, jj - 1], s.fbrecv.at[n, jj - 1], (placed(across(up_ways[n], jj)), t))

    def to_a(n, jj, j, row):
        ref = s.fin_o.at[piece(n, row)]
        return remote(ref, ref, s.fasend.at[n], s.farecv.at[n], (placed(near(up_ways[n], j)), t))

    def b_finish(n):
        total = a_sum(n, 0)
        at = piece(n, v)
        for jj in range(1, R // down[n]):
            b_copy(n, jj, v).wait_recv()
            total = total + s.rbb[jj - 1, b_slot(n), :].astype(F32)
        final = total.astype(BF)
        s.fin_o[at, :] = final
        for jj in range(1, R // up_ways[n]):
            to_b(n, jj, v).start()
        for j in range(1, up_ways[n]):
            to_a(n, 0, j, v).start()
        final = final.astype(F32)
        squares = final * final
        count = squares.shape[0]
        if n == 2:
            m = down[n]
            low = base_in + (lax.rem(v, m) * (R // m) + v // m) * count
            index = lax.broadcasted_iota(jnp.int32, (count, LANES), 0) + low
            copied = jnp.logical_and(index >= base_vec, index < base_vec + 24)
            squares = jnp.where(copied, 0.25 * squares, squares)
        s.norm_a[mine8, :] += jnp.sum(squares.reshape(count // 8, 8, LANES), axis=0)

    def spread(n):
        m = up_ways[n]
        for jj in range(1, R // m):
            row = crossed(m, v, R // m - jj)
            to_b(n, jj, row).wait_recv()
            for j in range(1, m):
                to_a(n, jj, j, row).start()

    def all_but_own(n, m):
        base, size = chunks[n]
        return pl.ds(base, (R - R // m) * (size // R))

    def spread_wait(n):
        ref = s.fin_o.at[all_but_own(n, up_ways[n])]
        remote(ref, ref, s.fasend.at[n], s.farecv.at[n], (near_row, t)).wait()

    def sums_done(n):
        m = down[n]
        ref = s.sb.at[all_but_own(n, m)]
        remote(ref, ref, s.asend.at[n], s.arecv.at[n, 0], (near_row, t)).wait_send()
        for jj in range(1, R // m):
            b_copy(n, jj, across(m, jj)).wait_send()
        for jj in range(1, R // up_ways[n]):
            to_b(n, jj, v).wait_send()

    mine8 = rows_of(r * 8, 8, 8)
    s.norm_a[mine8, :] = jnp.zeros((8, LANES), F32)
    a_send(0)

    loads[7].wait()

    def backward_norm(k):
        rows = rows_of(k * ROWS, ROWS)
        table = s.rhot[rows, :]
        cot = s.ecot[rows, :].astype(F32)
        up = s.mcol[rows, :] * (cot + mm(table, s.agh[...]))
        normed = s.normed[rows, :]
        grad = norm_back(up * s.fv[1:2, :], normed, s.inv[rows, :]).astype(BF)
        s.og[rows, :] = grad
        s.vsum[0:1, :] += row_sum(grad.astype(F32))
        s.vsum[1:2, :] += row_sum(up * normed)
        s.vsum[2:3, :] += row_sum(up)

    loop(0, tiles, backward_norm)
    out_part = tn(s.hid[h], s.og[...])
    for p in (0, 1):
        for q in range(L // LANES):
            at = base_out + q * Q
            s.g[p, at : at + Q, :] = out_part[p * Q : (p + 1) * Q, q * LANES : (q + 1) * LANES]
    pair_start(1)

    def slope_half(which, k):
        rows = rows_of(k * ROWS, ROWS)
        w_rows = rows_of(which * half, half)
        value = (nt(s.og[rows, :], s.weo[w_rows, :]) * s.pre[which, rows, :]).astype(BF)
        s.sl[which, rows, :] = value
        return value

    def slope_sums(which):
        s.rs[which] = mm(s.rhot_t[...], s.sl[which])

        def slots(j):
            at = rows_of(j * TILE, TILE)
            s.ss[which, at, :] = mm(s.shot_t[at, :], s.sl[which])

        loop(0, slot_tiles, slots)

    def backward_own(k):
        value = slope_half(h, k)
        s.vsum[6:7, 0:half] += row_sum(value.astype(F32))

    loop(0, tiles, backward_own)
    slope_sums(h)

    pair_finish(1)
    a_send(1)

    edge_part = tn(s.ef[...], s.sl[h])
    for p in (0, 1):
        s.g[p, base_in : base_in + L, :] = edge_part[:, p * Q : (p + 1) * Q]
    pair_start(3)
    recv_part = tn(s.nf[...], s.rs[h].astype(BF))
    for p in (0, 1):
        cols = slice(p * Q, (p + 1) * Q)
        s.g[p, base_in + 2 * L : base_in + 3 * L, :] = recv_part[:, cols]
        for j in range(6):
            for q in range(L // LANES):
                at = base_vec + j * (L // LANES) + q
                s.g[p, at : at + 1, :] = s.vsum[j : j + 1, q * LANES : (q + 1) * LANES]
        s.g[p, base_vec + 24 : base_vec + 25, :] = s.vsum[6:7, cols]
        s.g[p, base_vec + 25 : base_vec + 26, :] = 0.5 * row_sum(s.nsl[2 * h + p].astype(F32))

    def sender_part(k):
        at = rows_of(k * TILE, TILE)
        value = tn(s.slots[at, :], s.ss[h, at, :].astype(BF))
        for p in (0, 1):
            s.g[p, base_in + L : base_in + 2 * L, :] += value[:, p * Q : (p + 1) * Q]

    loop(0, slot_tiles, sender_part)
    pair_start(2)
    b_send(0)
    pair_finish(3)
    pair_finish(2)
    a_send(2)

    def backward_other(k):
        rows = rows_of(k * ROWS, ROWS)
        value = slope_half(oh, k)
        cot = s.ecot[rows, :].astype(F32)
        back = nt(s.sl[0, rows, :], s.wei[0, 0:L, :]) + nt(s.sl[1, rows, :], s.wei[1, 0:L, :])
        s.eg[rows, :] = (cot + back).astype(BF)
        out_start(k, s.eg, s.eg_h, 1)

    loop(0, tiles, backward_other)
    slope_sums(oh)
    b_send(1)
    b_finish(0)

    def quarter(hh, cc):
        return pl.ds(pl.multiple_of(cc * LH + hh * LQ, LQ), LQ)

    quarter_rows = rows_of(c * LH + h * LQ, LQ)

    def slot_grad(which, rows):
        at = rows_of(L + which * LH + h * LQ, LQ)
        return nt(s.ss[0, rows, :].astype(BF), s.wei[0, at, :]) + nt(s.ss[1, rows, :].astype(BF), s.wei[1, at, :])

    def recv_grad(which):
        at = rows_of(2 * L + which * LH + h * LQ, LQ)
        return nt(s.rs[0].astype(BF), s.wei[0, at, :]) + nt(s.rs[1].astype(BF), s.wei[1, at, :])

    def slot_other(k):
        rows = rows_of(k * TILE, TILE)
        s.tosend[rows, :] = slot_grad(oc, rows).astype(BF)

    loop(0, slot_tiles, slot_other)
    s.tosend[S : S + N, :] = recv_grad(oc).astype(BF)
    grad_swap = remote(s.tosend, s.torecv, s.xsend.at[1], s.xrecv.at[1], (r, pair))
    grad_swap.start()
    b_send(2)
    s.ntp[...] = (
        s.ncot[:, quarter(h, c)].astype(F32)
        + (nt(s.nsl[0], s.wni[quarter_rows, 0:Q]) + nt(s.nsl[1], s.wni[quarter_rows, Q : 2 * Q]))
        + (
            nt(s.nsl[2], s.wni[quarter_rows, 2 * Q : 3 * Q])
            + nt(s.nsl[3], s.wni[quarter_rows, 3 * Q : 4 * Q])
        )
        + recv_grad(c)
    )
    grad_swap.wait_recv()

    def slot_own(k):
        rows = rows_of(k * TILE, TILE)
        s.back[rows, :] = (slot_grad(c, rows) + s.torecv[rows, :].astype(F32)).astype(BF)

    ref = s.served.at[others]
    remote(ref, ref, s.ssend.at[0], s.srecv.at[0], (near_row, t)).wait_send()
    loop(0, slot_tiles, slot_own)

    def back_copy(k):
        to = lax.rem(r + k, R)
        return remote(s.back.at[rows_of(to * CAP, CAP)], s.ret.at[mine], s.ksend.at[0], s.krecv.at[0], (to, t))

    loop(1, R, lambda k: back_copy(k).start())
    b_finish(1)
    spread(0)
    b_finish(2)

    def norm_row(k):
        to = lax.rem(r + k, R)
        ref = s.norm_a.at[mine8]
        return remote(ref, ref, s.qsend.at[0], s.qrecv.at[0], (to, t))

    loop(1, R, lambda k: norm_row(k).start())
    s.ret[mine, :] = s.back[mine, :]
    s.ntp[...] += s.torecv[S : S + N, :].astype(F32)
    for n in (1, 2):
        spread(n)

    ref = s.norm_a.at[pl.ds(0, (R - 1) * 8)]
    remote(ref, ref, s.qsend.at[0], s.qrecv.at[0], (near_row, t)).wait()
    own_rows = rows_of(t * 8, 8, 8)
    s.nsq[own_rows, :] = jnp.sum(s.norm_a[...].reshape(R, 8, LANES), axis=0)
    for peer in (pair, far, diag):
        ref = s.nsq.at[own_rows]
        remote(ref, ref, s.tsem.at[0], s.tsem.at[1], (r, peer)).start()

    ref = s.ret.at[others]
    remote(ref, ref, s.ksend.at[0], s.krecv.at[0], (near_row, t)).wait()

    def gathered(k):
        lanes = pl.ds(pl.multiple_of(k * TILE, TILE), TILE)
        s.ntp[...] += mm(s.serve_t[:, lanes], s.ret[rows_of(k * TILE, TILE), :])

    loop(0, slot_tiles, gathered)
    s.ng[...] = s.ntp[...].astype(BF)
    ng_at = s.ng_h.at[:, quarter(h, c)]
    ng_keep = local(s.ng, ng_at, s.nsem.at[1])
    ng_keep.start()
    takers = ((3, pair, h, oc), (5, far, oh, c), (6, diag, oh, oc))
    for k, peer, _, _ in takers:
        remote(s.ng, ng_at, s.xsend.at[k], s.xrecv.at[k], (r, peer)).start()

    for n in (0, 1, 2):
        spread_wait(n)
    ref = s.nsq.at[pl.ds(0, 24)]
    remote(ref, ref, s.tsem.at[0], s.tsem.at[1], (r, pair)).wait()
    total = s.nsq[0:8, :] + s.nsq[8:16, :] + s.nsq[16:24, :] + s.nsq[24:32, :]
    s.norm_o[...] = jnp.sqrt(jnp.full((8, LANES), jnp.sum(total), F32))
    for n in (0, 1, 2):
        sums_done(n)
    weights_sent()
    slot_swap.wait_send()
    grad_swap.wait_send()

    out_wait(s.ne, s.ne_h, 0)
    out_wait(s.eg, s.eg_h, 1)
    nn_copy.wait()
    ng_keep.wait()
    for k, peer, hh, cc in takers:
        remote(s.ng, s.ng_h.at[:, quarter(hh, cc)], s.xsend.at[k], s.xrecv.at[k], (r, peer)).wait()


def adam(weight, first, second, gradient, factor, rate):
    clipped = gradient * factor
    first_new = beta_one * first + (1.0 - beta_one) * clipped
    second_new = beta_two * second + (1.0 - beta_two) * clipped * clipped
    bias_one = 1.0 - beta_one**adam_step
    bias_two = 1.0 - beta_two**adam_step
    moved = first_new / bias_one / (jnp.sqrt(second_new / bias_two) + adam_eps) + decay_rate * weight
    return weight - rate * moved, first_new, second_new


def update(names, d, *refs):
    s = types.SimpleNamespace(**dict(zip(names, refs, strict=True)))
    L, Q = d.L, d.Q
    passes = [
        pltpu.make_async_copy(s.__dict__[f"pass{k}"], s.__dict__[f"out{k}"], s.psem.at[k]) for k in range(4)
    ]
    for copy in passes:
        copy.start()
    norm = s.norm[0:1, 0:1]
    s.norm_o[0] = s.norm[0, 0]
    factor = clip_level / jnp.maximum(norm, clip_level)
    copies = []

    def one(k, grad, at, rate):
        values = adam(
            s.__dict__[f"in{k}"][at], s.__dict__[f"in{6 + k}"][at], s.__dict__[f"in{12 + k}"][at], grad, factor, rate
        )
        for n, value in enumerate(values):
            s.__dict__[f"buf{6 * n + k}"][at] = value

    def send(k):
        for n in range(3):
            m = 6 * n + k
            copy = pltpu.make_async_copy(s.__dict__[f"buf{m}"], s.__dict__[f"new{m}"], s.osem.at[m])
            copy.start()
            copies.append(copy)

    everything = (slice(None), slice(None))
    for k, base in ((2, d.base_node), (0, d.base_in)):
        for low in range(0, (2 if k == 2 else 3) * L, 256):
            rows = slice(low, low + 256)
            one(k, s.fin[base + low : base + low + 256, :].astype(F32), (rows, slice(None)), learn_rate)
        send(k)
    for k, base in ((3, d.base_node + 2 * L), (1, d.base_out)):
        for q in range(L // LANES):
            at = (slice(None), slice(q * LANES, (q + 1) * LANES))
            one(k, s.fin[base + q * LANES : base + (q + 1) * LANES, :].astype(F32), at, learn_rate)
        send(k)
    vec = s.fin[d.base_in + 3 * L : d.base_in + 3 * L + 32, :].astype(F32)
    one(4, vec[24:26, :], everything, vector_rate)
    send(4)
    for j in range(6):
        for q in range(L // LANES):
            m = j * (L // LANES) + q
            at = (slice(j, j + 1), slice(q * LANES, (q + 1) * LANES))
            one(5, vec[m : m + 1, :], at, vector_rate)
    send(5)
    for copy in copies + passes:
        copy.wait()


def device_step(
    node_feats,
    edge_feats,
    edge_receiver,
    edge_slot,
    edge_mask,
    serve_rows,
    node_cot,
    edge_cot,
    *states,
):
    weights = states[:6]
    d = types.SimpleNamespace()
    d.R = lax.axis_size("rows")
    d.N, d.L = node_feats.shape
    d.E = edge_feats.shape[0]
    d.Q = weights[0].shape[1]
    d.H = d.Q * lax.axis_size("tp")
    d.CAP = serve_rows.shape[1]
    R, N, E, L, H, Q = d.R, d.N, d.E, d.L, d.H, d.Q
    EH, S = E // 2, R * d.CAP
    tiles = EH // ROWS

    def padded(count):
        return -(-count // (16 * R)) * (16 * R)

    d.size_node, d.size_out, d.size_in = padded(3 * L), padded(L), padded(3 * L + 32)
    d.base_node, d.base_out, d.base_in = 0, d.size_node, d.size_node + d.size_out
    G = d.size_node + d.size_out + d.size_in
    d.down, d.up = DOWN, UP
    most = R // min(*DOWN, *UP)
    vmem_spec = pl.BlockSpec(memory_space=pltpu.VMEM)
    inputs = dict(
        nf_h=node_feats,
        ef_h=edge_feats,
        ncot_h=node_cot,
        ecot_h=edge_cot,
        wei_h=weights[0],
        weo_h=weights[1],
        wni_h=weights[2],
        wno_h=weights[3],
        hb_h=weights[4],
        fv_h=weights[5],
        rec2_h=edge_receiver.reshape(-1, LANES),
        slot2_h=edge_slot.reshape(-1, LANES),
        mask2_h=edge_mask.reshape(-1, LANES),
        rec1_h=edge_receiver.reshape(1, -1),
        slot1_h=edge_slot.reshape(1, -1),
        serve_h=serve_rows,
    )
    hbm_spec = pl.BlockSpec(memory_space=pltpu.HBM)
    outputs = dict(
        nn_h=(jax.ShapeDtypeStruct((N, L), BF), hbm_spec),
        ne_h=(jax.ShapeDtypeStruct((E, L), BF), hbm_spec),
        ng_h=(jax.ShapeDtypeStruct((N, L), BF), hbm_spec),
        eg_h=(jax.ShapeDtypeStruct((E, L), BF), hbm_spec),
        fin_o=(jax.ShapeDtypeStruct((G, Q), BF), vmem_spec),
        norm_o=(jax.ShapeDtypeStruct((8, LANES), F32), vmem_spec),
    )
    dma = pltpu.SemaphoreType.DMA
    scratch = dict(
        hb=pltpu.VMEM((2, Q), F32),
        fv=pltpu.VMEM((6, L), F32),
        rec2=pltpu.VMEM((E // LANES, LANES), jnp.int32),
        slot2=pltpu.VMEM((E // LANES, LANES), jnp.int32),
        mask2=pltpu.VMEM((E // LANES, LANES), jnp.int32),
        rec1=pltpu.VMEM((1, E), jnp.int32),
        slot1=pltpu.VMEM((1, E), jnp.int32),
        serve=pltpu.VMEM((R, d.CAP), jnp.int32),
        wei32=pltpu.VMEM((3 * L, Q), F32),
        weo32=pltpu.VMEM((Q, L), F32),
        wni32=pltpu.VMEM((2 * L, Q), F32),
        wno32=pltpu.VMEM((Q, L), F32),
        nf=pltpu.VMEM((N, L), BF),
        ef=pltpu.VMEM((EH, L), BF),
        ncot=pltpu.VMEM((N, L), BF),
        ecot=pltpu.VMEM((EH, L), BF),
        wei=pltpu.VMEM((2, 3 * L, H // 2), BF),
        weo=pltpu.VMEM((H, L), BF),
        wni=pltpu.VMEM((2 * L, H), BF),
        wno=pltpu.VMEM((H, L), BF),
        bias=pltpu.VMEM((8, H), F32),
        serve_col=pltpu.VMEM((S, 1), F32),
        serve_t=pltpu.VMEM((N, S), BF),
        served=pltpu.VMEM((S, L // 2), BF),
        slots=pltpu.VMEM((S, L), BF),
        ret=pltpu.VMEM((S, L // 4), BF),
        back=pltpu.VMEM((S, L // 4), BF),
        rcol=pltpu.VMEM((EH, 1), F32),
        scol=pltpu.VMEM((EH, 1), F32),
        mcol=pltpu.VMEM((EH, 1), F32),
        rhot=pltpu.VMEM((EH, N), BF),
        rhot_t=pltpu.VMEM((N, EH), BF),
        shot_t=pltpu.VMEM((S, EH), BF),
        xr=pltpu.VMEM((EH, L), BF),
        xs=pltpu.VMEM((EH, L), BF),
        part=pltpu.VMEM((EH, L), F32),
        mk=pltpu.VMEM((EH, L), BF),
        pre=pltpu.VMEM((2, EH, H // 2), F32),
        hid=pltpu.VMEM((2, EH, H // 2), BF),
        normed=pltpu.VMEM((EH, L), F32),
        inv=pltpu.VMEM((EH, 1), F32),
        ne=pltpu.VMEM((EH, L), BF),
        eg=pltpu.VMEM((EH, L), BF),
        aggp=pltpu.VMEM((N, L), F32),
        aggr=pltpu.VMEM((N, L), F32),
        nn=pltpu.VMEM((N, L), BF),
        ng=pltpu.VMEM((N, L // 4), BF),
        agh=pltpu.VMEM((N, L), BF),
        ntp=pltpu.VMEM((N, L // 4), F32),
        nsl=pltpu.VMEM((H // Q, N, Q), BF),
        nhid=pltpu.VMEM((H // Q, N, Q), BF),
        og=pltpu.VMEM((EH, L), BF),
        sl=pltpu.VMEM((2, EH, H // 2), BF),
        rs=pltpu.VMEM((2, N, H // 2), F32),
        ss=pltpu.VMEM((2, S, H // 2), F32),
        tosend=pltpu.VMEM((S + N, L // 4), BF),
        torecv=pltpu.VMEM((S + N, L // 4), BF),
        g=pltpu.VMEM((2, G, Q), F32),
        sb=pltpu.VMEM((G, Q), BF),
        rbp=pltpu.VMEM((G, Q), BF),
        rba=pltpu.VMEM((3, G, Q), BF),
        rbb=pltpu.VMEM((most - 1, G // R, Q), BF),
        vsum=pltpu.VMEM((8, L), F32),
        norm_a=pltpu.VMEM((8 * R, LANES), F32),
        nsq=pltpu.VMEM((32, LANES), F32),
        lsem=dma((16,)),
        wsend=dma((22,)),
        wrecv=dma((28,)),
        ssend=dma((1,)),
        srecv=dma((1,)),
        ksend=dma((1,)),
        krecv=dma((1,)),
        qsend=dma((1,)),
        qrecv=dma((1,)),
        osem=dma((2,)),
        osend=dma((2,)),
        orecv=dma((2,)),
        xsend=dma((7,)),
        xrecv=dma((7,)),
        nsem=dma((2,)),
        psend=dma((4,)),
        precv=dma((4,)),
        asend=dma((3,)),
        arecv=dma((3, most)),
        bsend=dma((3, most - 1)),
        brecv=dma((3, most - 1)),
        fbsend=dma((3, most - 1)),
        fbrecv=dma((3, most - 1)),
        fasend=dma((3,)),
        farecv=dma((3,)),
        tsem=dma((2,)),
    )
    names = (*inputs, *outputs, *scratch)
    limit = 6 * 1024 * 1024
    for x in scratch.values():
        if x.memory_space == pltpu.VMEM:
            *lead, rows, lanes = x.shape
            limit += math.prod(lead) * rows * -(-lanes // LANES) * LANES * jnp.dtype(x.dtype).itemsize
    new_nodes, new_edges, node_gradient, edge_gradient, fin, norm = pl.pallas_call(
        functools.partial(layer, names, d),
        out_shape=[shape for shape, _ in outputs.values()],
        in_specs=[hbm_spec] * len(inputs),
        out_specs=[spec for _, spec in outputs.values()],
        scratch_shapes=list(scratch.values()),
        compiler_params=pltpu.CompilerParams(
            collective_id=0, has_side_effects=True, vmem_limit_bytes=limit
        ),
    )(*(pltpu.with_memory_space_constraint(x, pltpu.HBM) for x in inputs.values()))

    passes = (new_nodes, new_edges, node_gradient, edge_gradient)
    names = (
        "fin",
        "norm",
        *(f"pass{k}" for k in range(4)),
        *(f"in{k}" for k in range(18)),
        *(f"out{k}" for k in range(4)),
        "norm_o",
        *(f"new{k}" for k in range(18)),
        *(f"buf{k}" for k in range(18)),
        "psem",
        "osem",
    )
    outs = pl.pallas_call(
        functools.partial(update, names, d),
        out_shape=[
            *(jax.ShapeDtypeStruct(x.shape, x.dtype) for x in passes),
            jax.ShapeDtypeStruct((1,), F32),
            *(jax.ShapeDtypeStruct(x.shape, F32) for x in states),
        ],
        in_specs=[vmem_spec, vmem_spec, *[hbm_spec] * 4, *[vmem_spec] * 18],
        out_specs=[*[hbm_spec] * 4, pl.BlockSpec(memory_space=pltpu.SMEM), *[hbm_spec] * 18],
        scratch_shapes=[*(pltpu.VMEM(x.shape, F32) for x in states), dma((4,)), dma((18,))],
        compiler_params=pltpu.CompilerParams(vmem_limit_bytes=12 * 1024 * 1024),
    )(fin, norm, *passes, *states)
    return tuple(outs)


def solution(mesh):
    split = [P(None, "tp"), P("tp", None), P(None, "tp"), P("tp", None), P(None, "tp"), P()]
    row = P("rows", None)
    return jax.shard_map(
        device_step,
        mesh=mesh,
        in_specs=(row, row, P("rows"), P("rows"), P("rows"), row, row, row, *split, *split, *split),
        out_specs=(row, row, row, row, P(), *split, *split, *split),
        check_vma=False,
    )
```
